32 devices in a mesh: kern: 4 (over y, x), tile: 8 (over z, core).
Axes of the slice: x: 2, y: 2, z: 4, core: 2. Of those that a mesh axis runs over, the one named last changes fastest.
Arguments:
- diag_tiles: float32 [4, 8, 512, 512], P('kern', 'tile'), may hold values from -0.25 to 0.25
- left_factors: float32 [4, 8, 8, 80, 512], P('kern', 'tile'), may hold values from -0.25 to 0.25
- right_factors: float32 [4, 8, 12, 80, 512], P('kern', 'tile'), may hold values from -0.25 to 0.25
- tile_offsets: int32 [4, 8, 8], P('kern', 'tile'), may hold values from -6 to 6, as said below
- tile_ranks: int32 [4, 8, 8], P('kern', 'tile'), may hold values from 32 to 80
- mixing: float32 [64, 4, 4], replicated, may hold values from -3 to 3
- block_index: int32 [4096], P('tile'), may hold values from 0 to 63
- rhs_field: float32 [4, 4096, 128], P('kern', 'tile'), may hold values from -6 to 6
Outputs:
- product: float32 [4, 4096, 128], P('kern', 'tile')
The draws below stay inside these ranges and needn't reach their ends.
Inputs may be any that keep to these rules, and one draw needn't show every extreme that they name: `tile_offsets`: each row's 8 offsets are distinct and nonzero.
All inputs are finite; a program needn't handle non-finite values.
Results may differ from the reference program's by a relative error of at most 0.00007.
Values sent between devices are 32-bit elements; how exact they have to be, the bound alone decides.
No kernel may reach another device: no remote copies, remote signals or barrier semaphores. Data moves between devices by JAX's collectives and lax.ppermute only.
A program may use at most 64 MiB of HBM per device.

```python
import jax
import jax.numpy as jnp
from jax import lax

LATENT_KERNELS = 4
B = 512
RMAX = 80
OFFDIAG_TILES = 8
REACH = 6
C = 128
NBLK = 64
TILE_ROWS = 8
N = 4096
RMIN = 32


def draw_tile_offsets(key, part):
    candidate_list = 2 * REACH
    rating_values = jax.random.randint(key, (LATENT_KERNELS, TILE_ROWS, candidate_list), 0, 2 ** 20) * 32 + jnp.arange(candidate_list, dtype=jnp.int32)
    extra_credit = jnp.zeros((LATENT_KERNELS, TILE_ROWS, candidate_list), jnp.int32).at[:, 0, 0].set(2 ** 26).at[:, TILE_ROWS - 1, candidate_list - 1].set(2 ** 26)
    sorted_order = jnp.argsort(rating_values - extra_credit, axis=-1)[..., :OFFDIAG_TILES]
    return jnp.where(sorted_order < REACH, sorted_order - REACH, sorted_order - REACH + 1).astype(jnp.int32)


def draw_tile_ranks(key, part):
    values = jax.random.randint(key, (LATENT_KERNELS, TILE_ROWS, OFFDIAG_TILES), RMIN, RMAX + 1)
    return values.at[:, 0, 0].set(RMAX).at[:, 0, 1].set(RMIN).astype(jnp.int32)


def draw_block_index(key, part):
    values = jax.random.randint(key, (N,), 0, NBLK)
    spread = jax.random.permutation(jax.random.fold_in(key, 7), NBLK)
    return values.at[:NBLK].set(spread).astype(jnp.int32)


def block_scale(key, shape, shards, least, top_value):
    def one(axis_at, parts):
        draws = jax.random.uniform(jax.random.fold_in(jax.random.fold_in(key, 6), axis_at), (parts,), jnp.float32, least / len(shards), top_value / len(shards))
        return jnp.repeat(jnp.exp(draws), shape[axis_at] // parts).reshape((-1,) + (1,) * (len(shape) - axis_at - 1))

    gain = one(*shards[0])
    for cut in shards[1:]:
        gain = gain * one(*cut)
    return gain


def centred(stream_key, shape, width, limit, cuts=(), kind=jnp.bfloat16):
    drawn = width * jax.random.normal(stream_key, shape, jnp.float32)
    if cuts:
        drawn = drawn * block_scale(stream_key, shape, cuts, -0.22, 0.18)
    return jnp.clip(drawn, -limit, limit).astype(kind)


def setup_inputs(seed: int = 0) -> dict:
    arg_keys = jax.random.split(jax.random.key(seed), 9)
    return {
        "diag_tiles": centred(arg_keys[0], (LATENT_KERNELS, TILE_ROWS, B, B), B ** -0.5, 0.25, ((0, 4), (1, 8)), jnp.float32),
        "left_factors": centred(arg_keys[1], (LATENT_KERNELS, TILE_ROWS, OFFDIAG_TILES, RMAX, B), (OFFDIAG_TILES * RMAX) ** -0.5, 0.25, ((0, 4), (1, 8)), jnp.float32),
        "right_factors": centred(arg_keys[2], (LATENT_KERNELS, TILE_ROWS, 2 * REACH, RMAX, B), B ** -0.5, 0.25, ((0, 4), (1, 8)), jnp.float32),
        "tile_offsets": draw_tile_offsets(jax.random.fold_in(arg_keys[8], 71), 0),
        "tile_ranks": draw_tile_ranks(jax.random.fold_in(arg_keys[8], 71), 0),
        "mixing": centred(arg_keys[5], (NBLK, LATENT_KERNELS, LATENT_KERNELS), 0.5, 3.0, (), jnp.float32),
        "block_index": draw_block_index(jax.random.fold_in(arg_keys[8], 71), 0),
        "rhs_field": centred(arg_keys[7], (LATENT_KERNELS, N, C), 1.0, 6.0, ((0, 4), (1, 8)), jnp.float32),
    }


highest = lax.Precision.HIGHEST


def apply_kernel(diag_group, left_group, right_group, offsets_group, ranks_group, columns):
    tiles_n = diag_group.shape[0]
    tile_width = diag_group.shape[1]
    blocks = columns.reshape(tiles_n, tile_width, -1)
    coeffs = jnp.einsum('tsqp,tpc->tsqc', right_group, blocks, precision=highest)
    source = (jnp.arange(tiles_n, dtype=jnp.int32)[:, None] + offsets_group) % tiles_n
    slot_pick = jnp.where(offsets_group < 0, offsets_group + REACH, offsets_group + REACH - 1)
    chosen = coeffs[source.astype(jnp.int32), slot_pick.astype(jnp.int32)]
    keeper = (jnp.arange(left_group.shape[2], dtype=jnp.int32)[None, None, :] < ranks_group[:, :, None]).astype(jnp.float32)
    chosen = chosen * keeper[..., None]
    result = jnp.einsum('tpr,trc->tpc', diag_group, blocks, precision=highest)
    result = result + jnp.einsum('tkqp,tkqc->tpc', left_group, chosen, precision=highest)
    return result.reshape(tiles_n * tile_width, -1)


def reference(diag_tiles, left_factors, right_factors, tile_offsets, tile_ranks, mixing, block_index, rhs_field):
    first = jnp.stack([apply_kernel(diag_tiles[group], left_factors[group], right_factors[group], tile_offsets[group], tile_ranks[group], rhs_field[group]) for group in range(LATENT_KERNELS)])
    per_location = mixing[block_index.astype(jnp.int32)]
    mixed = jnp.einsum('lab,blc->alc', per_location, first, precision=highest)
    return jnp.stack([apply_kernel(diag_tiles[group], left_factors[group], right_factors[group], tile_offsets[group], tile_ranks[group], mixed[group]) for group in range(LATENT_KERNELS)])
```

```python
import jax
import jax.numpy as jnp
from jax import lax
from jax.sharding import PartitionSpec as P

high = lax.Precision.HIGH


def offset_of(slot, reach):
    return slot - reach if slot < reach else slot - reach + 1


def deliver_all(coeffs, reach, count):
    groups = [[] for _ in range(count)]
    for slot in range(2 * reach):
        groups[offset_of(slot, reach) % count].append(slot)
    width = max(len(group) for group in groups)
    order = [(group + [0] * width)[:width] for group in groups]
    me = lax.axis_index("tile")
    dests = jnp.arange(count, dtype=jnp.int32)
    table = jnp.asarray(order, dtype=jnp.int32)[(me - dests) % count]
    packed = coeffs[table.reshape(-1)]
    packed = packed.reshape((count, width) + coeffs.shape[1:])
    received = lax.all_to_all(packed, "tile", split_axis=0, concat_axis=0, tiled=True)
    place = [0] * (2 * reach)
    for group in groups:
        for at, slot in enumerate(group):
            place[slot] = at
    return received, jnp.asarray(place, dtype=jnp.int32)


def apply_kernel(diag_tile, left_tile, right_tile, offsets_row, ranks_row, column_vals):
    reach = right_tile.shape[0] // 2
    count = lax.axis_size("tile")
    coeffs = jnp.einsum("sqp,pc->sqc", right_tile, column_vals, precision=high)
    slot_pick = jnp.where(offsets_row < 0, offsets_row + reach, offsets_row + reach - 1)
    keeper = jnp.arange(left_tile.shape[1])[None, :] < ranks_row[:, None]
    if count <= 2 * reach:
        received, place = deliver_all(coeffs, reach, count)
        me = lax.axis_index("tile")
        chosen = received[(me + offsets_row) % count, place[slot_pick]]
    else:
        arrived = []
        for slot in range(2 * reach):
            steps = -offset_of(slot, reach)
            pairs = [(source, (source + steps) % count) for source in range(count)]
            arrived.append(lax.ppermute(coeffs[slot], "tile", pairs))
        chosen = jnp.stack(arrived)[slot_pick]
    chosen = jnp.where(keeper[:, :, None], chosen, 0.0)
    result = jnp.dot(diag_tile, column_vals, precision=high, preferred_element_type=jnp.float32)
    return result + jnp.einsum("kqp,kqc->pc", left_tile, chosen, precision=high)


def local(
    diag_tiles,
    left_factors,
    right_factors,
    tile_offsets,
    tile_ranks,
    mixing,
    block_index,
    rhs_field,
):
    diag_tile = diag_tiles[0, 0]
    left_tile = left_factors[0, 0]
    right_tile = right_factors[0, 0]
    offsets_row = tile_offsets[0, 0]
    ranks_row = tile_ranks[0, 0]
    first = apply_kernel(diag_tile, left_tile, right_tile, offsets_row, ranks_row, rhs_field[0])
    own_group = lax.axis_index("kern")
    grouped = lax.all_to_all(first[None], "kern", split_axis=1, concat_axis=0, tiled=True)
    part_len = grouped.shape[1]
    local_index = lax.dynamic_slice_in_dim(block_index, own_group * part_len, part_len)
    per_location = mixing[local_index]
    blended = jnp.sum(per_location.transpose(1, 2, 0)[..., None] * grouped[None], axis=1)
    mixed = lax.all_to_all(blended, "kern", split_axis=0, concat_axis=1, tiled=True)[0]
    second = apply_kernel(diag_tile, left_tile, right_tile, offsets_row, ranks_row, mixed)
    return second[None]


def solution(mesh):
    in_specs = (
        P("kern", "tile", None, None),
        P("kern", "tile", None, None, None),
        P("kern", "tile", None, None, None),
        P("kern", "tile", None),
        P("kern", "tile", None),
        P(),
        P("tile"),
        P("kern", "tile", None),
    )
    out_specs = P("kern", "tile", None)
    return jax.shard_map(local, mesh=mesh, in_specs=in_specs, out_specs=out_specs, check_vma=False)
```

```python
import functools

import jax
import jax.numpy as jnp
from jax import lax
from jax.experimental import pallas as pl
from jax.experimental.pallas import tpu as pltpu
from jax.sharding import PartitionSpec as P

f32 = jnp.float32
bf16 = jnp.bfloat16
VMEM_BYTES = 24 * 1024 * 1024
in_vmem = pl.BlockSpec(memory_space=pltpu.VMEM)
in_smem = pl.BlockSpec(memory_space=pltpu.SMEM)
in_any = pl.BlockSpec(memory_space=pl.ANY)


def split(value):
    hi = value.astype(bf16)
    return hi, (value - hi.astype(f32)).astype(bf16)


def dot(left, right):
    return jnp.dot(left, right, preferred_element_type=f32)


def call(kernel, out_shape, in_specs, scratch=(), flops=0, moved=0):
    many = isinstance(out_shape, (list, tuple))
    return pl.pallas_call(
        kernel,
        out_shape=out_shape,
        in_specs=in_specs,
        out_specs=[in_vmem] * len(out_shape) if many else in_vmem,
        scratch_shapes=list(scratch),
        compiler_params=pltpu.CompilerParams(vmem_limit_bytes=VMEM_BYTES),
        cost_estimate=pl.CostEstimate(flops=flops, bytes_accessed=moved, transcendentals=0),
    )


def offset_of(slot, reach):
    return slot - reach if slot < reach else slot - reach + 1


def paired(count, reach):
    return reach < count <= 2 * reach


def coeff_kernel(count, chunks, cols_ref, right_ref, out_ref, held, sems):
    slots, rank, size = right_ref.shape
    reach = slots // 2
    step = slots // chunks
    copies = []
    for at in range(chunks):
        part = pl.ds(at * step, step)
        copies.append(pltpu.make_async_copy(right_ref.at[part], held.at[part], sems.at[at]))
        copies[-1].start()
    width = cols_ref.shape[1]
    both = jnp.concatenate(split(cols_ref[...]), axis=1)
    me = lax.axis_index("tile")
    for at in range(chunks):
        copies[at].wait()
        rows = held[pl.ds(at * step, step)].reshape(step * rank, size)
        hi, lo = split(rows)
        got = dot(hi, both) + dot(lo, both)
        got = got[:, :width] + got[:, width:]
        for s in range(step):
            slot = at * step + s
            piece = got[s * rank : (s + 1) * rank]
            if paired(count, reach):
                offset = offset_of(slot, reach)
                dest = lax.rem(me - offset + count, count)
                out_ref[dest, 0 if offset > 0 else 1] = piece
            else:
                out_ref[slot, 0] = piece


def coefficients(cols, right_tile):
    count = lax.axis_size("tile")
    slots, rank, size = right_tile.shape
    width = cols.shape[1]
    lead = (count, 2) if paired(count, slots // 2) else (slots, 1)
    chunks = 3 if slots % 3 == 0 else 1
    return call(
        functools.partial(coeff_kernel, count, chunks),
        jax.ShapeDtypeStruct(lead + (rank, width), f32),
        [in_vmem, in_any],
        [pltpu.VMEM(right_tile.shape, f32), pltpu.SemaphoreType.DMA((chunks,))],
        flops=8 * slots * rank * size * width,
        moved=4 * slots * rank * (size + width),
    )(cols, right_tile)


def diag_kernel(turned, diag_ref, cols_ref, out_ref):
    width = cols_ref.shape[1]
    both = jnp.concatenate(split(cols_ref[...]), axis=1)
    hi, lo = split(diag_ref[...])
    got = dot(hi, both) + dot(lo, both)
    got = got[:, :width] + got[:, width:]
    out_ref[...] = got.T if turned else got


def diagonal(diag_tile, cols, turned):
    size, width = cols.shape
    return call(
        functools.partial(diag_kernel, turned),
        jax.ShapeDtypeStruct((width, size) if turned else (size, width), f32),
        [in_vmem, in_vmem],
        flops=8 * size * size * width,
        moved=4 * size * (size + 2 * width),
    )(diag_tile, cols)


def weights_kernel(table_ref, index_ref, out_ref):
    entries = table_ref.shape[1]
    part = index_ref.shape[1]
    hot = (lax.broadcasted_iota(jnp.int32, (entries, part), 0) == index_ref[...]).astype(f32)
    out_ref[...] = jnp.dot(
        table_ref[...], hot, precision=lax.Precision.HIGHEST, preferred_element_type=f32
    )


def row_kernel(count, turned, offs_ref, ranks_ref, got_ref, left_ref, diag_ref, out_ref, picked):
    terms, rank, size = left_ref.shape
    width = got_ref.shape[3]
    reach = got_ref.shape[0] // 2
    me = lax.axis_index("tile")
    line = lax.broadcasted_iota(jnp.int32, (rank, width), 0)
    for k in range(terms):
        offset = offs_ref[0, k]
        if got_ref.shape[1] == 2:
            piece = got_ref[lax.rem(me + offset + count, count), jnp.where(offset > 0, 0, 1)]
        else:
            piece = got_ref[jnp.where(offset < 0, offset + reach, offset + reach - 1), 0]
        picked[pl.ds(k * rank, rank)] = jnp.where(line < ranks_ref[0, k], piece, 0.0)
    both = jnp.concatenate(split(picked[...].T), axis=0)
    hi, lo = split(left_ref[...].reshape(terms * rank, size))
    total = dot(both, hi) + dot(both, lo)
    total = total[:width] + total[width:]
    if turned:
        total = total + diag_ref[...]
        part = out_ref.shape[2]
        for at in range(out_ref.shape[0]):
            out_ref[at] = total[:, at * part : (at + 1) * part]
    else:
        out_ref[...] = total.T + diag_ref[...]


def rows(offsets, ranks, got, left_tile, diag_part, groups, turned):
    terms, rank, size = left_tile.shape
    width = got.shape[3]
    shape = (groups, width, size // groups) if turned else (size, width)
    return call(
        functools.partial(row_kernel, lax.axis_size("tile"), turned),
        jax.ShapeDtypeStruct(shape, f32),
        [in_smem, in_smem, in_vmem, in_vmem, in_vmem],
        [pltpu.VMEM((terms * rank, width), f32)],
        flops=8 * terms * rank * size * width,
        moved=4 * terms * rank * (size + width),
    )(offsets, ranks, got, left_tile, diag_part)


def mix_kernel(fields_ref, weights_ref, out_ref):
    groups = fields_ref.shape[0]
    for a in range(groups):
        total = fields_ref[0] * weights_ref[pl.ds(a * groups, 1)]
        for b in range(1, groups):
            total = total + fields_ref[b] * weights_ref[pl.ds(a * groups + b, 1)]
        out_ref[a] = total.T


def deliver(coeffs, reach):
    count = lax.axis_size("tile")
    if paired(count, reach):
        return lax.all_to_all(coeffs, "tile", split_axis=0, concat_axis=0, tiled=True)
    arrived = []
    for slot in range(2 * reach):
        steps = -offset_of(slot, reach)
        pairs = [(source, (source + steps) % count) for source in range(count)]
        arrived.append(lax.ppermute(coeffs[slot], "tile", pairs))
    return jnp.stack(arrived)


def local(
    diag_tiles,
    left_factors,
    right_factors,
    tile_offsets,
    tile_ranks,
    mixing,
    block_index,
    rhs_field,
):
    diag_tile = diag_tiles[0, 0]
    left_tile = left_factors[0, 0]
    right_tile = right_factors[0, 0]
    offsets = tile_offsets[0]
    ranks = tile_ranks[0]
    reach = right_tile.shape[0] // 2
    groups = lax.axis_size("kern")
    own_group = lax.axis_index("kern")
    size, width = rhs_field.shape[1:]
    part = size // groups

    def apply_kernel(cols, turned):
        got = deliver(coefficients(cols, right_tile), reach)
        diag_part = diagonal(diag_tile, cols, turned)
        return rows(offsets, ranks, got, left_tile, diag_part, groups, turned)

    first = apply_kernel(rhs_field[0], True)
    fields = lax.all_to_all(first, "kern", split_axis=0, concat_axis=0, tiled=True)
    table = mixing.reshape(mixing.shape[0], groups * groups).T
    index = lax.dynamic_slice_in_dim(block_index, own_group * part, part)[None]
    weights = call(
        weights_kernel, jax.ShapeDtypeStruct((groups * groups, part), f32), [in_vmem, in_vmem]
    )(table, index)
    blended = call(
        mix_kernel,
        jax.ShapeDtypeStruct((groups, part, width), f32),
        [in_vmem, in_vmem],
        flops=2 * groups * groups * part * width,
        moved=8 * groups * part * width,
    )(fields, weights)
    mixed = lax.all_to_all(blended, "kern", split_axis=0, concat_axis=0, tiled=True)
    return apply_kernel(mixed.reshape(size, width), False)[None]


def solution(mesh):
    in_specs = (
        P("kern", "tile", None, None),
        P("kern", "tile", None, None, None),
        P("kern", "tile", None, None, None),
        P("kern", "tile", None),
        P("kern", "tile", None),
        P(),
        P("tile"),
        P("kern", "tile", None),
    )
    out_specs = P("kern", "tile", None)
    return jax.shard_map(local, mesh=mesh, in_specs=in_specs, out_specs=out_specs, check_vma=False)
```

```python
import functools

import jax
import jax.numpy as jnp
from jax import lax
from jax.experimental import pallas as pl
from jax.experimental.pallas import tpu as pltpu
from jax.sharding import PartitionSpec as P

f32 = jnp.float32
bf16 = jnp.bfloat16
VMEM_BYTES = 24 * 1024 * 1024
in_vmem = pl.BlockSpec(memory_space=pltpu.VMEM)
in_smem = pl.BlockSpec(memory_space=pltpu.SMEM)
in_hbm = pl.BlockSpec(memory_space=pltpu.HBM)


def to_hbm(value):
    return pltpu.with_memory_space_constraint(value, pltpu.HBM)


def split(value):
    hi = value.astype(bf16)
    return hi, (value - hi.astype(f32)).astype(bf16)


def dot(left, right):
    return jnp.dot(left, right, preferred_element_type=f32)


def call(kernel, outs, out_specs, in_specs, scratch=(), flops=0, moved=0):
    return pl.pallas_call(
        kernel,
        out_shape=outs,
        in_specs=in_specs,
        out_specs=out_specs,
        scratch_shapes=list(scratch),
        compiler_params=pltpu.CompilerParams(vmem_limit_bytes=VMEM_BYTES),
        cost_estimate=pl.CostEstimate(flops=flops, bytes_accessed=moved, transcendentals=0),
    )


def struct(*shape, dtype=f32):
    return jax.ShapeDtypeStruct(shape, dtype)


def offset_of(slot, reach):
    return slot - reach if slot < reach else slot - reach + 1


def paired(count, reach):
    return reach < count <= 2 * reach


def partner(me, step, count):
    if count & (count - 1) == 0:
        return me ^ step, me ^ step
    return lax.rem(me + step, count), lax.rem(me + count - step, count)


def exchange(values, axis):
    count = lax.axis_size(axis)
    arrived = [values[0]]
    for step in range(1, count):
        if count & (count - 1) == 0:
            pairs = [(source, source ^ step) for source in range(count)]
        else:
            pairs = [(source, (source + step) % count) for source in range(count)]
        arrived.append(lax.ppermute(values[step], axis, pairs))
    return arrived


def send_rows(count, slot, reach, piece, held, out_ref, sems):
    held[slot] = piece
    if paired(count, reach):
        offset = offset_of(slot, reach)
        dest = lax.rem(lax.axis_index("tile") - offset + count, count)
        target = out_ref.at[dest, 0 if offset > 0 else 1]
    else:
        target = out_ref.at[slot, 0]
    copy = pltpu.make_async_copy(held.at[slot], target, sems.at[slot])
    copy.start()
    return copy


def first_coeff_kernel(count, chunks, cols_ref, right_ref, out_ref, cols, right, held, in_sems, out_sems):
    slots, rank, size = right_ref.shape
    width = cols_ref.shape[1]
    step = slots // chunks
    cols_copy = pltpu.make_async_copy(cols_ref, cols, in_sems.at[chunks])
    cols_copy.start()
    copies = []
    for at in range(chunks):
        part = pl.ds(at * step, step)
        copies.append(pltpu.make_async_copy(right_ref.at[part], right.at[part], in_sems.at[at]))
        copies[-1].start()
    cols_copy.wait()
    both = jnp.concatenate(split(cols[...]), axis=1)
    sent = []
    for at in range(chunks):
        copies[at].wait()
        hi, lo = split(right[pl.ds(at * step, step)].reshape(step * rank, size))
        got = dot(hi, both) + dot(lo, both)
        got = got[:, :width] + got[:, width:]
        for s in range(step):
            piece = got[s * rank : (s + 1) * rank]
            sent.append(send_rows(count, at * step + s, slots // 2, piece, held, out_ref, out_sems))
    for copy in sent:
        copy.wait()


def lead_shape(count, slots):
    return (count, 2) if paired(count, slots // 2) else (slots, 1)


def first_coefficients(cols, right_tile):
    count = lax.axis_size("tile")
    slots, rank, size = right_tile.shape
    width = cols.shape[1]
    chunks = 4 if slots % 4 == 0 else 1
    return call(
        functools.partial(first_coeff_kernel, count, chunks),
        pltpu.HBM(lead_shape(count, slots) + (rank, width), f32),
        in_hbm,
        [in_hbm, in_hbm],
        [
            pltpu.VMEM(cols.shape, f32),
            pltpu.VMEM(right_tile.shape, f32),
            pltpu.VMEM((slots, rank, width), f32),
            pltpu.SemaphoreType.DMA((chunks + 1,)),
            pltpu.SemaphoreType.DMA((slots,)),
        ],
        flops=8 * slots * rank * size * width,
        moved=4 * slots * rank * (size + width),
    )(to_hbm(cols), to_hbm(right_tile))


def next_coeff_kernel(count, chunks, groups, *refs):
    parts = refs[:groups]
    hi_ref, lo_ref, out_ref, cols_ref, held, out_sems = refs[groups:]
    slots, rank, width = held.shape
    step = slots // chunks
    part, width = parts[0].shape
    me = lax.axis_index("kern")
    for at in range(groups):
        source = partner(me, at, groups)[1]
        cols_ref[pl.ds(pl.multiple_of(source * part, part), part)] = parts[at][...]
    both = jnp.concatenate(split(cols_ref[...]), axis=1)
    sent = []
    for at in range(chunks):
        span = pl.ds(at * step * rank, step * rank)
        got = dot(hi_ref[span], both) + dot(lo_ref[span], both)
        got = got[:, :width] + got[:, width:]
        for s in range(step):
            piece = got[s * rank : (s + 1) * rank]
            sent.append(send_rows(count, at * step + s, slots // 2, piece, held, out_ref, out_sems))
    for copy in sent:
        copy.wait()


def next_coefficients(parts, right_hi, right_lo, slots):
    count = lax.axis_size("tile")
    groups = len(parts)
    part, width = parts[0].shape
    total, size = right_hi.shape
    rank = total // slots
    chunks = 4 if slots % 4 == 0 else 1
    return call(
        functools.partial(next_coeff_kernel, count, chunks, groups),
        [pltpu.HBM(lead_shape(count, slots) + (rank, width), f32), struct(size, width)],
        [in_hbm, in_vmem],
        [in_vmem] * (groups + 2),
        [pltpu.VMEM((slots, rank, width), f32), pltpu.SemaphoreType.DMA((slots,))],
        flops=8 * slots * rank * size * width,
        moved=4 * slots * rank * (size + width),
    )(*parts, right_hi, right_lo)


def times_diag(diag_ref, cols_ref):
    width = cols_ref.shape[1]
    both = jnp.concatenate(split(cols_ref[...]), axis=1)
    hi, lo = split(diag_ref[...])
    got = dot(hi, both) + dot(lo, both)
    return got[:, :width] + got[:, width:]


def diag_kernel(diag_ref, cols_ref, out_ref):
    out_ref[...] = times_diag(diag_ref, cols_ref)


def diagonal(diag_tile, cols):
    size, width = cols.shape
    return call(
        diag_kernel,
        struct(size, width),
        in_vmem,
        [in_vmem, in_vmem],
        flops=8 * size * size * width,
        moved=4 * size * (size + 2 * width),
    )(diag_tile, cols)


def prepare_kernel(
    diag_ref, cols_ref, left_ref, right_ref, table_ref, index_ref,
    diag_out, left_hi, left_lo, right_hi, right_lo, weights_ref,
):
    diag_out[...] = times_diag(diag_ref, cols_ref).T
    for whole, hi_ref, lo_ref in ((left_ref, left_hi, left_lo), (right_ref, right_hi, right_lo)):
        rank = whole.shape[1]
        for at in range(whole.shape[0]):
            span = pl.ds(at * rank, rank)
            hi_ref[span], lo_ref[span] = split(whole[at])
    entries = table_ref.shape[1]
    part = index_ref.shape[1]
    index = index_ref[pl.ds(lax.axis_index("kern"), 1)]
    hot = (lax.broadcasted_iota(jnp.int32, (entries, part), 0) == index).astype(f32)
    weights_ref[...] = jnp.dot(
        table_ref[...], hot, precision=lax.Precision.HIGHEST, preferred_element_type=f32
    )


def prepare(diag_tile, cols, left_tile, right_tile, table, index):
    size, width = cols.shape
    terms, rank, _ = left_tile.shape
    slots = right_tile.shape[0]
    return call(
        prepare_kernel,
        [
            struct(width, size),
            struct(terms * rank, size, dtype=bf16),
            struct(terms * rank, size, dtype=bf16),
            struct(slots * rank, size, dtype=bf16),
            struct(slots * rank, size, dtype=bf16),
            struct(table.shape[0], index.shape[1]),
        ],
        [in_vmem] * 6,
        [in_vmem] * 6,
        flops=8 * size * size * width,
        moved=8 * (terms + slots) * rank * size + 4 * size * (size + 2 * width),
    )(diag_tile, cols, left_tile, right_tile, table, index)


def row_kernel(count, terms, groups, offs_ref, ranks_ref, got_ref, hi_ref, lo_ref, diag_ref, *refs):
    outs, (picked, sems) = refs[:-2], refs[-2:]
    rank, width = got_ref.shape[2:]
    reach = got_ref.shape[0] // 2
    me = lax.axis_index("tile")
    copies = []
    for k in range(terms):
        offset = offs_ref[0, k]
        if got_ref.shape[1] == 2:
            block = got_ref.at[lax.rem(me + offset + count, count), jnp.where(offset > 0, 0, 1)]
        else:
            block = got_ref.at[jnp.where(offset < 0, offset + reach, offset + reach - 1), 0]
        copies.append(pltpu.make_async_copy(block, picked.at[pl.ds(k * rank, rank)], sems.at[k]))
        copies[-1].start()
    line = lax.broadcasted_iota(jnp.int32, (rank, width), 0)
    pieces = []
    for k in range(terms):
        copies[k].wait()
        piece = picked[pl.ds(k * rank, rank)]
        pieces.append(jnp.where(line < ranks_ref[0, k], piece, 0.0))
    both = jnp.concatenate(split(jnp.concatenate(pieces, axis=0).T), axis=0)
    total = dot(both, hi_ref[...]) + dot(both, lo_ref[...])
    total = total[:width] + total[width:]
    if groups > 1:
        total = total + diag_ref[...]
        part = total.shape[1] // groups
        stage = refs[-3]
        for at in range(groups):
            stage[at] = total[:, at * part : (at + 1) * part]
        own = lax.axis_index("kern")
        for at in range(groups):
            outs[at][...] = stage[partner(own, at, groups)[0]]
    else:
        outs[0][...] = total.T + diag_ref[...]


def rows(offsets, ranks, got, left_hi, left_lo, diag_part, groups):
    total, size = left_hi.shape
    rank, width = got.shape[2:]
    terms = total // rank
    part = size // groups
    outs = [struct(width, part)] * groups if groups > 1 else [struct(size, width)]
    scratch = [pltpu.VMEM((total, width), f32), pltpu.SemaphoreType.DMA((terms,))]
    if groups > 1:
        scratch = [pltpu.VMEM((groups, width, part), f32)] + scratch
    return call(
        functools.partial(row_kernel, lax.axis_size("tile"), terms, groups),
        outs,
        [in_vmem] * len(outs),
        [in_smem, in_smem, in_hbm, in_vmem, in_vmem, in_vmem],
        scratch,
        flops=8 * total * size * width,
        moved=4 * total * (size + width),
    )(offsets, ranks, to_hbm(got), left_hi, left_lo, diag_part)


def mix_kernel(groups, *refs):
    fields, weights_ref, outs = refs[:groups], refs[groups], refs[groups + 1 :]
    me = lax.axis_index("kern")
    for at in range(groups):
        base = partner(me, at, groups)[0] * groups
        total = None
        for b in range(groups):
            term = fields[b][...] * weights_ref[pl.ds(base + partner(me, b, groups)[1], 1)]
            total = term if total is None else total + term
        outs[at][...] = total.T


def mix(fields, weights):
    groups = len(fields)
    width, part = fields[0].shape
    return call(
        functools.partial(mix_kernel, groups),
        [struct(part, width)] * groups,
        [in_vmem] * groups,
        [in_vmem] * (groups + 1),
        flops=2 * groups * groups * part * width,
        moved=8 * groups * part * width,
    )(*fields, weights)


def deliver(coeffs, reach):
    count = lax.axis_size("tile")
    if paired(count, reach):
        return lax.all_to_all(coeffs, "tile", split_axis=0, concat_axis=0, tiled=True)
    arrived = []
    for slot in range(2 * reach):
        steps = -offset_of(slot, reach)
        pairs = [(source, (source + steps) % count) for source in range(count)]
        arrived.append(lax.ppermute(coeffs[slot], "tile", pairs))
    return jnp.stack(arrived)


def local(
    diag_tiles,
    left_factors,
    right_factors,
    tile_offsets,
    tile_ranks,
    mixing,
    block_index,
    rhs_field,
):
    diag_tile = diag_tiles[0, 0]
    left_tile = left_factors[0, 0]
    right_tile = right_factors[0, 0]
    offsets = tile_offsets[0]
    ranks = tile_ranks[0]
    slots = right_tile.shape[0]
    groups = lax.axis_size("kern")
    size = rhs_field.shape[1]
    table = mixing.reshape(mixing.shape[0], groups * groups).T
    index = block_index.reshape(groups, size // groups)
    cols = rhs_field[0]

    got = deliver(first_coefficients(cols, right_tile), slots // 2)
    diag_part, left_hi, left_lo, right_hi, right_lo, weights = prepare(
        diag_tile, cols, left_tile, right_tile, table, index
    )
    first = rows(offsets, ranks, got, left_hi, left_lo, diag_part, groups)
    mixed = exchange(mix(exchange(first, "kern"), weights), "kern")
    coeffs, cols = next_coefficients(mixed, right_hi, right_lo, slots)
    got = deliver(coeffs, slots // 2)
    diag_part = diagonal(diag_tile, cols)
    return rows(offsets, ranks, got, left_hi, left_lo, diag_part, 1)[0][None]


def solution(mesh):
    in_specs = (
        P("kern", "tile", None, None),
        P("kern", "tile", None, None, None),
        P("kern", "tile", None, None, None),
        P("kern", "tile", None),
        P("kern", "tile", None),
        P(),
        P("tile"),
        P("kern", "tile", None),
    )
    out_specs = P("kern", "tile", None)
    return jax.shard_map(local, mesh=mesh, in_specs=in_specs, out_specs=out_specs, check_vma=False)
```

```python
import functools

import jax
import jax.numpy as jnp
from jax import lax
from jax.experimental import pallas as pl
from jax.experimental.pallas import tpu as pltpu
from jax.sharding import PartitionSpec as P

f32 = jnp.float32
bf16 = jnp.bfloat16
VMEM_BYTES = 24 * 1024 * 1024
in_vmem = pl.BlockSpec(memory_space=pltpu.VMEM)
in_smem = pl.BlockSpec(memory_space=pltpu.SMEM)
in_hbm = pl.BlockSpec(memory_space=pltpu.HBM)


def to_hbm(value):
    return pltpu.with_memory_space_constraint(value, pltpu.HBM)


def struct(*shape, dtype=f32):
    return jax.ShapeDtypeStruct(shape, dtype)


def split(value):
    hi = value.astype(bf16)
    return hi, (value - hi.astype(f32)).astype(bf16)


def side_by_side(value):
    return jnp.concatenate(split(value), axis=1)


def dot(left, right):
    return jnp.dot(left, right, preferred_element_type=f32)


def fold(value):
    width = value.shape[1] // 2
    return value[:, :width] + value[:, width:]


def call(kernel, outs, out_specs, in_specs, scratch=(), flops=0, moved=0):
    return pl.pallas_call(
        kernel,
        out_shape=outs,
        in_specs=in_specs,
        out_specs=out_specs,
        scratch_shapes=list(scratch),
        compiler_params=pltpu.CompilerParams(vmem_limit_bytes=VMEM_BYTES),
        cost_estimate=pl.CostEstimate(flops=flops, bytes_accessed=moved, transcendentals=0),
    )


def step_pairs(count, step):
    if count & (count - 1) == 0:
        return [(source, source ^ step) for source in range(count)]
    return [(source, (source + step) % count) for source in range(count)]


def partner(me, step, count):
    if count & (count - 1) == 0:
        return me ^ step, me ^ step
    return lax.rem(me + step, count), lax.rem(me + count - step, count)


def exchange(values, axis):
    count = lax.axis_size(axis)
    arrived = [values[0]]
    for step in range(1, count):
        arrived.append(lax.ppermute(values[step], axis, step_pairs(count, step)))
    return arrived


class Message:
    def __init__(self, count, reach, step=None, slot=None):
        self.count, self.reach, self.step, self.slot = count, reach, step, slot
        if slot is not None:
            offset = slot - reach if slot < reach else slot - reach + 1
            self.width = 1
            self.pairs = [(source, (source - offset) % count) for source in range(count)]
        else:
            self.pairs = step_pairs(count, step)
            self.width = 1
            for source, dest in self.pairs:
                ahead = (source - dest) % count
                if ahead <= reach and count - ahead <= reach:
                    self.width = 2

    def slots(self, me, sending):
        if self.slot is not None:
            return [(self.slot, True)]
        count, reach = self.count, self.reach
        dest, source = partner(me, self.step, count)
        column, row = (me, dest) if sending else (source, me)
        ahead = lax.rem(column - row + count, count)
        first = jnp.where(ahead <= reach, ahead + reach - 1, ahead - count + reach)
        if self.width == 1:
            return [(first, True)]
        both = jnp.logical_and(ahead <= reach, count - ahead <= reach)
        return [(first, True), (jnp.where(both, ahead - count + reach, first), both)]


def messages_of(count, slots):
    reach = slots // 2
    if reach < count <= 2 * reach:
        return [Message(count, reach, step=step) for step in range(count - 1, 0, -1)]
    return [Message(count, reach, slot=slot) for slot in range(slots)]


def chunks_of(messages, most=4):
    chunks, held = [[]], 0
    for at, message in enumerate(messages):
        if held and held + message.width > most:
            chunks.append([])
            held = 0
        chunks[-1].append(at)
        held += message.width
    return chunks


def chunk_coefficients(split_ref, base, chunk, messages, rank, both, outs):
    size = rank * sum(messages[at].width for at in chunk)
    got = fold(dot(split_ref[pl.ds(base, 2 * size)], both))
    got = got[:size] + got[size:]
    row = 0
    for at in chunk:
        for w in range(messages[at].width):
            outs[at][w] = got[row : row + rank]
            row += rank
    return base + 2 * size


def first_coeff_kernel(messages, cols_ref, right_ref, *refs):
    outs, (split_ref, cols, right, sems) = refs[: len(messages)], refs[len(messages) :]
    rank = right_ref.shape[1]
    me = lax.axis_index("tile")
    cols_copy = pltpu.make_async_copy(cols_ref, cols, sems.at[right.shape[0]])
    cols_copy.start()
    copies = []
    for message in messages:
        for slot, _ in message.slots(me, True):
            at = len(copies)
            copies.append(pltpu.make_async_copy(right_ref.at[slot], right.at[at], sems.at[at]))
            copies[-1].start()
    cols_copy.wait()
    both = side_by_side(cols[...])
    base, block = 0, 0
    for chunk in chunks_of(messages):
        blocks = sum(messages[at].width for at in chunk)
        for b in range(blocks):
            copies[block].wait()
            hi, lo = split(right[block])
            split_ref[pl.ds(base + b * rank, rank)] = hi
            split_ref[pl.ds(base + (blocks + b) * rank, rank)] = lo
            block += 1
        base = chunk_coefficients(split_ref, base, chunk, messages, rank, both, outs)


def first_coefficients(cols, right_tile):
    slots, rank, size = right_tile.shape
    messages = messages_of(lax.axis_size("tile"), slots)
    blocks = sum(message.width for message in messages)
    width = cols.shape[1]
    outs = [struct(message.width, rank, width) for message in messages]
    outs.append(struct(2 * blocks * rank, size, dtype=bf16))
    got = call(
        functools.partial(first_coeff_kernel, messages),
        outs,
        [in_vmem] * len(outs),
        [in_hbm, in_hbm],
        [
            pltpu.VMEM(cols.shape, f32),
            pltpu.VMEM((blocks, rank, size), f32),
            pltpu.SemaphoreType.DMA((blocks + 1,)),
        ],
        flops=8 * blocks * rank * size * width,
        moved=4 * blocks * rank * (2 * size + width),
    )(to_hbm(cols), to_hbm(right_tile))
    return got[:-1], got[-1]


def next_coeff_kernel(messages, groups, *refs):
    parts, split_ref = refs[:groups], refs[groups]
    outs, cols_ref = refs[groups + 1 : -1], refs[-1]
    part = parts[0].shape[0]
    rank = outs[0].shape[1]
    me = lax.axis_index("kern")
    for at in range(groups):
        source = partner(me, at, groups)[1]
        cols_ref[pl.ds(pl.multiple_of(source * part, part), part)] = parts[at][...]
    both = side_by_side(cols_ref[...])
    base = 0
    for chunk in chunks_of(messages):
        base = chunk_coefficients(split_ref, base, chunk, messages, rank, both, outs)


def next_coefficients(parts, split_right, slots, rank):
    messages = messages_of(lax.axis_size("tile"), slots)
    groups = len(parts)
    part, width = parts[0].shape
    size = part * groups
    total = split_right.shape[0]
    outs = [struct(message.width, rank, width) for message in messages]
    outs.append(struct(size, width))
    got = call(
        functools.partial(next_coeff_kernel, messages, groups),
        outs,
        [in_vmem] * len(outs),
        [in_vmem] * (groups + 1),
        flops=4 * total * size * width,
        moved=2 * total * (size + width),
    )(*parts, split_right)
    return got[:-1], got[-1]


def times_diag(diag_ref, cols_ref):
    both = side_by_side(cols_ref[...])
    hi, lo = split(diag_ref[...])
    return fold(dot(hi, both) + dot(lo, both))


def diag_kernel(diag_ref, cols_ref, out_ref):
    out_ref[...] = times_diag(diag_ref, cols_ref)


def diagonal(diag_tile, cols):
    size, width = cols.shape
    return call(
        diag_kernel,
        struct(size, width),
        in_vmem,
        [in_vmem, in_vmem],
        flops=8 * size * size * width,
        moved=4 * size * (size + 2 * width),
    )(diag_tile, cols)


def prepare_kernel(
    diag_ref, cols_ref, left_ref, table_ref, index_ref, diag_out, left_hi, left_lo, weights_ref
):
    diag_out[...] = times_diag(diag_ref, cols_ref)
    total = left_ref.shape[0]
    step = 128 if total % 128 == 0 else total
    for at in range(0, total, step):
        span = slice(at, at + step)
        left_hi[:, span], left_lo[:, span] = split(left_ref[span].T)
    entries = table_ref.shape[1]
    part = index_ref.shape[1]
    index = index_ref[pl.ds(lax.axis_index("kern"), 1)]
    hot = (lax.broadcasted_iota(jnp.int32, (entries, part), 0) == index).astype(f32)
    weights = jnp.dot(
        table_ref[...], hot, precision=lax.Precision.HIGHEST, preferred_element_type=f32
    )
    width = weights_ref.shape[2]
    for at in range(weights_ref.shape[0]):
        weights_ref[at] = jnp.broadcast_to(weights[at : at + 1], (width, part)).T


def prepare(diag_tile, cols, left_rows, table, index):
    size, width = cols.shape
    total = left_rows.shape[0]
    part = index.shape[1]
    return call(
        prepare_kernel,
        [
            struct(size, width),
            struct(size, total, dtype=bf16),
            struct(size, total, dtype=bf16),
            struct(table.shape[0], part, width),
        ],
        [in_vmem] * 4,
        [in_vmem] * 5,
        flops=8 * size * size * width,
        moved=8 * total * size + 4 * size * (size + 2 * width),
    )(diag_tile, cols, left_rows, table, index)


def row_kernel(messages, groups, offs_ref, ranks_ref, *refs):
    gots = refs[: len(messages)]
    hi_ref, lo_ref, diag_ref = refs[len(messages) : len(messages) + 3]
    outs, (stage, picked, term_of) = refs[len(messages) + 3 : -3], refs[-3:]
    terms = offs_ref.shape[1]
    rank, width = gots[0].shape[1:]
    slots = term_of.shape[0]
    reach = slots // 2
    for slot in range(slots):
        term_of[slot] = -1
    for k in range(terms):
        offset = offs_ref[0, k]
        term_of[jnp.where(offset < 0, offset + reach, offset + reach - 1)] = k
    me = lax.axis_index("tile")
    line = lax.broadcasted_iota(jnp.int32, (rank, width), 0)

    def pick(got, w, term):
        @pl.when(term >= 0)
        def _():
            kept = jnp.where(line < ranks_ref[0, term], got[w], 0.0)
            picked[pl.ds(pl.multiple_of(term * rank, rank), rank)] = kept

    for got, message in zip(gots, messages):
        for w, (slot, there) in enumerate(message.slots(me, False)):
            pick(got, w, jnp.where(there, term_of[slot], -1))
    both = side_by_side(picked[...])
    total = fold(dot(hi_ref[...], both) + dot(lo_ref[...], both)) + diag_ref[...]
    if groups == 1:
        outs[0][...] = total
        return
    stage[...] = total
    part = total.shape[0] // groups
    own = lax.axis_index("kern")
    for at in range(groups):
        dest = partner(own, at, groups)[0]
        outs[at][...] = stage[pl.ds(pl.multiple_of(dest * part, part), part)]


def rows(offsets, ranks, gots, left_hi, left_lo, diag_part, slots, groups):
    size, total = left_hi.shape
    width = diag_part.shape[1]
    messages = messages_of(lax.axis_size("tile"), slots)
    return call(
        functools.partial(row_kernel, messages, groups),
        [struct(size // groups, width)] * groups,
        [in_vmem] * groups,
        [in_smem, in_smem] + [in_vmem] * (len(messages) + 3),
        [
            pltpu.VMEM((size, width), f32),
            pltpu.VMEM((total, width), f32),
            pltpu.SMEM((slots,), jnp.int32),
        ],
        flops=8 * total * size * width,
        moved=4 * total * (size + width),
    )(offsets, ranks, *gots, left_hi, left_lo, diag_part)


def mix_kernel(groups, *refs):
    fields, weights_ref, outs = refs[:groups], refs[groups], refs[groups + 1 :]
    me = lax.axis_index("kern")
    for at in range(groups):
        base = partner(me, at, groups)[0] * groups
        total = None
        for b in range(groups):
            term = fields[b][...] * weights_ref[base + partner(me, b, groups)[1]]
            total = term if total is None else total + term
        outs[at][...] = total


def mix(fields, weights):
    groups = len(fields)
    part, width = fields[0].shape
    return call(
        functools.partial(mix_kernel, groups),
        [struct(part, width)] * groups,
        [in_vmem] * groups,
        [in_vmem] * (groups + 1),
        flops=2 * groups * groups * part * width,
        moved=8 * groups * part * width,
    )(*fields, weights)


def deliver(coeffs, slots):
    messages = messages_of(lax.axis_size("tile"), slots)
    return [lax.ppermute(sent, "tile", message.pairs) for sent, message in zip(coeffs, messages)]


def local(
    diag_tiles,
    left_factors,
    right_factors,
    tile_offsets,
    tile_ranks,
    mixing,
    block_index,
    rhs_field,
):
    diag_tile = diag_tiles[0, 0]
    right_tile = right_factors[0, 0]
    offsets = tile_offsets[0]
    ranks = tile_ranks[0]
    slots, rank, size = right_tile.shape
    groups = lax.axis_size("kern")
    left_rows = left_factors.reshape(-1, size)
    table = mixing.reshape(mixing.shape[0], groups * groups).T
    index = block_index.reshape(groups, size // groups)
    cols = rhs_field[0]

    coeffs, split_right = first_coefficients(cols, right_tile)
    gots = deliver(coeffs, slots)
    diag_part, left_hi, left_lo, weights = prepare(diag_tile, cols, left_rows, table, index)
    first = rows(offsets, ranks, gots, left_hi, left_lo, diag_part, slots, groups)
    mixed = exchange(mix(exchange(first, "kern"), weights), "kern")
    coeffs, cols = next_coefficients(mixed, split_right, slots, rank)
    gots = deliver(coeffs, slots)
    diag_part = diagonal(diag_tile, cols)
    return rows(offsets, ranks, gots, left_hi, left_lo, diag_part, slots, 1)[0][None]


def solution(mesh):
    in_specs = (
        P("kern", "tile", None, None),
        P("kern", "tile", None, None, None),
        P("kern", "tile", None, None, None),
        P("kern", "tile", None),
        P("kern", "tile", None),
        P(),
        P("tile"),
        P("kern", "tile", None),
    )
    out_specs = P("kern", "tile", None)
    return jax.shard_map(local, mesh=mesh, in_specs=in_specs, out_specs=out_specs, check_vma=False)
```

```python
import functools

import jax
import jax.numpy as jnp
from jax import lax
from jax.experimental import pallas as pl
from jax.experimental.pallas import tpu as pltpu
from jax.sharding import PartitionSpec as P

f32 = jnp.float32
bf16 = jnp.bfloat16
VMEM_BYTES = 24 * 1024 * 1024
in_vmem = pl.BlockSpec(memory_space=pltpu.VMEM)
in_smem = pl.BlockSpec(memory_space=pltpu.SMEM)
in_hbm = pl.BlockSpec(memory_space=pltpu.HBM)


def to_hbm(value):
    return pltpu.with_memory_space_constraint(value, pltpu.HBM)


def struct(*shape, dtype=f32):
    return jax.ShapeDtypeStruct(shape, dtype)


def split(value):
    hi = value.astype(bf16)
    return hi, (value - hi.astype(f32)).astype(bf16)


def side_by_side(value):
    return jnp.concatenate(split(value), axis=1)


def dot(left, right):
    return jnp.dot(left, right, preferred_element_type=f32)


def fold(value):
    width = value.shape[1] // 2
    return value[:, :width] + value[:, width:]


def call(kernel, outs, out_specs, in_specs, scratch=(), flops=0, moved=0):
    return pl.pallas_call(
        kernel,
        out_shape=outs,
        in_specs=in_specs,
        out_specs=out_specs,
        scratch_shapes=list(scratch),
        compiler_params=pltpu.CompilerParams(vmem_limit_bytes=VMEM_BYTES),
        cost_estimate=pl.CostEstimate(flops=flops, bytes_accessed=moved, transcendentals=0),
    )


def step_pairs(count, step):
    if count & (count - 1) == 0:
        return [(source, source ^ step) for source in range(count)]
    return [(source, (source + step) % count) for source in range(count)]


def partner(me, step, count):
    if count & (count - 1) == 0:
        return me ^ step, me ^ step
    return lax.rem(me + step, count), lax.rem(me + count - step, count)


class Message:
    def __init__(self, count, reach, step=None, slot=None):
        self.count, self.reach, self.step, self.slot = count, reach, step, slot
        if slot is not None:
            offset = slot - reach if slot < reach else slot - reach + 1
            self.width = 1
            self.pairs = [(source, (source - offset) % count) for source in range(count)]
        else:
            self.pairs = step_pairs(count, step)
            self.width = 1
            for source, dest in self.pairs:
                ahead = (source - dest) % count
                if ahead <= reach and count - ahead <= reach:
                    self.width = 2

    def slots(self, me, sending):
        if self.slot is not None:
            return [(self.slot, True)]
        count, reach = self.count, self.reach
        dest, source = partner(me, self.step, count)
        column, row = (me, dest) if sending else (source, me)
        ahead = lax.rem(column - row + count, count)
        first = jnp.where(ahead <= reach, ahead + reach - 1, ahead - count + reach)
        if self.width == 1:
            return [(first, True)]
        both = jnp.logical_and(ahead <= reach, count - ahead <= reach)
        return [(first, True), (jnp.where(both, ahead - count + reach, first), both)]


def messages_of(count, slots):
    reach = slots // 2
    if reach < count <= 2 * reach:
        return [Message(count, reach, step=step) for step in range(count - 1, 0, -1)]
    return [Message(count, reach, slot=slot) for slot in range(slots)]


def chunks_of(messages, most=4):
    chunks, held = [[]], 0
    for at, message in enumerate(messages):
        if held and held + message.width > most:
            chunks.append([])
            held = 0
        chunks[-1].append(at)
        held += message.width
    return chunks


def chunk_coefficients(split_ref, base, chunk, messages, rank, both, outs):
    size = rank * sum(messages[at].width for at in chunk)
    got = fold(dot(split_ref[pl.ds(base, 2 * size)], both))
    got = got[:size] + got[size:]
    row = 0
    for at in chunk:
        for w in range(messages[at].width):
            outs[at][w] = got[row : row + rank]
            row += rank
    return base + 2 * size


def first_coeff_kernel(messages, cols_ref, right_ref, *refs):
    outs, (split_ref, cols, right, sems) = refs[: len(messages)], refs[len(messages) :]
    rank = right_ref.shape[1]
    me = lax.axis_index("tile")
    cols_copy = pltpu.make_async_copy(cols_ref, cols, sems.at[right.shape[0]])
    cols_copy.start()
    copies = []
    for message in messages:
        for slot, _ in message.slots(me, True):
            at = len(copies)
            copies.append(pltpu.make_async_copy(right_ref.at[slot], right.at[at], sems.at[at]))
            copies[-1].start()
    cols_copy.wait()
    both = side_by_side(cols[...])
    base, block = 0, 0
    for chunk in chunks_of(messages):
        blocks = sum(messages[at].width for at in chunk)
        for b in range(blocks):
            copies[block].wait()
            hi, lo = split(right[block])
            split_ref[pl.ds(base + b * rank, rank)] = hi
            split_ref[pl.ds(base + (blocks + b) * rank, rank)] = lo
            block += 1
        base = chunk_coefficients(split_ref, base, chunk, messages, rank, both, outs)


def first_coefficients(cols, right_tile):
    slots, rank, size = right_tile.shape
    messages = messages_of(lax.axis_size("tile"), slots)
    blocks = sum(message.width for message in messages)
    width = cols.shape[1]
    outs = [struct(message.width, rank, width) for message in messages]
    outs.append(struct(2 * blocks * rank, size, dtype=bf16))
    got = call(
        functools.partial(first_coeff_kernel, messages),
        outs,
        [in_vmem] * len(outs),
        [in_hbm, in_hbm],
        [
            pltpu.VMEM(cols.shape, f32),
            pltpu.VMEM((blocks, rank, size), f32),
            pltpu.SemaphoreType.DMA((blocks + 1,)),
        ],
        flops=8 * blocks * rank * size * width,
        moved=4 * blocks * rank * (2 * size + width),
    )(to_hbm(cols), to_hbm(right_tile))
    return got[:-1], got[-1]


def next_coeff_kernel(messages, fields_ref, weights_ref, split_ref, *refs):
    outs, cols_ref = refs[:-1], refs[-1]
    rank = outs[0].shape[1]
    mixed = fields_ref[0] * weights_ref[0]
    for b in range(1, fields_ref.shape[0]):
        mixed = mixed + fields_ref[b] * weights_ref[b]
    cols_ref[...] = mixed
    both = side_by_side(mixed)
    base = 0
    for chunk in chunks_of(messages):
        base = chunk_coefficients(split_ref, base, chunk, messages, rank, both, outs)


def next_coefficients(fields, weights, split_right, slots, rank):
    messages = messages_of(lax.axis_size("tile"), slots)
    _, size, width = fields.shape
    total = split_right.shape[0]
    outs = [struct(message.width, rank, width) for message in messages]
    outs.append(struct(size, width))
    got = call(
        functools.partial(next_coeff_kernel, messages),
        outs,
        [in_vmem] * len(outs),
        [in_vmem] * 3,
        flops=4 * total * size * width,
        moved=2 * total * (size + width),
    )(fields, weights, split_right)
    return got[:-1], got[-1]


def times_diag(diag_ref, cols_ref):
    both = side_by_side(cols_ref[...])
    hi, lo = split(diag_ref[...])
    return fold(dot(hi, both) + dot(lo, both))


def diag_kernel(diag_ref, cols_ref, out_ref):
    out_ref[...] = times_diag(diag_ref, cols_ref)


def diagonal(diag_tile, cols):
    size, width = cols.shape
    return call(
        diag_kernel,
        struct(size, width),
        in_vmem,
        [in_vmem, in_vmem],
        flops=8 * size * size * width,
        moved=4 * size * (size + 2 * width),
    )(diag_tile, cols)


def prepare_kernel(
    diag_ref, cols_ref, left_ref, table_ref, index_ref, diag_out, left_hi, left_lo, weights_ref
):
    diag_out[...] = times_diag(diag_ref, cols_ref)
    total = left_ref.shape[0]
    step = 128 if total % 128 == 0 else total
    for at in range(0, total, step):
        span = slice(at, at + step)
        left_hi[:, span], left_lo[:, span] = split(left_ref[span].T)
    own = table_ref[lax.axis_index("kern")]
    groups, entries = own.shape
    size = index_ref.shape[1]
    hot = (lax.broadcasted_iota(jnp.int32, (entries, size), 0) == index_ref[...]).astype(f32)
    weights = jnp.dot(own, hot, precision=lax.Precision.HIGHEST, preferred_element_type=f32)
    width = weights_ref.shape[2]
    for b in range(groups):
        weights_ref[b] = jnp.broadcast_to(weights[b : b + 1], (width, size)).T


def prepare(diag_tile, cols, left_rows, table, index):
    size, width = cols.shape
    total = left_rows.shape[0]
    return call(
        prepare_kernel,
        [
            struct(size, width),
            struct(size, total, dtype=bf16),
            struct(size, total, dtype=bf16),
            struct(table.shape[0], size, width),
        ],
        [in_vmem] * 4,
        [in_vmem] * 5,
        flops=8 * size * size * width,
        moved=8 * total * size + 4 * size * (size + 2 * width),
    )(diag_tile, cols, left_rows, table, index)


def row_kernel(messages, offs_ref, ranks_ref, *refs):
    gots = refs[: len(messages)]
    hi_ref, lo_ref, diag_ref = refs[len(messages) : len(messages) + 3]
    out_ref, picked, term_of = refs[-3:]
    terms = offs_ref.shape[1]
    rank, width = gots[0].shape[1:]
    slots = term_of.shape[0]
    reach = slots // 2
    for slot in range(slots):
        term_of[slot] = -1
    for k in range(terms):
        offset = offs_ref[0, k]
        term_of[jnp.where(offset < 0, offset + reach, offset + reach - 1)] = k
    me = lax.axis_index("tile")
    line = lax.broadcasted_iota(jnp.int32, (rank, width), 0)

    def pick(got, w, term):
        @pl.when(term >= 0)
        def _():
            kept = jnp.where(line < ranks_ref[0, term], got[w], 0.0)
            picked[pl.ds(pl.multiple_of(term * rank, rank), rank)] = kept

    for got, message in zip(gots, messages):
        for w, (slot, there) in enumerate(message.slots(me, False)):
            pick(got, w, jnp.where(there, term_of[slot], -1))
    both = side_by_side(picked[...])
    out_ref[...] = fold(dot(hi_ref[...], both) + dot(lo_ref[...], both)) + diag_ref[...]


def rows(offsets, ranks, gots, left_hi, left_lo, diag_part, slots):
    size, total = left_hi.shape
    width = diag_part.shape[1]
    messages = messages_of(lax.axis_size("tile"), slots)
    return call(
        functools.partial(row_kernel, messages),
        struct(size, width),
        in_vmem,
        [in_smem, in_smem] + [in_vmem] * (len(messages) + 3),
        [
            pltpu.VMEM((total, width), f32),
            pltpu.SMEM((slots,), jnp.int32),
        ],
        flops=8 * total * size * width,
        moved=4 * total * (size + width),
    )(offsets, ranks, *gots, left_hi, left_lo, diag_part)


def deliver(coeffs, slots):
    messages = messages_of(lax.axis_size("tile"), slots)
    return [lax.ppermute(sent, "tile", message.pairs) for sent, message in zip(coeffs, messages)]


def local(
    diag_tiles,
    left_factors,
    right_factors,
    tile_offsets,
    tile_ranks,
    mixing,
    block_index,
    rhs_field,
):
    diag_tile = diag_tiles[0, 0]
    right_tile = right_factors[0, 0]
    offsets = tile_offsets[0]
    ranks = tile_ranks[0]
    slots, rank, size = right_tile.shape
    left_rows = left_factors.reshape(-1, size)
    table = mixing.transpose(1, 2, 0)
    index = block_index[None]
    cols = rhs_field[0]

    coeffs, split_right = first_coefficients(cols, right_tile)
    gots = deliver(coeffs, slots)
    diag_part, left_hi, left_lo, weights = prepare(diag_tile, cols, left_rows, table, index)
    first = rows(offsets, ranks, gots, left_hi, left_lo, diag_part, slots)
    fields = lax.all_gather(first, "kern")
    coeffs, cols = next_coefficients(fields, weights, split_right, slots, rank)
    gots = deliver(coeffs, slots)
    diag_part = diagonal(diag_tile, cols)
    return rows(offsets, ranks, gots, left_hi, left_lo, diag_part, slots)[None]


def solution(mesh):
    in_specs = (
        P("kern", "tile", None, None),
        P("kern", "tile", None, None, None),
        P("kern", "tile", None, None, None),
        P("kern", "tile", None),
        P("kern", "tile", None),
        P(),
        P("tile"),
        P("kern", "tile", None),
    )
    out_specs = P("kern", "tile", None)
    return jax.shard_map(local, mesh=mesh, in_specs=in_specs, out_specs=out_specs, check_vma=False)
```

```python
import functools

import jax
import jax.numpy as jnp
from jax import lax
from jax.experimental import pallas as pl
from jax.experimental.pallas import tpu as pltpu
from jax.sharding import PartitionSpec as P

f32 = jnp.float32
bf16 = jnp.bfloat16
VMEM_BYTES = 24 * 1024 * 1024
in_vmem = pl.BlockSpec(memory_space=pltpu.VMEM)
in_smem = pl.BlockSpec(memory_space=pltpu.SMEM)
in_hbm = pl.BlockSpec(memory_space=pltpu.HBM)


def to_hbm(value):
    return pltpu.with_memory_space_constraint(value, pltpu.HBM)


def struct(*shape, dtype=f32):
    return jax.ShapeDtypeStruct(shape, dtype)


def split(value):
    hi = value.astype(bf16)
    return hi, (value - hi.astype(f32)).astype(bf16)


def side_by_side(value):
    return jnp.concatenate(split(value), axis=1)


def dot(left, right):
    return jnp.dot(left, right, preferred_element_type=f32)


def fold(value):
    width = value.shape[1] // 2
    return value[:, :width] + value[:, width:]


def call(kernel, outs, out_specs, in_specs, scratch=(), flops=0, moved=0):
    return pl.pallas_call(
        kernel,
        out_shape=outs,
        in_specs=in_specs,
        out_specs=out_specs,
        scratch_shapes=list(scratch),
        compiler_params=pltpu.CompilerParams(vmem_limit_bytes=VMEM_BYTES),
        cost_estimate=pl.CostEstimate(flops=flops, bytes_accessed=moved, transcendentals=0),
    )


def step_pairs(count, step):
    if count & (count - 1) == 0:
        return [(source, source ^ step) for source in range(count)]
    return [(source, (source + step) % count) for source in range(count)]


def partner(me, step, count):
    if count & (count - 1) == 0:
        return me ^ step, me ^ step
    return lax.rem(me + step, count), lax.rem(me + count - step, count)


def gather_fields(halves):
    count = lax.axis_size("kern")
    if count == 4 and len(halves) == 2:
        near, across = step_pairs(count, 1), step_pairs(count, 2)
        low, high = halves
        near_low = lax.ppermute(low, "kern", near)
        across_high = lax.ppermute(high, "kern", across)
        near_high = lax.ppermute(high, "kern", near)
        across_low = lax.ppermute(low, "kern", across)
        last_low = lax.ppermute(near_low, "kern", across)
        last_high = lax.ppermute(across_high, "kern", near)
        return [halves, [near_low, near_high], [across_low, across_high], [last_low, last_high]]
    fields = [halves]
    for step in range(1, count):
        fields.append([lax.ppermute(half, "kern", step_pairs(count, step)) for half in halves])
    return fields


class Message:
    def __init__(self, count, reach, step=None, slot=None):
        self.count, self.reach, self.step, self.slot = count, reach, step, slot
        if slot is not None:
            offset = slot - reach if slot < reach else slot - reach + 1
            self.width = 1
            self.pairs = [(source, (source - offset) % count) for source in range(count)]
        else:
            self.pairs = step_pairs(count, step)
            self.width = 1
            for source, dest in self.pairs:
                ahead = (source - dest) % count
                if ahead <= reach and count - ahead <= reach:
                    self.width = 2

    def slots(self, me, sending):
        if self.slot is not None:
            return [(self.slot, True)]
        count, reach = self.count, self.reach
        dest, source = partner(me, self.step, count)
        column, row = (me, dest) if sending else (source, me)
        ahead = lax.rem(column - row + count, count)
        first = jnp.where(ahead <= reach, ahead + reach - 1, ahead - count + reach)
        if self.width == 1:
            return [(first, True)]
        both = jnp.logical_and(ahead <= reach, count - ahead <= reach)
        return [(first, True), (jnp.where(both, ahead - count + reach, first), both)]


def messages_of(count, slots):
    reach = slots // 2
    if reach < count <= 2 * reach:
        return [Message(count, reach, step=step) for step in range(count - 1, 0, -1)]
    return [Message(count, reach, slot=slot) for slot in range(slots)]


def chunks_of(messages, most=4):
    chunks, held = [[]], 0
    for at, message in enumerate(messages):
        if held and held + message.width > most:
            chunks.append([])
            held = 0
        chunks[-1].append(at)
        held += message.width
    return chunks


def chunk_coefficients(split_ref, base, chunk, messages, rank, both, outs):
    size = rank * sum(messages[at].width for at in chunk)
    got = fold(dot(split_ref[pl.ds(base, 2 * size)], both))
    got = got[:size] + got[size:]
    row = 0
    for at in chunk:
        for w in range(messages[at].width):
            outs[at][w] = got[row : row + rank]
            row += rank
    return base + 2 * size


def first_coeff_kernel(messages, fresh, cols_ref, right_ref, *refs):
    outs, refs = refs[: len(messages)], refs[len(messages) :]
    split_ref = refs[0]
    rank = right_ref.shape[1]
    me = lax.axis_index("tile")
    if fresh:
        both_ref, right, sems, cols = refs[1:]
        cols_copy = pltpu.make_async_copy(cols_ref, cols, sems.at[right.shape[0]])
        cols_copy.start()
    else:
        both_ref = cols_ref
        right, sems = refs[1:]
    copies = []
    for message in messages:
        for slot, _ in message.slots(me, True):
            at = len(copies)
            copies.append(pltpu.make_async_copy(right_ref.at[slot], right.at[at], sems.at[at]))
            copies[-1].start()
    if fresh:
        cols_copy.wait()
        both_ref[...] = side_by_side(cols[...])
    both = both_ref[...]
    base, block = 0, 0
    for chunk in chunks_of(messages):
        blocks = sum(messages[at].width for at in chunk)
        for b in range(blocks):
            copies[block].wait()
            hi, lo = split(right[block])
            split_ref[pl.ds(base + b * rank, rank)] = hi
            split_ref[pl.ds(base + (blocks + b) * rank, rank)] = lo
            block += 1
        base = chunk_coefficients(split_ref, base, chunk, messages, rank, both, outs)


def first_coefficients(cols, right_tile, messages, fresh):
    slots, rank, size = right_tile.shape
    blocks = sum(message.width for message in messages)
    width = cols.shape[1] if fresh else cols.shape[1] // 2
    outs = [struct(message.width, rank, width) for message in messages]
    outs.append(struct(2 * blocks * rank, size, dtype=bf16))
    scratch = [pltpu.VMEM((blocks, rank, size), f32), pltpu.SemaphoreType.DMA((blocks + 1,))]
    if fresh:
        outs.append(struct(size, 2 * width, dtype=bf16))
        scratch.append(pltpu.VMEM(cols.shape, f32))
    got = call(
        functools.partial(first_coeff_kernel, messages, fresh),
        outs,
        [in_vmem] * len(outs),
        [in_hbm if fresh else in_vmem, in_hbm],
        scratch,
        flops=8 * blocks * rank * size * width,
        moved=4 * blocks * rank * (2 * size + width),
    )(to_hbm(cols) if fresh else cols, to_hbm(right_tile))
    return got[: len(messages)], got[len(messages)], got[-1] if fresh else cols


def next_coeff_kernel(message_sets, halves, *refs):
    count = lax.axis_size("kern")
    fields = refs[: count * halves]
    weights_ref = refs[count * halves]
    splits = refs[count * halves + 1 : count * halves + 1 + len(message_sets)]
    outs, cols_ref = refs[count * halves + 1 + len(message_sets) : -1], refs[-1]
    me = lax.axis_index("kern")
    part = fields[0].shape[0]
    for half in range(halves):
        rows_of = pl.ds(half * part, part)
        total = None
        for step in range(count):
            source = partner(me, step, count)[1]
            term = fields[step * halves + half][...] * weights_ref[source, rows_of]
            total = term if total is None else total + term
        cols_ref[rows_of] = total
    both = side_by_side(cols_ref[...])
    rank = outs[0].shape[1]
    done = 0
    for messages, split_ref in zip(message_sets, splits):
        here = outs[done : done + len(messages)]
        done += len(messages)
        base = 0
        for chunk in chunks_of(messages):
            base = chunk_coefficients(split_ref, base, chunk, messages, rank, both, here)


def next_coefficients(fields, weights, splits, message_sets, rank):
    halves = len(fields[0])
    part, width = fields[0][0].shape
    size = part * halves
    outs = [struct(message.width, rank, width) for group in message_sets for message in group]
    outs.append(struct(size, width))
    total = sum(split_right.shape[0] for split_right in splits)
    flat = [half for field in fields for half in field]
    got = call(
        functools.partial(next_coeff_kernel, message_sets, halves),
        outs,
        [in_vmem] * len(outs),
        [in_vmem] * (len(flat) + 1 + len(splits)),
        flops=4 * total * size * width,
        moved=2 * total * (size + width),
    )(*flat, weights, *splits)
    return got[:-1], got[-1]


def times_diag(diag_ref, cols_ref):
    both = side_by_side(cols_ref[...])
    hi, lo = split(diag_ref[...])
    return fold(dot(hi, both) + dot(lo, both))


def diag_kernel(diag_ref, cols_ref, out_ref):
    out_ref[...] = times_diag(diag_ref, cols_ref)


def diagonal(diag_tile, cols):
    size, width = cols.shape
    return call(
        diag_kernel,
        struct(size, width),
        in_vmem,
        [in_vmem, in_vmem],
        flops=8 * size * size * width,
        moved=4 * size * (size + 2 * width),
    )(diag_tile, cols)


def prepare_kernel(
    halves, diag_hbm, cols_hbm, left_hbm, table_ref, index_ref,
    diag_out, left_out, weights_ref, diag_ref, cols_ref, left_ref, sems,
):
    copies = []
    for at, (source, target) in enumerate(
        ((diag_hbm, diag_ref), (cols_hbm, cols_ref), (left_hbm, left_ref))
    ):
        copies.append(pltpu.make_async_copy(source, target, sems.at[at]))
        copies[-1].start()
    own = table_ref[lax.axis_index("kern")]
    groups, entries = own.shape
    size = index_ref.shape[1]
    hot = (lax.broadcasted_iota(jnp.int32, (entries, size), 0) == index_ref[...]).astype(f32)
    weights = jnp.dot(own, hot, precision=lax.Precision.HIGHEST, preferred_element_type=f32)
    width = weights_ref.shape[2]
    for b in range(groups):
        weights_ref[b] = jnp.broadcast_to(weights[b : b + 1], (width, size)).T
    copies[0].wait()
    copies[1].wait()
    diag_out[...] = times_diag(diag_ref, cols_ref)
    copies[2].wait()
    total = left_ref.shape[0]
    step = 128 if total % 128 == 0 else total
    part = size // halves
    for at in range(0, total, step):
        span = slice(at, at + step)
        hi, lo = split(left_ref[span].T)
        for half in range(halves):
            base = 2 * half * part
            rows_of = slice(half * part, (half + 1) * part)
            left_out[base : base + part, span] = hi[rows_of]
            left_out[base + part : base + 2 * part, span] = lo[rows_of]


def prepare(diag_tile, cols, left_rows, table, index, halves):
    size, width = cols.shape
    total = left_rows.shape[0]
    groups = table.shape[0]
    return call(
        functools.partial(prepare_kernel, halves),
        [
            struct(size, width),
            struct(2 * size, total, dtype=bf16),
            struct(groups, size, width),
        ],
        [in_vmem] * 3,
        [in_hbm] * 3 + [in_vmem] * 2,
        [
            pltpu.VMEM(diag_tile.shape, f32),
            pltpu.VMEM(cols.shape, f32),
            pltpu.VMEM(left_rows.shape, f32),
            pltpu.SemaphoreType.DMA((3,)),
        ],
        flops=8 * size * size * width,
        moved=8 * total * size + 4 * size * (size + 2 * width),
    )(to_hbm(diag_tile), to_hbm(cols), to_hbm(left_rows), table, index)


def row_kernel(messages, halves, final, offs_ref, ranks_ref, *refs):
    gots = refs[: len(messages)]
    left_ref, diag_ref = refs[len(messages) : len(messages) + 2]
    outs = refs[len(messages) + 2 :]
    if final:
        outs, (picked, term_of, stage, sems) = outs[:-4], outs[-4:]
    else:
        outs, (picked, term_of) = outs[:-2], outs[-2:]
    terms = offs_ref.shape[1]
    rank, width = gots[0].shape[1:]
    slots = term_of.shape[0]
    reach = slots // 2
    for slot in range(slots):
        term_of[slot] = -1
    for k in range(terms):
        offset = offs_ref[0, k]
        term_of[jnp.where(offset < 0, offset + reach, offset + reach - 1)] = k
    me = lax.axis_index("tile")
    line = lax.broadcasted_iota(jnp.int32, (rank, width), 0)

    def pick(got, w, term):
        @pl.when(term >= 0)
        def _():
            kept = jnp.where(line < ranks_ref[0, term], got[w], 0.0)
            picked[pl.ds(pl.multiple_of(term * rank, rank), rank)] = kept

    for got, message in zip(gots, messages):
        for w, (slot, there) in enumerate(message.slots(me, False)):
            pick(got, w, jnp.where(there, term_of[slot], -1))
    both = side_by_side(picked[...])
    part = diag_ref.shape[0] // halves
    sent = []
    for half in range(halves):
        rows_of = pl.ds(half * part, part)
        got = fold(dot(left_ref[pl.ds(2 * half * part, 2 * part)], both))
        total = got[:part] + got[part:] + diag_ref[rows_of]
        if final:
            stage[rows_of] = total
            sent.append(
                pltpu.make_async_copy(stage.at[rows_of], outs[0].at[rows_of], sems.at[half])
            )
            sent[-1].start()
        else:
            outs[half][...] = total
    for copy in sent:
        copy.wait()


def rows(offsets, ranks, gots, messages, left_split, diag_part, slots, halves, final):
    size, width = diag_part.shape
    total = left_split.shape[1]
    scratch = [pltpu.VMEM((total, width), f32), pltpu.SMEM((slots,), jnp.int32)]
    if final:
        scratch += [pltpu.VMEM((size, width), f32), pltpu.SemaphoreType.DMA((halves,))]
    return call(
        functools.partial(row_kernel, messages, halves, final),
        pltpu.HBM((size, width), f32) if final else [struct(size // halves, width)] * halves,
        in_hbm if final else [in_vmem] * halves,
        [in_smem, in_smem] + [in_vmem] * (len(messages) + 2),
        scratch,
        flops=8 * total * size * width,
        moved=4 * total * (size + width),
    )(offsets, ranks, *gots, left_split, diag_part)


def deliver(coeffs, messages):
    return [lax.ppermute(sent, "tile", message.pairs) for sent, message in zip(coeffs, messages)]


def local(
    diag_tiles,
    left_factors,
    right_factors,
    tile_offsets,
    tile_ranks,
    mixing,
    block_index,
    rhs_field,
):
    diag_tile = diag_tiles[0, 0]
    right_tile = right_factors[0, 0]
    offsets = tile_offsets[0]
    ranks = tile_ranks[0]
    slots, rank, size = right_tile.shape
    halves = 2 if size % 32 == 0 else 1
    left_rows = left_factors.reshape(-1, size)
    table = mixing.transpose(1, 2, 0)
    index = block_index[None]
    cols = rhs_field[0]

    messages = messages_of(lax.axis_size("tile"), slots)
    far = (len(messages) + 1) // 2
    message_sets = [messages[:far], messages[far:]]
    gots, splits, given = [], [], cols
    for group in message_sets:
        coeffs, split_right, given = first_coefficients(given, right_tile, group, not splits)
        gots += deliver(coeffs, group)
        splits.append(split_right)
    diag_part, left_split, weights = prepare(diag_tile, cols, left_rows, table, index, halves)
    first = rows(offsets, ranks, gots, messages, left_split, diag_part, slots, halves, False)
    fields = gather_fields(first)
    coeffs, cols = next_coefficients(fields, weights, splits, message_sets, rank)
    gots = deliver(coeffs, messages)
    diag_part = diagonal(diag_tile, cols)
    return rows(offsets, ranks, gots, messages, left_split, diag_part, slots, halves, True)[None]


def solution(mesh):
    in_specs = (
        P("kern", "tile", None, None),
        P("kern", "tile", None, None, None),
        P("kern", "tile", None, None, None),
        P("kern", "tile", None),
        P("kern", "tile", None),
        P(),
        P("tile"),
        P("kern", "tile", None),
    )
    out_specs = P("kern", "tile", None)
    return jax.shard_map(local, mesh=mesh, in_specs=in_specs, out_specs=out_specs, check_vma=False)
```

```python
import functools

import jax
import jax.numpy as jnp
from jax import lax
from jax.experimental import pallas as pl
from jax.experimental.pallas import tpu as pltpu
from jax.sharding import PartitionSpec as P

f32 = jnp.float32
bf16 = jnp.bfloat16
VMEM_BYTES = 24 * 1024 * 1024
in_vmem = pl.BlockSpec(memory_space=pltpu.VMEM)
in_smem = pl.BlockSpec(memory_space=pltpu.SMEM)
in_hbm = pl.BlockSpec(memory_space=pltpu.HBM)


def to_hbm(value):
    return pltpu.with_memory_space_constraint(value, pltpu.HBM)


def struct(*shape, dtype=f32):
    return jax.ShapeDtypeStruct(shape, dtype)


def split(value):
    hi = value.astype(bf16)
    return hi, (value - hi.astype(f32)).astype(bf16)


def side_by_side(value):
    return jnp.concatenate(split(value), axis=1)


def dot(left, right):
    return jnp.dot(left, right, preferred_element_type=f32)


def fold(value):
    width = value.shape[1] // 2
    return value[:, :width] + value[:, width:]


def call(kernel, outs, out_specs, in_specs, scratch=(), flops=0, moved=0):
    return pl.pallas_call(
        kernel,
        out_shape=outs,
        in_specs=in_specs,
        out_specs=out_specs,
        scratch_shapes=list(scratch),
        compiler_params=pltpu.CompilerParams(vmem_limit_bytes=VMEM_BYTES),
        cost_estimate=pl.CostEstimate(flops=flops, bytes_accessed=moved, transcendentals=0),
    )


def step_pairs(count, step):
    if count & (count - 1) == 0:
        return [(source, source ^ step) for source in range(count)]
    return [(source, (source + step) % count) for source in range(count)]


def partner(me, step, count):
    if count & (count - 1) == 0:
        return me ^ step, me ^ step
    return lax.rem(me + step, count), lax.rem(me + count - step, count)


def exchange(values, axis):
    count = lax.axis_size(axis)
    arrived = [values[0]] * count
    for step in range(count - 1, 0, -1):
        arrived[step] = lax.ppermute(values[step], axis, step_pairs(count, step))
    return arrived


class Message:
    def __init__(self, count, reach, pairs, step=None, places=(0,), slot=None):
        self.count, self.reach, self.pairs = count, reach, pairs
        self.step, self.places, self.slot = step, places, slot
        self.width = len(places)

    def slots(self, me, sending):
        if self.slot is not None:
            return [(self.slot, True)]
        count, reach = self.count, self.reach
        dest, source = partner(me, self.step, count)
        column, row = (me, dest) if sending else (source, me)
        ahead = lax.rem(column - row + count, count)
        first = jnp.where(ahead <= reach, ahead + reach - 1, ahead - count + reach)
        both = jnp.logical_and(ahead <= reach, count - ahead <= reach)
        second = jnp.where(both, ahead - count + reach, first)
        return [((first, True), (second, both))[place] for place in self.places]


def step_messages(count, reach, step):
    pairs = step_pairs(count, step)
    doubles = []
    for source, dest in pairs:
        ahead = (source - dest) % count
        if ahead <= reach and count - ahead <= reach:
            doubles.append((source, dest))
    if not doubles:
        return [Message(count, reach, pairs, step)]
    if len(doubles) < len(pairs) and step >= count // 2:
        return [Message(count, reach, pairs, step), Message(count, reach, doubles, step, (1,))]
    return [Message(count, reach, pairs, step, (0, 1))]


def message_sets_of(count, slots):
    reach = slots // 2
    if reach < count <= 2 * reach:
        sets = [[], []]
        for step in range(count - 1, 0, -1):
            sets[step < count // 2] += step_messages(count, reach, step)
        return sets
    messages = []
    for slot in range(slots):
        offset = slot - reach if slot < reach else slot - reach + 1
        pairs = [(source, (source - offset) % count) for source in range(count)]
        messages.append(Message(count, reach, pairs, slot=slot))
    return [messages]


def chunks_of(messages, most=4):
    chunks, held = [[]], 0
    for at, message in enumerate(messages):
        if held and held + message.width > most:
            chunks.append([])
            held = 0
        chunks[-1].append(at)
        held += message.width
    return chunks


def chunk_coefficients(split_ref, base, chunk, messages, rank, both, outs):
    size = rank * sum(messages[at].width for at in chunk)
    got = fold(dot(split_ref[pl.ds(base, 2 * size)], both))
    got = got[:size] + got[size:]
    row = 0
    for at in chunk:
        for w in range(messages[at].width):
            outs[at][w] = got[row : row + rank]
            row += rank
    return base + 2 * size


def first_coeff_kernel(messages, fresh, cols_ref, right_ref, *refs):
    outs, refs = refs[: len(messages)], refs[len(messages) :]
    split_ref = refs[0]
    rank = right_ref.shape[1]
    me = lax.axis_index("tile")
    if fresh:
        both_ref, right, sems, cols = refs[1:]
        cols_copy = pltpu.make_async_copy(cols_ref, cols, sems.at[right.shape[0]])
        cols_copy.start()
    else:
        both_ref = cols_ref
        right, sems = refs[1:]
    copies = []
    for message in messages:
        for slot, _ in message.slots(me, True):
            at = len(copies)
            copies.append(pltpu.make_async_copy(right_ref.at[slot], right.at[at], sems.at[at]))
            copies[-1].start()
    if fresh:
        cols_copy.wait()
        both_ref[...] = side_by_side(cols[...])
    both = both_ref[...]
    base, block = 0, 0
    for chunk in chunks_of(messages):
        blocks = sum(messages[at].width for at in chunk)
        for b in range(blocks):
            copies[block].wait()
            hi, lo = split(right[block])
            split_ref[pl.ds(base + b * rank, rank)] = hi
            split_ref[pl.ds(base + (blocks + b) * rank, rank)] = lo
            block += 1
        base = chunk_coefficients(split_ref, base, chunk, messages, rank, both, outs)


def first_coefficients(cols, right_tile, messages, fresh):
    slots, rank, size = right_tile.shape
    blocks = sum(message.width for message in messages)
    width = cols.shape[1] if fresh else cols.shape[1] // 2
    outs = [struct(message.width, rank, width) for message in messages]
    outs.append(struct(2 * blocks * rank, size, dtype=bf16))
    scratch = [pltpu.VMEM((blocks, rank, size), f32), pltpu.SemaphoreType.DMA((blocks + 1,))]
    if fresh:
        outs.append(struct(size, 2 * width, dtype=bf16))
        scratch.append(pltpu.VMEM(cols.shape, f32))
    got = call(
        functools.partial(first_coeff_kernel, messages, fresh),
        outs,
        [in_vmem] * len(outs),
        [in_hbm if fresh else in_vmem, in_hbm],
        scratch,
        flops=8 * blocks * rank * size * width,
        moved=4 * blocks * rank * (2 * size + width),
    )(to_hbm(cols) if fresh else cols, to_hbm(right_tile))
    return got[: len(messages)], got[len(messages)], got[-1] if fresh else cols


def next_coeff_kernel(message_sets, groups, *refs):
    parts, refs = refs[:groups], refs[groups:]
    splits, outs, cols_ref = refs[: len(message_sets)], refs[len(message_sets) : -1], refs[-1]
    part = parts[0].shape[0]
    me = lax.axis_index("kern")
    for at in range(groups):
        source = partner(me, at, groups)[1]
        cols_ref[pl.ds(pl.multiple_of(source * part, part), part)] = parts[at][...]
    both = side_by_side(cols_ref[...])
    rank = outs[0].shape[1]
    done = 0
    for messages, split_ref in zip(message_sets, splits):
        here = outs[done : done + len(messages)]
        done += len(messages)
        base = 0
        for chunk in chunks_of(messages):
            base = chunk_coefficients(split_ref, base, chunk, messages, rank, both, here)


def next_coefficients(parts, splits, message_sets, rank):
    groups = len(parts)
    part, width = parts[0].shape
    size = part * groups
    outs = [struct(message.width, rank, width) for group in message_sets for message in group]
    outs.append(struct(size, width))
    total = sum(split_right.shape[0] for split_right in splits)
    got = call(
        functools.partial(next_coeff_kernel, message_sets, groups),
        outs,
        [in_vmem] * len(outs),
        [in_vmem] * (groups + len(splits)),
        flops=4 * total * size * width,
        moved=2 * total * (size + width),
    )(*parts, *splits)
    return got[:-1], got[-1]


def times_diag(diag_ref, cols_ref):
    both = side_by_side(cols_ref[...])
    hi, lo = split(diag_ref[...])
    return fold(dot(hi, both) + dot(lo, both))


def diag_kernel(diag_ref, cols_ref, out_ref):
    out_ref[...] = times_diag(diag_ref, cols_ref)


def diagonal(diag_tile, cols):
    size, width = cols.shape
    return call(
        diag_kernel,
        struct(size, width),
        in_vmem,
        [in_vmem, in_vmem],
        flops=8 * size * size * width,
        moved=4 * size * (size + 2 * width),
    )(diag_tile, cols)


def prepare_kernel(
    halves, diag_hbm, cols_hbm, left_hbm, table_ref, index_ref,
    diag_out, left_out, weights_ref, diag_ref, cols_ref, left_ref, sems,
):
    copies = []
    for at, (source, target) in enumerate(
        ((diag_hbm, diag_ref), (cols_hbm, cols_ref), (left_hbm, left_ref))
    ):
        copies.append(pltpu.make_async_copy(source, target, sems.at[at]))
        copies[-1].start()
    entries = table_ref.shape[1]
    part = index_ref.shape[1]
    index = index_ref[pl.ds(lax.axis_index("kern"), 1)]
    hot = (lax.broadcasted_iota(jnp.int32, (entries, part), 0) == index).astype(f32)
    weights = jnp.dot(
        table_ref[...], hot, precision=lax.Precision.HIGHEST, preferred_element_type=f32
    )
    width = weights_ref.shape[2]
    for at in range(weights_ref.shape[0]):
        weights_ref[at] = jnp.broadcast_to(weights[at : at + 1], (width, part)).T
    copies[0].wait()
    copies[1].wait()
    diag_out[...] = times_diag(diag_ref, cols_ref)
    copies[2].wait()
    total, size = left_ref.shape
    step = 128 if total % 128 == 0 else total
    part = size // halves
    for at in range(0, total, step):
        span = slice(at, at + step)
        hi, lo = split(left_ref[span].T)
        for half in range(halves):
            base = 2 * half * part
            rows_of = slice(half * part, (half + 1) * part)
            left_out[base : base + part, span] = hi[rows_of]
            left_out[base + part : base + 2 * part, span] = lo[rows_of]


def prepare(diag_tile, cols, left_rows, table, index, halves):
    size, width = cols.shape
    total = left_rows.shape[0]
    part = index.shape[1]
    return call(
        functools.partial(prepare_kernel, halves),
        [
            struct(size, width),
            struct(2 * size, total, dtype=bf16),
            struct(table.shape[0], part, width),
        ],
        [in_vmem] * 3,
        [in_hbm] * 3 + [in_vmem] * 2,
        [
            pltpu.VMEM(diag_tile.shape, f32),
            pltpu.VMEM(cols.shape, f32),
            pltpu.VMEM(left_rows.shape, f32),
            pltpu.SemaphoreType.DMA((3,)),
        ],
        flops=8 * size * size * width,
        moved=8 * total * size + 4 * size * (size + 2 * width),
    )(to_hbm(diag_tile), to_hbm(cols), to_hbm(left_rows), table, index)


def row_kernel(messages, halves, groups, offs_ref, ranks_ref, *refs):
    gots = refs[: len(messages)]
    left_ref, diag_ref = refs[len(messages) : len(messages) + 2]
    refs = refs[len(messages) + 2 :]
    outs, (picked, term_of, stage, sems) = refs[:groups], refs[groups:]
    terms = offs_ref.shape[1]
    rank, width = gots[0].shape[1:]
    slots = term_of.shape[0]
    reach = slots // 2
    for slot in range(slots):
        term_of[slot] = -1
    for k in range(terms):
        offset = offs_ref[0, k]
        term_of[jnp.where(offset < 0, offset + reach, offset + reach - 1)] = k
    me = lax.axis_index("tile")
    line = lax.broadcasted_iota(jnp.int32, (rank, width), 0)

    def pick(got, w, term):
        @pl.when(term >= 0)
        def _():
            kept = jnp.where(line < ranks_ref[0, term], got[w], 0.0)
            picked[pl.ds(pl.multiple_of(term * rank, rank), rank)] = kept

    for got, message in zip(gots, messages):
        for w, (slot, there) in enumerate(message.slots(me, False)):
            pick(got, w, jnp.where(there, term_of[slot], -1))
    both = side_by_side(picked[...])
    part = diag_ref.shape[0] // halves
    sent = []
    for half in range(halves):
        rows_of = pl.ds(half * part, part)
        got = fold(dot(left_ref[pl.ds(2 * half * part, 2 * part)], both))
        total = got[:part] + got[part:] + diag_ref[rows_of]
        stage[rows_of] = total
        if groups == 1:
            sent.append(
                pltpu.make_async_copy(stage.at[rows_of], outs[0].at[rows_of], sems.at[half])
            )
            sent[-1].start()
    for copy in sent:
        copy.wait()
    if groups > 1:
        part = stage.shape[0] // groups
        own = lax.axis_index("kern")
        for at in range(groups):
            dest = partner(own, at, groups)[0]
            outs[at][...] = stage[pl.ds(pl.multiple_of(dest * part, part), part)]


def mix_kernel(groups, *refs):
    fields, weights_ref, outs = refs[:groups], refs[groups], refs[groups + 1 :]
    me = lax.axis_index("kern")
    for at in range(groups):
        base = partner(me, at, groups)[0] * groups
        total = None
        for b in range(groups):
            term = fields[b][...] * weights_ref[base + partner(me, b, groups)[1]]
            total = term if total is None else total + term
        outs[at][...] = total


def mix(fields, weights):
    groups = len(fields)
    part, width = fields[0].shape
    return call(
        functools.partial(mix_kernel, groups),
        [struct(part, width)] * groups,
        [in_vmem] * groups,
        [in_vmem] * (groups + 1),
        flops=2 * groups * groups * part * width,
        moved=8 * groups * part * width,
    )(*fields, weights)


def rows(offsets, ranks, gots, messages, left_split, diag_part, slots, halves, groups):
    size, width = diag_part.shape
    total = left_split.shape[1]
    last = groups == 1
    return call(
        functools.partial(row_kernel, messages, halves, groups),
        pltpu.HBM((size, width), f32) if last else [struct(size // groups, width)] * groups,
        in_hbm if last else [in_vmem] * groups,
        [in_smem, in_smem] + [in_vmem] * (len(messages) + 2),
        [
            pltpu.VMEM((total, width), f32),
            pltpu.SMEM((slots,), jnp.int32),
            pltpu.VMEM((size, width), f32),
            pltpu.SemaphoreType.DMA((halves,)),
        ],
        flops=8 * total * size * width,
        moved=4 * total * (size + width),
    )(offsets, ranks, *gots, left_split, diag_part)


def deliver(coeffs, messages):
    return [lax.ppermute(sent, "tile", message.pairs) for sent, message in zip(coeffs, messages)]


def local(
    diag_tiles,
    left_factors,
    right_factors,
    tile_offsets,
    tile_ranks,
    mixing,
    block_index,
    rhs_field,
):
    diag_tile = diag_tiles[0, 0]
    right_tile = right_factors[0, 0]
    offsets = tile_offsets[0]
    ranks = tile_ranks[0]
    slots, rank, size = right_tile.shape
    halves = 2 if size % 32 == 0 else 1
    left_rows = left_factors.reshape(-1, size)
    groups = lax.axis_size("kern")
    table = mixing.reshape(mixing.shape[0], groups * groups).T
    index = block_index.reshape(groups, size // groups)
    cols = rhs_field[0]

    message_sets = message_sets_of(lax.axis_size("tile"), slots)
    messages = [message for group in message_sets for message in group]
    gots, splits, given = [], [], cols
    for group in message_sets:
        coeffs, split_right, given = first_coefficients(given, right_tile, group, not splits)
        gots += deliver(coeffs, group)
        splits.append(split_right)
    diag_part, left_split, weights = prepare(diag_tile, cols, left_rows, table, index, halves)
    first = rows(offsets, ranks, gots, messages, left_split, diag_part, slots, halves, groups)
    mixed = exchange(mix(exchange(first, "kern"), weights), "kern")
    coeffs, cols = next_coefficients(mixed, splits, message_sets, rank)
    gots = deliver(coeffs, messages)
    diag_part = diagonal(diag_tile, cols)
    return rows(offsets, ranks, gots, messages, left_split, diag_part, slots, halves, 1)[None]


def solution(mesh):
    in_specs = (
        P("kern", "tile", None, None),
        P("kern", "tile", None, None, None),
        P("kern", "tile", None, None, None),
        P("kern", "tile", None),
        P("kern", "tile", None),
        P(),
        P("tile"),
        P("kern", "tile", None),
    )
    out_specs = P("kern", "tile", None)
    return jax.shard_map(local, mesh=mesh, in_specs=in_specs, out_specs=out_specs, check_vma=False)
```

```python
import functools
import math

import jax
import jax.numpy as jnp
from jax import lax
from jax.experimental import pallas as pl
from jax.experimental.pallas import tpu as pltpu
from jax.sharding import PartitionSpec as P

f32 = jnp.float32
bf16 = jnp.bfloat16
VMEM_BYTES = 24 * 1024 * 1024
in_vmem = pl.BlockSpec(memory_space=pltpu.VMEM)
in_smem = pl.BlockSpec(memory_space=pltpu.SMEM)
in_hbm = pl.BlockSpec(memory_space=pltpu.HBM)


def to_hbm(value):
    return pltpu.with_memory_space_constraint(value, pltpu.HBM)


def struct(*shape, dtype=f32):
    return jax.ShapeDtypeStruct(shape, dtype)


def split(value):
    hi = value.astype(bf16)
    return hi, (value - hi.astype(f32)).astype(bf16)


def side_by_side(value):
    return jnp.concatenate(split(value), axis=1)


def dot(left, right):
    return jnp.dot(left, right, preferred_element_type=f32)


def fold(value):
    width = value.shape[1] // 2
    return value[:, :width] + value[:, width:]


def call(kernel, outs, out_specs, in_specs, scratch=(), flops=0, moved=0):
    return pl.pallas_call(
        kernel,
        out_shape=outs,
        in_specs=in_specs,
        out_specs=out_specs,
        scratch_shapes=list(scratch),
        compiler_params=pltpu.CompilerParams(vmem_limit_bytes=VMEM_BYTES),
        cost_estimate=pl.CostEstimate(flops=flops, bytes_accessed=moved, transcendentals=0),
    )


def kern_step(tile, step, groups):
    if groups != 4 or step not in (1, 2):
        return step
    return step + (tile & 1) * (3 - 2 * step)


def partner(me, step, count):
    if count & (count - 1) == 0:
        return me ^ step, me ^ step
    return (me + step) % count, (me + count - step) % count


def kern_partner(step, groups):
    return partner(
        lax.axis_index("kern"), kern_step(lax.axis_index("tile"), step, groups), groups
    )


def exchange(values):
    groups, count = lax.axis_size("kern"), lax.axis_size("tile")
    arrived = [values[0]]
    for step in range(1, groups):
        pairs = []
        for group in range(groups):
            for tile in range(count):
                dest = partner(group, kern_step(tile, step, groups), groups)[0]
                pairs.append((group * count + tile, dest * count + tile))
        arrived.append(lax.ppermute(values[step], ("kern", "tile"), pairs))
    return arrived


class Message:
    def __init__(self, count, reach, ahead=None, turn=0, slot=None):
        self.count, self.reach, self.slot = count, reach, slot
        self.ahead, self.turn = ahead, turn
        self.width = 1
        if slot is None and ahead <= reach and count - ahead <= reach:
            self.width = 2
        offset = ahead if slot is None else offset_of(slot, reach)
        self.pairs = [(source, (source - offset) % count) for source in range(count)]
        if slot is None and turn is not None:
            self.pairs = [(source, self.mate(source)) for source in range(count)]

    def mate(self, me):
        upward = 1 - 2 * ((me // math.gcd(self.ahead, self.count) + self.turn) % 2)
        return (me + upward * self.ahead + self.count) % self.count

    def across(self):
        half = self.count // 2
        return self.width * sum((a < half) != (b < half) for a, b in self.pairs)

    def slots(self, me, sending):
        if self.slot is not None:
            return [self.slot]
        count, reach = self.count, self.reach
        if self.turn is None:
            ahead = self.ahead
        else:
            mate = self.mate(me)
            ahead = lax.rem((me - mate if sending else mate - me) + count, count)
        below = ahead - count + reach
        if self.width == 1:
            return [jnp.where(ahead <= reach, ahead + reach - 1, below)]
        return [ahead + reach - 1, below]


def offset_of(slot, reach):
    return slot - reach if slot < reach else slot - reach + 1


def message_sets_of(count, slots):
    reach = slots // 2
    if not reach < count <= 2 * reach:
        return [[Message(count, reach, slot=slot) for slot in range(slots)]]
    messages = []
    if count & (count - 1) == 0:
        for ahead in range(1, count // 2 + 1):
            for turn in range(1 if 2 * ahead == count else 2):
                messages.append(Message(count, reach, ahead, turn))
    else:
        messages = [Message(count, reach, ahead, None) for ahead in range(1, count)]
    messages.sort(key=lambda message: -message.across())
    return [messages[: count // 2 - 1], messages[count // 2 - 1 :]]


def chunks_of(messages, most=4):
    chunks, held = [[]], 0
    for at, message in enumerate(messages):
        if held and held + message.width > most:
            chunks.append([])
            held = 0
        chunks[-1].append(at)
        held += message.width
    return chunks


def chunk_coefficients(split_ref, base, chunk, messages, rank, both, outs):
    size = rank * sum(messages[at].width for at in chunk)
    got = fold(dot(split_ref[pl.ds(base, 2 * size)], both))
    got = got[:size] + got[size:]
    row = 0
    for at in chunk:
        for w in range(messages[at].width):
            outs[at][w] = got[row : row + rank]
            row += rank
    return base + 2 * size


def first_coeff_kernel(messages, fresh, cols_ref, right_ref, *refs):
    outs, refs = refs[: len(messages)], refs[len(messages) :]
    split_ref = refs[0]
    rank = right_ref.shape[1]
    me = lax.axis_index("tile")
    if fresh:
        both_ref, right, sems, cols = refs[1:]
        cols_copy = pltpu.make_async_copy(cols_ref, cols, sems.at[right.shape[0]])
        cols_copy.start()
    else:
        both_ref = cols_ref
        right, sems = refs[1:]
    copies = []
    for message in messages:
        for slot in message.slots(me, True):
            at = len(copies)
            copies.append(pltpu.make_async_copy(right_ref.at[slot], right.at[at], sems.at[at]))
            copies[-1].start()
    if fresh:
        cols_copy.wait()
        both_ref[...] = side_by_side(cols[...])
    both = both_ref[...]
    base, block = 0, 0
    for chunk in chunks_of(messages):
        blocks = sum(messages[at].width for at in chunk)
        for b in range(blocks):
            copies[block].wait()
            hi, lo = split(right[block])
            split_ref[pl.ds(base + b * rank, rank)] = hi
            split_ref[pl.ds(base + (blocks + b) * rank, rank)] = lo
            block += 1
        base = chunk_coefficients(split_ref, base, chunk, messages, rank, both, outs)


def first_coefficients(cols, right_tile, messages, fresh):
    slots, rank, size = right_tile.shape
    blocks = sum(message.width for message in messages)
    width = cols.shape[1] if fresh else cols.shape[1] // 2
    outs = [struct(message.width, rank, width) for message in messages]
    outs.append(struct(2 * blocks * rank, size, dtype=bf16))
    scratch = [pltpu.VMEM((blocks, rank, size), f32), pltpu.SemaphoreType.DMA((blocks + 1,))]
    if fresh:
        outs.append(struct(size, 2 * width, dtype=bf16))
        scratch.append(pltpu.VMEM(cols.shape, f32))
    got = call(
        functools.partial(first_coeff_kernel, messages, fresh),
        outs,
        [in_vmem] * len(outs),
        [in_hbm if fresh else in_vmem, in_hbm],
        scratch,
        flops=8 * blocks * rank * size * width,
        moved=4 * blocks * rank * (2 * size + width),
    )(to_hbm(cols) if fresh else cols, to_hbm(right_tile))
    return got[: len(messages)], got[len(messages)], got[-1] if fresh else cols


def next_coeff_kernel(message_sets, groups, *refs):
    parts, refs = refs[:groups], refs[groups:]
    splits, outs, cols_ref = refs[: len(message_sets)], refs[len(message_sets) : -1], refs[-1]
    part = parts[0].shape[0]
    for at in range(groups):
        source = kern_partner(at, groups)[1]
        cols_ref[pl.ds(pl.multiple_of(source * part, part), part)] = parts[at][...]
    both = side_by_side(cols_ref[...])
    rank = outs[0].shape[1]
    done = 0
    for messages, split_ref in zip(message_sets, splits):
        here = outs[done : done + len(messages)]
        done += len(messages)
        base = 0
        for chunk in chunks_of(messages):
            base = chunk_coefficients(split_ref, base, chunk, messages, rank, both, here)


def next_coefficients(parts, splits, message_sets, rank):
    groups = len(parts)
    part, width = parts[0].shape
    size = part * groups
    outs = [struct(message.width, rank, width) for group in message_sets for message in group]
    outs.append(struct(size, width))
    total = sum(split_right.shape[0] for split_right in splits)
    got = call(
        functools.partial(next_coeff_kernel, message_sets, groups),
        outs,
        [in_vmem] * len(outs),
        [in_vmem] * (groups + len(splits)),
        flops=4 * total * size * width,
        moved=2 * total * (size + width),
    )(*parts, *splits)
    return got[:-1], got[-1]


def times_diag(diag_ref, cols_ref):
    both = side_by_side(cols_ref[...])
    hi, lo = split(diag_ref[...])
    return fold(dot(hi, both) + dot(lo, both))


def diag_kernel(diag_ref, cols_ref, out_ref):
    out_ref[...] = times_diag(diag_ref, cols_ref)


def diagonal(diag_tile, cols):
    size, width = cols.shape
    return call(
        diag_kernel,
        struct(size, width),
        in_vmem,
        [in_vmem, in_vmem],
        flops=8 * size * size * width,
        moved=4 * size * (size + 2 * width),
    )(diag_tile, cols)


def prepare_kernel(
    halves, diag_hbm, cols_hbm, left_hbm, table_ref, index_ref,
    diag_out, left_out, weights_ref, diag_ref, cols_ref, left_ref, sems,
):
    copies = []
    for at, (source, target) in enumerate(
        ((diag_hbm, diag_ref), (cols_hbm, cols_ref), (left_hbm, left_ref))
    ):
        copies.append(pltpu.make_async_copy(source, target, sems.at[at]))
        copies[-1].start()
    entries = table_ref.shape[1]
    part = index_ref.shape[1]
    index = index_ref[pl.ds(lax.axis_index("kern"), 1)]
    hot = (lax.broadcasted_iota(jnp.int32, (entries, part), 0) == index).astype(f32)
    weights = jnp.dot(
        table_ref[...], hot, precision=lax.Precision.HIGHEST, preferred_element_type=f32
    )
    width = weights_ref.shape[2]
    for at in range(weights_ref.shape[0]):
        weights_ref[at] = jnp.broadcast_to(weights[at : at + 1], (width, part)).T
    copies[0].wait()
    copies[1].wait()
    diag_out[...] = times_diag(diag_ref, cols_ref)
    copies[2].wait()
    total, size = left_ref.shape
    step = 128 if total % 128 == 0 else total
    part = size // halves
    for at in range(0, total, step):
        span = slice(at, at + step)
        hi, lo = split(left_ref[span].T)
        for half in range(halves):
            base = 2 * half * part
            rows_of = slice(half * part, (half + 1) * part)
            left_out[base : base + part, span] = hi[rows_of]
            left_out[base + part : base + 2 * part, span] = lo[rows_of]


def prepare(diag_tile, cols, left_rows, table, index, halves):
    size, width = cols.shape
    total = left_rows.shape[0]
    part = index.shape[1]
    return call(
        functools.partial(prepare_kernel, halves),
        [
            struct(size, width),
            struct(2 * size, total, dtype=bf16),
            struct(table.shape[0], part, width),
        ],
        [in_vmem] * 3,
        [in_hbm] * 3 + [in_vmem] * 2,
        [
            pltpu.VMEM(diag_tile.shape, f32),
            pltpu.VMEM(cols.shape, f32),
            pltpu.VMEM(left_rows.shape, f32),
            pltpu.SemaphoreType.DMA((3,)),
        ],
        flops=8 * size * size * width,
        moved=8 * total * size + 4 * size * (size + 2 * width),
    )(to_hbm(diag_tile), to_hbm(cols), to_hbm(left_rows), table, index)


def row_kernel(messages, halves, groups, offs_ref, ranks_ref, *refs):
    gots = refs[: len(messages)]
    left_ref, diag_ref = refs[len(messages) : len(messages) + 2]
    refs = refs[len(messages) + 2 :]
    outs, (picked, term_of, stage, sems) = refs[:groups], refs[groups:]
    terms = offs_ref.shape[1]
    rank, width = gots[0].shape[1:]
    slots = term_of.shape[0]
    reach = slots // 2
    for slot in range(slots):
        term_of[slot] = -1
    for k in range(terms):
        offset = offs_ref[0, k]
        term_of[jnp.where(offset < 0, offset + reach, offset + reach - 1)] = k
    me = lax.axis_index("tile")
    line = lax.broadcasted_iota(jnp.int32, (rank, width), 0)

    def pick(got, w, term):
        @pl.when(term >= 0)
        def _():
            kept = jnp.where(line < ranks_ref[0, term], got[w], 0.0)
            picked[pl.ds(pl.multiple_of(term * rank, rank), rank)] = kept

    for got, message in zip(gots, messages):
        for w, slot in enumerate(message.slots(me, False)):
            pick(got, w, term_of[slot])
    both = side_by_side(picked[...])
    part = diag_ref.shape[0] // halves
    sent = []
    for half in range(halves):
        rows_of = pl.ds(half * part, part)
        got = fold(dot(left_ref[pl.ds(2 * half * part, 2 * part)], both))
        total = got[:part] + got[part:] + diag_ref[rows_of]
        stage[rows_of] = total
        if groups == 1:
            sent.append(
                pltpu.make_async_copy(stage.at[rows_of], outs[0].at[rows_of], sems.at[half])
            )
            sent[-1].start()
    for copy in sent:
        copy.wait()
    if groups > 1:
        part = stage.shape[0] // groups
        for at in range(groups):
            dest = kern_partner(at, groups)[0]
            outs[at][...] = stage[pl.ds(pl.multiple_of(dest * part, part), part)]


def mix_kernel(groups, *refs):
    fields, weights_ref, outs = refs[:groups], refs[groups], refs[groups + 1 :]
    for at in range(groups):
        base = kern_partner(at, groups)[0] * groups
        total = None
        for b in range(groups):
            term = fields[b][...] * weights_ref[base + kern_partner(b, groups)[1]]
            total = term if total is None else total + term
        outs[at][...] = total


def mix(fields, weights):
    groups = len(fields)
    part, width = fields[0].shape
    return call(
        functools.partial(mix_kernel, groups),
        [struct(part, width)] * groups,
        [in_vmem] * groups,
        [in_vmem] * (groups + 1),
        flops=2 * groups * groups * part * width,
        moved=8 * groups * part * width,
    )(*fields, weights)


def rows(offsets, ranks, gots, messages, left_split, diag_part, slots, halves, groups):
    size, width = diag_part.shape
    total = left_split.shape[1]
    last = groups == 1
    return call(
        functools.partial(row_kernel, messages, halves, groups),
        pltpu.HBM((size, width), f32) if last else [struct(size // groups, width)] * groups,
        in_hbm if last else [in_vmem] * groups,
        [in_smem, in_smem] + [in_vmem] * (len(messages) + 2),
        [
            pltpu.VMEM((total, width), f32),
            pltpu.SMEM((slots,), jnp.int32),
            pltpu.VMEM((size, width), f32),
            pltpu.SemaphoreType.DMA((halves,)),
        ],
        flops=8 * total * size * width,
        moved=4 * total * (size + width),
    )(offsets, ranks, *gots, left_split, diag_part)


def deliver(coeffs, messages):
    return [lax.ppermute(sent, "tile", message.pairs) for sent, message in zip(coeffs, messages)]


def local(
    diag_tiles,
    left_factors,
    right_factors,
    tile_offsets,
    tile_ranks,
    mixing,
    block_index,
    rhs_field,
):
    diag_tile = diag_tiles[0, 0]
    right_tile = right_factors[0, 0]
    offsets = tile_offsets[0]
    ranks = tile_ranks[0]
    slots, rank, size = right_tile.shape
    halves = 2 if size % 32 == 0 else 1
    left_rows = left_factors.reshape(-1, size)
    groups = lax.axis_size("kern")
    table = mixing.reshape(mixing.shape[0], groups * groups).T
    index = block_index.reshape(groups, size // groups)
    cols = rhs_field[0]

    message_sets = message_sets_of(lax.axis_size("tile"), slots)
    messages = [message for group in message_sets for message in group]
    gots, splits, given = [], [], cols
    for group in message_sets:
        coeffs, split_right, given = first_coefficients(given, right_tile, group, not splits)
        gots += deliver(coeffs, group)
        splits.append(split_right)
    diag_part, left_split, weights = prepare(diag_tile, cols, left_rows, table, index, halves)
    first = rows(offsets, ranks, gots, messages, left_split, diag_part, slots, halves, groups)
    mixed = exchange(mix(exchange(first), weights))
    coeffs, cols = next_coefficients(mixed, splits, message_sets, rank)
    gots = deliver(coeffs, messages)
    diag_part = diagonal(diag_tile, cols)
    return rows(offsets, ranks, gots, messages, left_split, diag_part, slots, halves, 1)[None]


def solution(mesh):
    in_specs = (
        P("kern", "tile", None, None),
        P("kern", "tile", None, None, None),
        P("kern", "tile", None, None, None),
        P("kern", "tile", None),
        P("kern", "tile", None),
        P(),
        P("tile"),
        P("kern", "tile", None),
    )
    out_specs = P("kern", "tile", None)
    return jax.shard_map(local, mesh=mesh, in_specs=in_specs, out_specs=out_specs, check_vma=False)
```

```python
import functools
import math

import jax
import jax.numpy as jnp
from jax import lax
from jax.experimental import pallas as pl
from jax.experimental.pallas import tpu as pltpu
from jax.sharding import PartitionSpec as P

f32 = jnp.float32
bf16 = jnp.bfloat16
VMEM_BYTES = 24 * 1024 * 1024
in_vmem = pl.BlockSpec(memory_space=pltpu.VMEM)
in_smem = pl.BlockSpec(memory_space=pltpu.SMEM)
in_hbm = pl.BlockSpec(memory_space=pltpu.HBM)
in_any = pl.BlockSpec(memory_space=pl.ANY)


def to_hbm(value):
    return pltpu.with_memory_space_constraint(value, pltpu.HBM)


def struct(*shape, dtype=f32):
    return jax.ShapeDtypeStruct(shape, dtype)


def split(value):
    hi = value.astype(bf16)
    return hi, (value - hi.astype(f32)).astype(bf16)


def side_by_side(value):
    return jnp.concatenate(split(value), axis=1)


def dot(left, right):
    return jnp.dot(left, right, preferred_element_type=f32)


def fold(value):
    width = value.shape[1] // 2
    return value[:, :width] + value[:, width:]


def call(kernel, outs, out_specs, in_specs, scratch=(), flops=0, moved=0):
    return pl.pallas_call(
        kernel,
        out_shape=outs,
        in_specs=in_specs,
        out_specs=out_specs,
        scratch_shapes=list(scratch),
        compiler_params=pltpu.CompilerParams(vmem_limit_bytes=VMEM_BYTES),
        cost_estimate=pl.CostEstimate(flops=flops, bytes_accessed=moved, transcendentals=0),
    )


def step_pairs(count, step):
    if count & (count - 1) == 0:
        return [(source, source ^ step) for source in range(count)]
    return [(source, (source + step) % count) for source in range(count)]


def partner(me, step, count):
    if count & (count - 1) == 0:
        return me ^ step, me ^ step
    return (me + step) % count, (me + count - step) % count


def gather_fields(halves):
    count = lax.axis_size("kern")
    if count == 4 and len(halves) == 2:
        near, across = step_pairs(count, 1), step_pairs(count, 2)
        low, high = halves
        near_low = lax.ppermute(low, "kern", near)
        across_high = lax.ppermute(high, "kern", across)
        near_high = lax.ppermute(high, "kern", near)
        across_low = lax.ppermute(low, "kern", across)
        last_low = lax.ppermute(near_low, "kern", across)
        last_high = lax.ppermute(across_high, "kern", near)
        return [halves, [near_low, near_high], [across_low, across_high], [last_low, last_high]]
    fields = [halves]
    for step in range(1, count):
        fields.append([lax.ppermute(half, "kern", step_pairs(count, step)) for half in halves])
    return fields


class Message:
    def __init__(self, count, reach, ahead=None, turn=0, slot=None):
        self.count, self.reach, self.slot = count, reach, slot
        self.ahead, self.turn = ahead, turn
        self.width = 1
        if slot is None and ahead <= reach and count - ahead <= reach:
            self.width = 2
        offset = ahead if slot is None else offset_of(slot, reach)
        self.pairs = [(source, (source - offset) % count) for source in range(count)]
        if slot is None and turn is not None:
            self.pairs = [(source, self.mate(source)) for source in range(count)]

    def mate(self, me):
        upward = 1 - 2 * ((me // math.gcd(self.ahead, self.count) + self.turn) % 2)
        return (me + upward * self.ahead + self.count) % self.count

    def across(self):
        half = self.count // 2
        return self.width * sum((a < half) != (b < half) for a, b in self.pairs)

    def slots(self, me, sending):
        if self.slot is not None:
            return [self.slot]
        count, reach = self.count, self.reach
        if self.turn is None:
            ahead = self.ahead
        else:
            mate = self.mate(me)
            ahead = lax.rem((me - mate if sending else mate - me) + count, count)
        below = ahead - count + reach
        if self.width == 1:
            return [jnp.where(ahead <= reach, ahead + reach - 1, below)]
        return [ahead + reach - 1, below]


def offset_of(slot, reach):
    return slot - reach if slot < reach else slot - reach + 1


def message_sets_of(count, slots):
    reach = slots // 2
    if not reach < count <= 2 * reach:
        return [[Message(count, reach, slot=slot) for slot in range(slots)]]
    messages = []
    if count & (count - 1) == 0:
        for ahead in range(1, count // 2 + 1):
            for turn in range(1 if 2 * ahead == count else 2):
                messages.append(Message(count, reach, ahead, turn))
    else:
        messages = [Message(count, reach, ahead, None) for ahead in range(1, count)]
    messages.sort(key=lambda message: -message.across())
    return [messages[: count // 2 - 1], messages[count // 2 - 1 :]]


def chunks_of(messages, most=4):
    chunks, held = [[]], 0
    for at, message in enumerate(messages):
        if held and held + message.width > most:
            chunks.append([])
            held = 0
        chunks[-1].append(at)
        held += message.width
    return chunks


def chunk_coefficients(split_ref, base, chunk, messages, rank, both, outs):
    size = rank * sum(messages[at].width for at in chunk)
    got = fold(dot(split_ref[pl.ds(base, 2 * size)], both))
    got = got[:size] + got[size:]
    row = 0
    for at in chunk:
        for w in range(messages[at].width):
            outs[at][w] = got[row : row + rank]
            row += rank
    return base + 2 * size


def first_coeff_kernel(messages, fresh, cols_ref, right_ref, *refs):
    refs = refs if fresh else refs[1:]
    outs, refs = refs[: len(messages)], refs[len(messages) :]
    split_ref = refs[0]
    rank = right_ref.shape[1]
    me = lax.axis_index("tile")
    if fresh:
        both_ref, right, sems, cols = refs[1:]
        cols_copy = pltpu.make_async_copy(cols_ref, cols, sems.at[right.shape[0]])
        cols_copy.start()
    else:
        both_ref = cols_ref
        right, sems = refs[1:]
    copies = []
    for message in messages:
        for slot in message.slots(me, True):
            at = len(copies)
            copies.append(pltpu.make_async_copy(right_ref.at[slot], right.at[at], sems.at[at]))
            copies[-1].start()
    if fresh:
        cols_copy.wait()
        both_ref[...] = side_by_side(cols[...])
    both = both_ref[...]
    base, block = 0, 0
    for chunk in chunks_of(messages):
        blocks = sum(messages[at].width for at in chunk)
        for b in range(blocks):
            copies[block].wait()
            hi, lo = split(right[block])
            split_ref[pl.ds(base + b * rank, rank)] = hi
            split_ref[pl.ds(base + (blocks + b) * rank, rank)] = lo
            block += 1
        base = chunk_coefficients(split_ref, base, chunk, messages, rank, both, outs)


def first_coefficients(cols, right_tile, messages, after=None):
    fresh = after is None
    slots, rank, size = right_tile.shape
    blocks = sum(message.width for message in messages)
    width = cols.shape[1] if fresh else cols.shape[1] // 2
    outs = [struct(message.width, rank, width) for message in messages]
    outs.append(struct(2 * blocks * rank, size, dtype=bf16))
    scratch = [pltpu.VMEM((blocks, rank, size), f32), pltpu.SemaphoreType.DMA((blocks + 1,))]
    if fresh:
        outs.append(struct(size, 2 * width, dtype=bf16))
        scratch.append(pltpu.VMEM(cols.shape, f32))
    got = call(
        functools.partial(first_coeff_kernel, messages, fresh),
        outs,
        [in_vmem] * len(outs),
        [in_hbm, in_hbm] if fresh else [in_vmem, in_hbm, in_any],
        scratch,
        flops=8 * blocks * rank * size * width,
        moved=4 * blocks * rank * (2 * size + width),
    )(*((to_hbm(cols), to_hbm(right_tile)) if fresh else (cols, to_hbm(right_tile), after)))
    return got[: len(messages)], got[len(messages)], got[-1] if fresh else cols


def mix_coeff_kernel(messages, halves, *refs):
    count = lax.axis_size("kern")
    fields, refs = refs[: count * halves], refs[count * halves :]
    weights_ref, split_ref = refs[:2]
    outs, (cols_ref, both_ref) = refs[2:-2], refs[-2:]
    me = lax.axis_index("kern")
    part = fields[0].shape[0]
    for half in range(halves):
        rows_of = pl.ds(half * part, part)
        total = None
        for step in range(count):
            source = partner(me, step, count)[1]
            term = fields[step * halves + half][...] * weights_ref[source, rows_of]
            total = term if total is None else total + term
        cols_ref[rows_of] = total
        both_ref[rows_of] = side_by_side(total)
    both = both_ref[...]
    rank = outs[0].shape[1]
    base = 0
    for chunk in chunks_of(messages):
        base = chunk_coefficients(split_ref, base, chunk, messages, rank, both, outs)


def mixed_coefficients(fields, weights, split_right, messages, rank):
    halves = len(fields[0])
    part, width = fields[0][0].shape
    size = part * halves
    total = split_right.shape[0]
    outs = [struct(message.width, rank, width) for message in messages]
    outs += [struct(size, width), struct(size, 2 * width, dtype=bf16)]
    flat = [half for field in fields for half in field]
    got = call(
        functools.partial(mix_coeff_kernel, messages, halves),
        outs,
        [in_vmem] * len(outs),
        [in_vmem] * (len(flat) + 2),
        flops=4 * total * size * width,
        moved=2 * total * (size + width),
    )(*flat, weights, split_right)
    return got[: len(messages)], got[-2], got[-1]


def next_coeff_kernel(messages, both_ref, split_ref, after_ref, *outs):
    both = both_ref[...]
    rank = outs[0].shape[1]
    base = 0
    for chunk in chunks_of(messages):
        base = chunk_coefficients(split_ref, base, chunk, messages, rank, both, outs)


def next_coefficients(both, split_right, messages, rank, after):
    size, width = both.shape[0], both.shape[1] // 2
    total = split_right.shape[0]
    return call(
        functools.partial(next_coeff_kernel, messages),
        [struct(message.width, rank, width) for message in messages],
        [in_vmem] * len(messages),
        [in_vmem, in_vmem, in_any],
        flops=4 * total * size * width,
        moved=2 * total * (size + width),
    )(both, split_right, after)


def times_diag(diag_ref, cols_ref):
    both = side_by_side(cols_ref[...])
    hi, lo = split(diag_ref[...])
    return fold(dot(hi, both) + dot(lo, both))


def diag_kernel(diag_ref, cols_ref, out_ref):
    out_ref[...] = times_diag(diag_ref, cols_ref)


def diagonal(diag_tile, cols):
    size, width = cols.shape
    return call(
        diag_kernel,
        struct(size, width),
        in_vmem,
        [in_vmem, in_vmem],
        flops=8 * size * size * width,
        moved=4 * size * (size + 2 * width),
    )(diag_tile, cols)


def prepare_kernel(
    halves, diag_hbm, cols_hbm, left_hbm, table_ref, index_ref,
    diag_out, left_out, weights_ref, diag_ref, cols_ref, left_ref, sems,
):
    copies = []
    for at, (source, target) in enumerate(
        ((diag_hbm, diag_ref), (cols_hbm, cols_ref), (left_hbm, left_ref))
    ):
        copies.append(pltpu.make_async_copy(source, target, sems.at[at]))
        copies[-1].start()
    own = table_ref[lax.axis_index("kern")]
    groups, entries = own.shape
    size = index_ref.shape[1]
    hot = (lax.broadcasted_iota(jnp.int32, (entries, size), 0) == index_ref[...]).astype(f32)
    weights = jnp.dot(own, hot, precision=lax.Precision.HIGHEST, preferred_element_type=f32)
    width = weights_ref.shape[2]
    for b in range(groups):
        weights_ref[b] = jnp.broadcast_to(weights[b : b + 1], (width, size)).T
    copies[0].wait()
    copies[1].wait()
    diag_out[...] = times_diag(diag_ref, cols_ref)
    copies[2].wait()
    total = left_ref.shape[0]
    step = 128 if total % 128 == 0 else total
    part = size // halves
    for at in range(0, total, step):
        span = slice(at, at + step)
        hi, lo = split(left_ref[span].T)
        for half in range(halves):
            base = 2 * half * part
            rows_of = slice(half * part, (half + 1) * part)
            left_out[base : base + part, span] = hi[rows_of]
            left_out[base + part : base + 2 * part, span] = lo[rows_of]


def prepare(diag_tile, cols, left_rows, table, index, halves):
    size, width = cols.shape
    total = left_rows.shape[0]
    groups = table.shape[0]
    return call(
        functools.partial(prepare_kernel, halves),
        [
            struct(size, width),
            struct(2 * size, total, dtype=bf16),
            struct(groups, size, width),
        ],
        [in_vmem] * 3,
        [in_hbm] * 3 + [in_vmem] * 2,
        [
            pltpu.VMEM(diag_tile.shape, f32),
            pltpu.VMEM(cols.shape, f32),
            pltpu.VMEM(left_rows.shape, f32),
            pltpu.SemaphoreType.DMA((3,)),
        ],
        flops=8 * size * size * width,
        moved=8 * total * size + 4 * size * (size + 2 * width),
    )(to_hbm(diag_tile), to_hbm(cols), to_hbm(left_rows), table, index)


def row_kernel(messages, halves, final, offs_ref, ranks_ref, *refs):
    gots = refs[: len(messages)]
    left_ref, diag_ref = refs[len(messages) : len(messages) + 2]
    outs = refs[len(messages) + 2 :]
    if final:
        outs, (picked, term_of, stage, sems) = outs[:-4], outs[-4:]
    else:
        outs, (picked, term_of) = outs[:-2], outs[-2:]
    terms = offs_ref.shape[1]
    rank, width = gots[0].shape[1:]
    slots = term_of.shape[0]
    reach = slots // 2
    for slot in range(slots):
        term_of[slot] = -1
    for k in range(terms):
        offset = offs_ref[0, k]
        term_of[jnp.where(offset < 0, offset + reach, offset + reach - 1)] = k
    me = lax.axis_index("tile")
    line = lax.broadcasted_iota(jnp.int32, (rank, width), 0)

    def pick(got, w, term):
        @pl.when(term >= 0)
        def _():
            kept = jnp.where(line < ranks_ref[0, term], got[w], 0.0)
            picked[pl.ds(pl.multiple_of(term * rank, rank), rank)] = kept

    for got, message in zip(gots, messages):
        for w, slot in enumerate(message.slots(me, False)):
            pick(got, w, term_of[slot])
    both = side_by_side(picked[...])
    part = diag_ref.shape[0] // halves
    sent = []
    for half in range(halves):
        rows_of = pl.ds(half * part, part)
        got = fold(dot(left_ref[pl.ds(2 * half * part, 2 * part)], both))
        total = got[:part] + got[part:] + diag_ref[rows_of]
        if final:
            stage[rows_of] = total
            sent.append(
                pltpu.make_async_copy(stage.at[rows_of], outs[0].at[rows_of], sems.at[half])
            )
            sent[-1].start()
        else:
            outs[half][...] = total
    for copy in sent:
        copy.wait()


def rows(offsets, ranks, gots, messages, left_split, diag_part, slots, halves, final):
    size, width = diag_part.shape
    total = left_split.shape[1]
    scratch = [pltpu.VMEM((total, width), f32), pltpu.SMEM((slots,), jnp.int32)]
    if final:
        scratch += [pltpu.VMEM((size, width), f32), pltpu.SemaphoreType.DMA((halves,))]
    return call(
        functools.partial(row_kernel, messages, halves, final),
        pltpu.HBM((size, width), f32) if final else [struct(size // halves, width)] * halves,
        in_hbm if final else [in_vmem] * halves,
        [in_smem, in_smem] + [in_vmem] * (len(messages) + 2),
        scratch,
        flops=8 * total * size * width,
        moved=4 * total * (size + width),
    )(offsets, ranks, *gots, left_split, diag_part)


def deliver(coeffs, messages):
    return [lax.ppermute(sent, "tile", message.pairs) for sent, message in zip(coeffs, messages)]


def local(
    diag_tiles,
    left_factors,
    right_factors,
    tile_offsets,
    tile_ranks,
    mixing,
    block_index,
    rhs_field,
):
    diag_tile = diag_tiles[0, 0]
    right_tile = right_factors[0, 0]
    offsets = tile_offsets[0]
    ranks = tile_ranks[0]
    slots, rank, size = right_tile.shape
    halves = 2 if size % 32 == 0 else 1
    left_rows = left_factors.reshape(-1, size)
    table = mixing.transpose(1, 2, 0)
    index = block_index[None]
    cols = rhs_field[0]

    far, *near = message_sets_of(lax.axis_size("tile"), slots)
    messages = far + [message for group in near for message in group]
    coeffs, split_right, both = first_coefficients(cols, right_tile, far)
    gots, splits = deliver(coeffs, far), [split_right]
    for group in near:
        coeffs, split_right, _ = first_coefficients(both, right_tile, group, gots[0])
        gots += deliver(coeffs, group)
        splits.append(split_right)
    diag_part, left_split, weights = prepare(diag_tile, cols, left_rows, table, index, halves)
    first = rows(offsets, ranks, gots, messages, left_split, diag_part, slots, halves, False)
    fields = gather_fields(first)
    coeffs, cols, both = mixed_coefficients(fields, weights, splits[0], far, rank)
    gots = deliver(coeffs, far)
    for group, split_right in zip(near, splits[1:]):
        gots += deliver(next_coefficients(both, split_right, group, rank, gots[0]), group)
    diag_part = diagonal(diag_tile, cols)
    return rows(offsets, ranks, gots, messages, left_split, diag_part, slots, halves, True)[None]


def solution(mesh):
    in_specs = (
        P("kern", "tile", None, None),
        P("kern", "tile", None, None, None),
        P("kern", "tile", None, None, None),
        P("kern", "tile", None),
        P("kern", "tile", None),
        P(),
        P("tile"),
        P("kern", "tile", None),
    )
    out_specs = P("kern", "tile", None)
    return jax.shard_map(local, mesh=mesh, in_specs=in_specs, out_specs=out_specs, check_vma=False)
```

```python
import functools

import jax
import jax.numpy as jnp
from jax import lax
from jax.experimental import pallas as pl
from jax.experimental.pallas import tpu as pltpu
from jax.sharding import PartitionSpec as P

f32 = jnp.float32
bf16 = jnp.bfloat16
VMEM_BYTES = 24 * 1024 * 1024
in_vmem = pl.BlockSpec(memory_space=pltpu.VMEM)
in_smem = pl.BlockSpec(memory_space=pltpu.SMEM)
in_hbm = pl.BlockSpec(memory_space=pltpu.HBM)
in_any = pl.BlockSpec(memory_space=pl.ANY)


def to_hbm(value):
    return pltpu.with_memory_space_constraint(value, pltpu.HBM)


def struct(*shape, dtype=f32):
    return jax.ShapeDtypeStruct(shape, dtype)


def split(value):
    hi = value.astype(bf16)
    return hi, (value - hi.astype(f32)).astype(bf16)


def side_by_side(value):
    return jnp.concatenate(split(value), axis=1)


def dot(left, right):
    return jnp.dot(left, right, preferred_element_type=f32)


def fold(value):
    width = value.shape[1] // 2
    return value[:, :width] + value[:, width:]


def call(kernel, outs, out_specs, in_specs, scratch=(), flops=0, moved=0):
    return pl.pallas_call(
        kernel,
        out_shape=outs,
        in_specs=in_specs,
        out_specs=out_specs,
        scratch_shapes=list(scratch),
        compiler_params=pltpu.CompilerParams(vmem_limit_bytes=VMEM_BYTES),
        cost_estimate=pl.CostEstimate(flops=flops, bytes_accessed=moved, transcendentals=0),
    )


class Message:
    def __init__(self, pairs, slots, odd_slots=None):
        self.pairs = pairs
        self.slots = slots
        self.odd_slots = odd_slots
        self.width = len(slots)
        half = len(pairs) // 2
        self.across = self.width * sum((a < half) != (b < half) for a, b in pairs)


def messages_of(count, slots, per):
    reach = slots // 2
    groups = {}
    for slot in range(slots):
        offset = slot - reach if slot < reach else slot - reach + 1
        groups.setdefault(offset % count, []).append(slot)
    messages = []
    below, above = reach - 1, reach
    single = groups.get(1) == [above] and groups.get(count - 1) == [below]
    if single and count % 2 == 0 and below // per == above // per:
        del groups[1], groups[count - 1]
        for turn, (even, odd) in enumerate(((below, above), (above, below))):
            pairs = [(at, (at + (1, -1)[(at + turn) % 2]) % count) for at in range(count)]
            messages.append(Message(pairs, [even], [odd]))
    for ahead, group in groups.items():
        messages.append(Message([(at, (at - ahead) % count) for at in range(count)], group))
    return sorted(messages, key=lambda message: -message.across)


def store_coefficients(got, chunk, per, messages, rank, outs):
    size = per * rank
    got = got[:size] + got[size:]

    def piece(slot):
        row = (slot - chunk * per) * rank
        return got[row : row + rank]

    odd = jnp.full((rank, got.shape[1]), lax.axis_index("tile") & 1, jnp.int32) == 1
    for message, out in zip(messages, outs):
        for w, slot in enumerate(message.slots):
            if slot // per == chunk:
                value = piece(slot)
                if message.odd_slots is not None:
                    value = jnp.where(odd, piece(message.odd_slots[w]), value)
                out[w] = value


def first_coeff_kernel(messages, per, cols_ref, right_ref, *refs):
    outs, (split_ref, cols, right, sems) = refs[: len(messages)], refs[len(messages) :]
    slots, rank, size = right.shape
    chunks = slots // per
    cols_copy = pltpu.make_async_copy(cols_ref, cols, sems.at[chunks])
    cols_copy.start()
    copies = []
    for chunk in range(chunks):
        span = pl.ds(chunk * per, per)
        copies.append(pltpu.make_async_copy(right_ref.at[span], right.at[span], sems.at[chunk]))
        copies[-1].start()
    cols_copy.wait()
    both = side_by_side(cols[...])
    for chunk in range(chunks):
        copies[chunk].wait()
        hi, lo = split(right[pl.ds(chunk * per, per)].reshape(per * rank, size))
        base = 2 * chunk * per * rank
        split_ref[pl.ds(base, per * rank)] = hi
        split_ref[pl.ds(base + per * rank, per * rank)] = lo
        got = fold(dot(split_ref[pl.ds(base, 2 * per * rank)], both))
        store_coefficients(got, chunk, per, messages, rank, outs)


def first_coefficients(cols, right_tile, messages, per):
    slots, rank, size = right_tile.shape
    width = cols.shape[1]
    outs = [struct(message.width, rank, width) for message in messages]
    outs.append(struct(2 * slots * rank, size, dtype=bf16))
    got = call(
        functools.partial(first_coeff_kernel, messages, per),
        outs,
        [in_vmem] * len(outs),
        [in_hbm, in_hbm],
        [
            pltpu.VMEM(cols.shape, f32),
            pltpu.VMEM(right_tile.shape, f32),
            pltpu.SemaphoreType.DMA((slots // per + 1,)),
        ],
        flops=8 * slots * rank * size * width,
        moved=4 * slots * rank * (2 * size + width),
    )(to_hbm(cols), to_hbm(right_tile))
    return got[:-1], got[-1]


def halve_kernel(base, own_ref, got_ref, weights_ref, keep_ref, send_ref):
    own, got = own_ref[...], got_ref[...]
    keep_ref[...] = own * weights_ref[base] + got * weights_ref[base + 1]
    send_ref[...] = own * weights_ref[base + 2] + got * weights_ref[base + 3]


def halve(own, got, weights, half):
    part, width = own.shape
    return call(
        functools.partial(halve_kernel, 4 * half),
        [struct(part, width)] * 2,
        [in_vmem] * 2,
        [in_vmem] * 3,
        flops=6 * part * width,
        moved=32 * part * width,
    )(own, got, weights)


def mix(first, weights):
    groups = lax.axis_size("kern")
    if groups != 4:
        fields = [lax.all_gather(part, "kern") for part in first]
        mixed = jnp.sum(jnp.concatenate(fields, axis=1) * weights, axis=0)
        return [(mixed, jnp.zeros_like(mixed))]
    count = lax.axis_size("tile")
    steps = ([], [])
    for group in range(groups):
        for tile in range(count):
            for turn, pairs in enumerate(steps):
                dest = group ^ (1 + (turn + tile) % 2)
                pairs.append((group * count + tile, dest * count + tile))
    axes = ("kern", "tile")
    came = [lax.ppermute(part, axes, pairs) for part, pairs in zip(first, steps)]
    sums = [
        halve(part, got, weights, half)
        for half, (part, got) in enumerate(zip(first, came))
    ]
    return [
        (keep, lax.ppermute(send, axes, pairs)) for (keep, send), pairs in zip(sums, steps[::-1])
    ]


def mixed_coeff_kernel(messages, per, terms, *refs):
    fields, split_ref, outs, cols_ref = refs[:terms], refs[terms], refs[terms + 1 : -1], refs[-1]
    part = fields[0].shape[0]
    for at in range(0, terms, 2):
        total = fields[at][...] + fields[at + 1][...]
        cols_ref[pl.ds(at // 2 * part, part)] = total
    both = side_by_side(cols_ref[...])
    rank = outs[0].shape[1]
    got = fold(dot(split_ref[...], both))
    size = 2 * per * rank
    for chunk in range(split_ref.shape[0] // size):
        here = got[chunk * size : (chunk + 1) * size]
        store_coefficients(here, chunk, per, messages, rank, outs)


def mixed_coefficients(mixed, split_right, messages, per, rank):
    flat = [term for pair in mixed for term in pair]
    part, width = flat[0].shape
    size = part * len(mixed)
    total = split_right.shape[0]
    outs = [struct(message.width, rank, width) for message in messages]
    outs.append(struct(size, width))
    got = call(
        functools.partial(mixed_coeff_kernel, messages, per, len(flat)),
        outs,
        [in_vmem] * len(outs),
        [in_vmem] * (len(flat) + 1),
        flops=4 * total * size * width,
        moved=2 * total * (size + width),
    )(*flat, split_right)
    return got[:-1], got[-1]


def times_diag(diag_ref, cols_ref):
    both = side_by_side(cols_ref[...])
    hi, lo = split(diag_ref[...])
    return fold(dot(hi, both) + dot(lo, both))


def relay_kernel(count, *refs):
    for source, target in zip(refs[:count], refs[-count:]):
        target[...] = source[...]


def relay(values, after):
    return call(
        functools.partial(relay_kernel, len(values)),
        [struct(*value.shape) for value in values],
        [in_vmem] * len(values),
        [in_vmem] * len(values) + [in_any] * len(after),
        moved=8 * sum(value.size for value in values),
    )(*values, *after)


def diag_kernel(diag_ref, cols_ref, out_ref):
    out_ref[...] = times_diag(diag_ref, cols_ref)


def diagonal(diag_tile, cols):
    size, width = cols.shape
    return call(
        diag_kernel,
        struct(size, width),
        in_vmem,
        [in_vmem, in_vmem],
        flops=8 * size * size * width,
        moved=4 * size * (size + 2 * width),
    )(diag_tile, cols)


def weight_rows(size):
    groups = lax.axis_size("kern")
    me = lax.axis_index("kern")
    if groups != 4:
        return [(me * groups + b, slice(0, size)) for b in range(groups)]
    rows_of = []
    odd = lax.axis_index("tile") & 1
    one, two = me ^ (1 + odd), me ^ (2 - odd)
    for half, (first, second) in enumerate(((one, two), (two, one))):
        lanes = slice(half * (size // 2), (half + 1) * (size // 2))
        for a in (me, second):
            for b in (me, first):
                rows_of.append((a * groups + b, lanes))
    return rows_of


def prepare_kernel(
    halves, diag_hbm, cols_hbm, left_hbm, table_ref, index_ref,
    diag_out, left_out, weights_ref, diag_ref, cols_ref, left_ref, full_ref, sems,
):
    copies = []
    for at, (source, target) in enumerate(
        ((diag_hbm, diag_ref), (cols_hbm, cols_ref), (left_hbm, left_ref))
    ):
        copies.append(pltpu.make_async_copy(source, target, sems.at[at]))
        copies[-1].start()
    entries = table_ref.shape[1]
    size = index_ref.shape[1]
    hot = (lax.broadcasted_iota(jnp.int32, (entries, size), 0) == index_ref[...]).astype(f32)
    full_ref[...] = jnp.dot(
        table_ref[...], hot, precision=lax.Precision.HIGHEST, preferred_element_type=f32
    )
    width = weights_ref.shape[2]
    for at, (row, lanes) in enumerate(weight_rows(size)):
        piece = full_ref[pl.ds(row, 1), lanes]
        weights_ref[at] = jnp.broadcast_to(piece, (width, piece.shape[1])).T
    copies[0].wait()
    copies[1].wait()
    diag_out[...] = times_diag(diag_ref, cols_ref)
    copies[2].wait()
    total = left_ref.shape[0]
    step = 128 if total % 128 == 0 else total
    part = size // halves
    for at in range(0, total, step):
        span = slice(at, at + step)
        hi, lo = split(left_ref[span].T)
        for half in range(halves):
            base = 2 * half * part
            rows_of = slice(half * part, (half + 1) * part)
            left_out[base : base + part, span] = hi[rows_of]
            left_out[base + part : base + 2 * part, span] = lo[rows_of]


def prepare(diag_tile, cols, left_rows, table, index, halves):
    size, width = cols.shape
    total = left_rows.shape[0]
    weights = weight_rows(size)
    part = weights[0][1].stop
    return call(
        functools.partial(prepare_kernel, halves),
        [
            struct(size, width),
            struct(2 * size, total, dtype=bf16),
            struct(len(weights), part, width),
        ],
        [in_vmem] * 3,
        [in_hbm] * 3 + [in_vmem] * 2,
        [
            pltpu.VMEM(diag_tile.shape, f32),
            pltpu.VMEM(cols.shape, f32),
            pltpu.VMEM(left_rows.shape, f32),
            pltpu.VMEM((table.shape[0], size), f32),
            pltpu.SemaphoreType.DMA((3,)),
        ],
        flops=8 * size * size * width,
        moved=8 * total * size + 4 * size * (size + 2 * width),
    )(to_hbm(diag_tile), to_hbm(cols), to_hbm(left_rows), table, index)


def row_kernel(messages, halves, final, offs_ref, ranks_ref, *refs):
    gots = refs[: len(messages)]
    left_ref, diag_ref = refs[len(messages) : len(messages) + 2]
    outs = refs[len(messages) + 2 :]
    if final:
        outs, (picked, term_of, stage, sems) = outs[:-4], outs[-4:]
    else:
        outs, (picked, term_of) = outs[:-2], outs[-2:]
    terms = offs_ref.shape[1]
    rank, width = gots[0].shape[1:]
    slots = term_of.shape[0]
    reach = slots // 2
    for slot in range(slots):
        term_of[slot] = -1
    for k in range(terms):
        offset = offs_ref[0, k]
        term_of[jnp.where(offset < 0, offset + reach, offset + reach - 1)] = k
    line = lax.broadcasted_iota(jnp.int32, (rank, width), 0)

    def pick(got, w, term):
        @pl.when(term >= 0)
        def _():
            kept = jnp.where(line < ranks_ref[0, term], got[w], 0.0)
            picked[pl.ds(pl.multiple_of(term * rank, rank), rank)] = kept

    for got, message in zip(gots, messages):
        for w, slot in enumerate(message.slots):
            if message.odd_slots is not None:
                slot = jnp.where((lax.axis_index("tile") & 1) == 1, slot, message.odd_slots[w])
            pick(got, w, term_of[slot])
    both = side_by_side(picked[...])
    part = diag_ref.shape[0] // halves
    sent = []
    got = fold(dot(left_ref[...], both))
    for half in range(halves):
        rows_of = pl.ds(half * part, part)
        base = 2 * half * part
        total = got[base : base + part] + got[base + part : base + 2 * part] + diag_ref[rows_of]
        if final:
            stage[rows_of] = total
            sent.append(
                pltpu.make_async_copy(stage.at[rows_of], outs[0].at[rows_of], sems.at[half])
            )
            sent[-1].start()
        else:
            outs[half][...] = total
    for copy in sent:
        copy.wait()


def rows(offsets, ranks, gots, messages, left_split, diag_part, slots, halves, final):
    size, width = diag_part.shape
    total = left_split.shape[1]
    scratch = [pltpu.VMEM((total, width), f32), pltpu.SMEM((slots,), jnp.int32)]
    if final:
        scratch += [pltpu.VMEM((size, width), f32), pltpu.SemaphoreType.DMA((halves,))]
    return call(
        functools.partial(row_kernel, messages, halves, final),
        pltpu.HBM((size, width), f32) if final else [struct(size // halves, width)] * halves,
        in_hbm if final else [in_vmem] * halves,
        [in_smem, in_smem] + [in_vmem] * (len(messages) + 2),
        scratch,
        flops=8 * total * size * width,
        moved=4 * total * (size + width),
    )(offsets, ranks, *gots, left_split, diag_part)


def deliver(coeffs, messages, beside=None):
    gots = {}
    small = [at for at, message in enumerate(messages) if message.width < messages[0].width]
    if beside is None:
        small = []
    for at, message in enumerate(messages):
        if at not in small:
            gots[at] = lax.ppermute(coeffs[at], "tile", message.pairs)
    if small:
        values = relay([coeffs[at] for at in small], [gots[0], beside])
        for at, value in zip(small, values):
            gots[at] = lax.ppermute(value, "tile", messages[at].pairs)
    return [gots[at] for at in range(len(messages))]


def local(
    diag_tiles,
    left_factors,
    right_factors,
    tile_offsets,
    tile_ranks,
    mixing,
    block_index,
    rhs_field,
):
    diag_tile = diag_tiles[0, 0]
    right_tile = right_factors[0, 0]
    offsets = tile_offsets[0]
    ranks = tile_ranks[0]
    slots, rank, size = right_tile.shape
    halves = 2 if size % 32 == 0 else 1
    left_rows = left_factors.reshape(-1, size)
    groups = lax.axis_size("kern")
    table = mixing.reshape(mixing.shape[0], groups * groups).T
    index = block_index[None]
    cols = rhs_field[0]

    per = 4 if slots % 4 == 0 else slots
    messages = messages_of(lax.axis_size("tile"), slots, per)
    coeffs, split_right = first_coefficients(cols, right_tile, messages, per)
    gots = deliver(coeffs, messages)
    diag_part, left_split, weights = prepare(diag_tile, cols, left_rows, table, index, halves)
    first = rows(offsets, ranks, gots, messages, left_split, diag_part, slots, halves, False)
    mixed = mix(first, weights)
    coeffs, cols = mixed_coefficients(mixed, split_right, messages, per, rank)
    diag_part = diagonal(diag_tile, cols)
    gots = deliver(coeffs, messages, diag_part)
    return rows(offsets, ranks, gots, messages, left_split, diag_part, slots, halves, True)[None]


def solution(mesh):
    in_specs = (
        P("kern", "tile", None, None),
        P("kern", "tile", None, None, None),
        P("kern", "tile", None, None, None),
        P("kern", "tile", None),
        P("kern", "tile", None),
        P(),
        P("tile"),
        P("kern", "tile", None),
    )
    out_specs = P("kern", "tile", None)
    return jax.shard_map(local, mesh=mesh, in_specs=in_specs, out_specs=out_specs, check_vma=False)
```

```python
import functools

import jax
import jax.numpy as jnp
from jax import lax
from jax.experimental import pallas as pl
from jax.experimental.pallas import tpu as pltpu
from jax.sharding import PartitionSpec as P

f32 = jnp.float32
bf16 = jnp.bfloat16
VMEM_BYTES = 24 * 1024 * 1024
in_vmem = pl.BlockSpec(memory_space=pltpu.VMEM)
in_smem = pl.BlockSpec(memory_space=pltpu.SMEM)
in_hbm = pl.BlockSpec(memory_space=pltpu.HBM)
in_any = pl.BlockSpec(memory_space=pl.ANY)


def to_hbm(value):
    return pltpu.with_memory_space_constraint(value, pltpu.HBM)


def struct(*shape, dtype=f32):
    return jax.ShapeDtypeStruct(shape, dtype)


def split(value):
    hi = value.astype(bf16)
    return hi, (value - hi.astype(f32)).astype(bf16)


def side_by_side(value):
    return jnp.concatenate(split(value), axis=1)


def dot(left, right):
    return jnp.dot(left, right, preferred_element_type=f32)


def fold(value):
    width = value.shape[1] // 2
    return value[:, :width] + value[:, width:]


def call(kernel, outs, out_specs, in_specs, scratch=(), flops=0, moved=0):
    return pl.pallas_call(
        kernel,
        out_shape=outs,
        in_specs=in_specs,
        out_specs=out_specs,
        scratch_shapes=list(scratch),
        compiler_params=pltpu.CompilerParams(vmem_limit_bytes=VMEM_BYTES),
        cost_estimate=pl.CostEstimate(flops=flops, bytes_accessed=moved, transcendentals=0),
    )


class Message:
    def __init__(self, pairs, slots, odd_slots=None):
        self.pairs = pairs
        self.slots = slots
        self.odd_slots = odd_slots
        self.width = len(slots)
        half = len(pairs) // 2
        self.across = self.width * sum((a < half) != (b < half) for a, b in pairs)


def message_sets_of(count, slots):
    reach = slots // 2
    groups = {}
    for slot in range(slots):
        offset = slot - reach if slot < reach else slot - reach + 1
        groups.setdefault(offset % count, []).append(slot)
    messages = []
    below, above = reach - 1, reach
    if groups.get(1) == [above] and groups.get(count - 1) == [below] and count % 2 == 0:
        del groups[1], groups[count - 1]
        for turn, (even, odd) in enumerate(((below, above), (above, below))):
            pairs = [(at, (at + (1, -1)[(at + turn) % 2]) % count) for at in range(count)]
            messages.append(Message(pairs, [even], [odd]))
    for ahead, group in groups.items():
        messages.append(Message([(at, (at - ahead) % count) for at in range(count)], group))
    messages.sort(key=lambda message: -message.across)
    return [messages[: len(messages) // 2], messages[len(messages) // 2 :]]


def slots_of(messages):
    return sorted({slot for m in messages for slot in m.slots + (m.odd_slots or [])})


def copy_runs(slots, source, target, sems):
    copies, at = [], 0
    while at < len(slots):
        count = 1
        while at + count < len(slots) and slots[at + count] == slots[at] + count:
            count += 1
        copies.append(
            pltpu.make_async_copy(
                source.at[pl.ds(slots[at], count)], target.at[pl.ds(at, count)], sems.at[at]
            )
        )
        copies[-1].start()
        at += count
    return copies


def store_coefficients(split_ref, both, messages, rank, outs):
    slots = slots_of(messages)
    size = len(slots) * rank
    got = fold(dot(split_ref[...], both))
    got = got[:size] + got[size:]

    def piece(slot):
        row = slots.index(slot) * rank
        return got[row : row + rank]

    odd = jnp.full((rank, got.shape[1]), lax.axis_index("tile") & 1, jnp.int32) == 1
    for message, out in zip(messages, outs):
        for w, slot in enumerate(message.slots):
            value = piece(slot)
            if message.odd_slots is not None:
                value = jnp.where(odd, piece(message.odd_slots[w]), value)
            out[w] = value


def split_rows(right, split_ref):
    count, rank, size = right.shape
    rows = count * rank
    hi, lo = split(right[...].reshape(rows, size))
    split_ref[:rows] = hi
    split_ref[rows:] = lo


def first_coeff_kernel(messages, others, cols_ref, right_ref, *refs):
    outs, refs = refs[: len(messages)], refs[len(messages) :]
    split_ref, both_ref, rest_ref, cols, right, cols_sem, sems, rest_sems = refs
    cols_copy = pltpu.make_async_copy(cols_ref, cols, cols_sem)
    cols_copy.start()
    copies = copy_runs(slots_of(messages), right_ref, right, sems)
    rest = copy_runs(slots_of(others), right_ref, rest_ref, rest_sems)
    cols_copy.wait()
    both_ref[...] = side_by_side(cols[...])
    for copy in copies:
        copy.wait()
    split_rows(right, split_ref)
    store_coefficients(split_ref, both_ref[...], messages, right.shape[1], outs)
    for copy in rest:
        copy.wait()


def first_coefficients(cols, right_tile, messages, others):
    _, rank, size = right_tile.shape
    width = cols.shape[1]
    count, rest = len(slots_of(messages)), len(slots_of(others))
    outs = [struct(message.width, rank, width) for message in messages]
    outs += [
        struct(2 * count * rank, size, dtype=bf16),
        struct(size, 2 * width, dtype=bf16),
        struct(rest, rank, size),
    ]
    got = call(
        functools.partial(first_coeff_kernel, messages, others),
        outs,
        [in_vmem] * len(outs),
        [in_hbm, in_hbm],
        [
            pltpu.VMEM(cols.shape, f32),
            pltpu.VMEM((count, rank, size), f32),
            pltpu.SemaphoreType.DMA,
            pltpu.SemaphoreType.DMA((count,)),
            pltpu.SemaphoreType.DMA((rest,)),
        ],
        flops=8 * count * rank * size * width,
        moved=4 * (count + rest) * rank * size,
    )(to_hbm(cols), to_hbm(right_tile))
    return got[:-3], got[-3], got[-2], got[-1]


def rest_coeff_kernel(messages, both_ref, right_ref, *refs):
    outs, split_ref = refs[:-1], refs[-1]
    split_rows(right_ref, split_ref)
    store_coefficients(split_ref, both_ref[...], messages, right_ref.shape[1], outs)


def rest_coefficients(both, right, messages):
    count, rank, size = right.shape
    width = both.shape[1] // 2
    outs = [struct(message.width, rank, width) for message in messages]
    outs.append(struct(2 * count * rank, size, dtype=bf16))
    got = call(
        functools.partial(rest_coeff_kernel, messages),
        outs,
        [in_vmem] * len(outs),
        [in_vmem] * 2,
        flops=8 * count * rank * size * width,
        moved=8 * count * rank * size,
    )(both, right)
    return got[:-1], got[-1]


def halve_kernel(base, own_ref, got_ref, weights_ref, keep_ref, send_ref):
    own, got = own_ref[...], got_ref[...]
    keep_ref[...] = own * weights_ref[base] + got * weights_ref[base + 1]
    send_ref[...] = own * weights_ref[base + 2] + got * weights_ref[base + 3]


def halve(own, got, weights, half):
    part, width = own.shape
    return call(
        functools.partial(halve_kernel, 4 * half),
        [struct(part, width)] * 2,
        [in_vmem] * 2,
        [in_vmem] * 3,
        flops=6 * part * width,
        moved=32 * part * width,
    )(own, got, weights)


def mix(first, weights):
    groups = lax.axis_size("kern")
    if groups != 4:
        fields = [lax.all_gather(part, "kern") for part in first]
        mixed = jnp.sum(jnp.concatenate(fields, axis=1) * weights, axis=0)
        return [(mixed, jnp.zeros_like(mixed))]
    count = lax.axis_size("tile")
    steps = ([], [])
    for group in range(groups):
        for tile in range(count):
            for turn, pairs in enumerate(steps):
                dest = group ^ (1 + (turn + tile) % 2)
                pairs.append((group * count + tile, dest * count + tile))
    axes = ("kern", "tile")
    came = [lax.ppermute(part, axes, pairs) for part, pairs in zip(first, steps)]
    sums = [
        halve(part, got, weights, half)
        for half, (part, got) in enumerate(zip(first, came))
    ]
    return [
        (keep, lax.ppermute(send, axes, pairs)) for (keep, send), pairs in zip(sums, steps[::-1])
    ]


def mixed_coeff_kernel(messages, terms, *refs):
    fields, split_ref = refs[:terms], refs[terms]
    outs, cols_ref, both_ref = refs[terms + 1 : -2], refs[-2], refs[-1]
    part = fields[0].shape[0]
    for at in range(0, terms, 2):
        rows_of = pl.ds(at // 2 * part, part)
        total = fields[at][...] + fields[at + 1][...]
        cols_ref[rows_of] = total
        both_ref[rows_of] = side_by_side(total)
    store_coefficients(split_ref, both_ref[...], messages, outs[0].shape[1], outs)


def mixed_coefficients(mixed, split_right, messages, rank):
    flat = [term for pair in mixed for term in pair]
    part, width = flat[0].shape
    size = part * len(mixed)
    total = split_right.shape[0]
    outs = [struct(message.width, rank, width) for message in messages]
    outs += [struct(size, width), struct(size, 2 * width, dtype=bf16)]
    got = call(
        functools.partial(mixed_coeff_kernel, messages, len(flat)),
        outs,
        [in_vmem] * len(outs),
        [in_vmem] * (len(flat) + 1),
        flops=4 * total * size * width,
        moved=2 * total * (size + width),
    )(*flat, split_right)
    return got[:-2], got[-2], got[-1]


def next_coeff_kernel(messages, both_ref, split_ref, *outs):
    store_coefficients(split_ref, both_ref[...], messages, outs[0].shape[1], outs)


def next_coefficients(both, split_right, messages, rank):
    size, width = both.shape[0], both.shape[1] // 2
    total = split_right.shape[0]
    return call(
        functools.partial(next_coeff_kernel, messages),
        [struct(message.width, rank, width) for message in messages],
        [in_vmem] * len(messages),
        [in_vmem] * 2,
        flops=4 * total * size * width,
        moved=2 * total * (size + width),
    )(both, split_right)


def times_diag(diag_ref, cols_ref):
    both = side_by_side(cols_ref[...])
    hi, lo = split(diag_ref[...])
    return fold(dot(hi, both) + dot(lo, both))


def relay_kernel(count, *refs):
    for source, target in zip(refs[:count], refs[-count:]):
        target[...] = source[...]


def relay(values, after):
    return call(
        functools.partial(relay_kernel, len(values)),
        [struct(*value.shape) for value in values],
        [in_vmem] * len(values),
        [in_vmem] * len(values) + [in_any] * len(after),
        moved=8 * sum(value.size for value in values),
    )(*values, *after)


def diag_kernel(diag_ref, cols_ref, out_ref):
    out_ref[...] = times_diag(diag_ref, cols_ref)


def diagonal(diag_tile, cols):
    size, width = cols.shape
    return call(
        diag_kernel,
        struct(size, width),
        in_vmem,
        [in_vmem, in_vmem],
        flops=8 * size * size * width,
        moved=4 * size * (size + 2 * width),
    )(diag_tile, cols)


def weight_rows(size):
    groups = lax.axis_size("kern")
    me = lax.axis_index("kern")
    if groups != 4:
        return [(me * groups + b, slice(0, size)) for b in range(groups)]
    rows_of = []
    odd = lax.axis_index("tile") & 1
    one, two = me ^ (1 + odd), me ^ (2 - odd)
    for half, (first, second) in enumerate(((one, two), (two, one))):
        lanes = slice(half * (size // 2), (half + 1) * (size // 2))
        for a in (me, second):
            for b in (me, first):
                rows_of.append((a * groups + b, lanes))
    return rows_of


def prepare_kernel(
    halves, diag_hbm, cols_hbm, left_hbm, table_ref, index_ref,
    diag_out, left_out, weights_ref, diag_ref, cols_ref, left_ref, full_ref, sems,
):
    copies = []
    for at, (source, target) in enumerate(
        ((diag_hbm, diag_ref), (cols_hbm, cols_ref), (left_hbm, left_ref))
    ):
        copies.append(pltpu.make_async_copy(source, target, sems.at[at]))
        copies[-1].start()
    entries = table_ref.shape[1]
    size = index_ref.shape[1]
    hot = (lax.broadcasted_iota(jnp.int32, (entries, size), 0) == index_ref[...]).astype(f32)
    full_ref[...] = jnp.dot(
        table_ref[...], hot, precision=lax.Precision.HIGHEST, preferred_element_type=f32
    )
    width = weights_ref.shape[2]
    for at, (row, lanes) in enumerate(weight_rows(size)):
        piece = full_ref[pl.ds(row, 1), lanes]
        weights_ref[at] = jnp.broadcast_to(piece, (width, piece.shape[1])).T
    copies[0].wait()
    copies[1].wait()
    diag_out[...] = times_diag(diag_ref, cols_ref)
    copies[2].wait()
    total = left_ref.shape[0]
    step = 128 if total % 128 == 0 else total
    part = size // halves
    for at in range(0, total, step):
        span = slice(at, at + step)
        hi, lo = split(left_ref[span].T)
        for half in range(halves):
            base = 2 * half * part
            rows_of = slice(half * part, (half + 1) * part)
            left_out[base : base + part, span] = hi[rows_of]
            left_out[base + part : base + 2 * part, span] = lo[rows_of]


def prepare(diag_tile, cols, left_rows, table, index, halves):
    size, width = cols.shape
    total = left_rows.shape[0]
    weights = weight_rows(size)
    part = weights[0][1].stop
    return call(
        functools.partial(prepare_kernel, halves),
        [
            struct(size, width),
            struct(2 * size, total, dtype=bf16),
            struct(len(weights), part, width),
        ],
        [in_vmem] * 3,
        [in_hbm] * 3 + [in_vmem] * 2,
        [
            pltpu.VMEM(diag_tile.shape, f32),
            pltpu.VMEM(cols.shape, f32),
            pltpu.VMEM(left_rows.shape, f32),
            pltpu.VMEM((table.shape[0], size), f32),
            pltpu.SemaphoreType.DMA((3,)),
        ],
        flops=8 * size * size * width,
        moved=8 * total * size + 4 * size * (size + 2 * width),
    )(to_hbm(diag_tile), to_hbm(cols), to_hbm(left_rows), table, index)


def row_kernel(messages, halves, final, offs_ref, ranks_ref, *refs):
    gots = refs[: len(messages)]
    left_ref, diag_ref = refs[len(messages) : len(messages) + 2]
    outs = refs[len(messages) + 2 :]
    if final:
        outs, (picked, term_of, stage, sems) = outs[:-4], outs[-4:]
    else:
        outs, (picked, term_of) = outs[:-2], outs[-2:]
    terms = offs_ref.shape[1]
    rank, width = gots[0].shape[1:]
    slots = term_of.shape[0]
    reach = slots // 2
    for slot in range(slots):
        term_of[slot] = -1
    for k in range(terms):
        offset = offs_ref[0, k]
        term_of[jnp.where(offset < 0, offset + reach, offset + reach - 1)] = k
    line = lax.broadcasted_iota(jnp.int32, (rank, width), 0)

    def pick(got, w, term):
        @pl.when(term >= 0)
        def _():
            kept = jnp.where(line < ranks_ref[0, term], got[w], 0.0)
            picked[pl.ds(pl.multiple_of(term * rank, rank), rank)] = kept

    for got, message in zip(gots, messages):
        for w, slot in enumerate(message.slots):
            if message.odd_slots is not None:
                slot = jnp.where((lax.axis_index("tile") & 1) == 1, slot, message.odd_slots[w])
            pick(got, w, term_of[slot])
    both = side_by_side(picked[...])
    part = diag_ref.shape[0] // halves
    sent = []
    got = fold(dot(left_ref[...], both))
    for half in range(halves):
        rows_of = pl.ds(half * part, part)
        base = 2 * half * part
        total = got[base : base + part] + got[base + part : base + 2 * part] + diag_ref[rows_of]
        if final:
            stage[rows_of] = total
            sent.append(
                pltpu.make_async_copy(stage.at[rows_of], outs[0].at[rows_of], sems.at[half])
            )
            sent[-1].start()
        else:
            outs[half][...] = total
    for copy in sent:
        copy.wait()


def rows(offsets, ranks, gots, messages, left_split, diag_part, slots, halves, final):
    size, width = diag_part.shape
    total = left_split.shape[1]
    scratch = [pltpu.VMEM((total, width), f32), pltpu.SMEM((slots,), jnp.int32)]
    if final:
        scratch += [pltpu.VMEM((size, width), f32), pltpu.SemaphoreType.DMA((halves,))]
    return call(
        functools.partial(row_kernel, messages, halves, final),
        pltpu.HBM((size, width), f32) if final else [struct(size // halves, width)] * halves,
        in_hbm if final else [in_vmem] * halves,
        [in_smem, in_smem] + [in_vmem] * (len(messages) + 2),
        scratch,
        flops=8 * total * size * width,
        moved=4 * total * (size + width),
    )(offsets, ranks, *gots, left_split, diag_part)


def send(value, message):
    return lax.ppermute(value, "tile", message.pairs)


def send_near(coeffs, messages, after):
    gots = []
    for value, message in zip(coeffs, messages):
        if message.odd_slots is not None and message.across:
            value = relay([value], after)[0]
        gots.append(send(value, message))
    return gots


def local(
    diag_tiles,
    left_factors,
    right_factors,
    tile_offsets,
    tile_ranks,
    mixing,
    block_index,
    rhs_field,
):
    diag_tile = diag_tiles[0, 0]
    right_tile = right_factors[0, 0]
    offsets = tile_offsets[0]
    ranks = tile_ranks[0]
    slots, rank, size = right_tile.shape
    halves = 2 if size % 32 == 0 else 1
    left_rows = left_factors.reshape(-1, size)
    groups = lax.axis_size("kern")
    table = mixing.reshape(mixing.shape[0], groups * groups).T
    index = block_index[None]
    cols = rhs_field[0]

    far, near = message_sets_of(lax.axis_size("tile"), slots)
    messages = far + near
    coeffs, split_far, both, rest = first_coefficients(cols, right_tile, far, near)
    gots = [send(value, message) for value, message in zip(coeffs, far)]
    coeffs, split_near = rest_coefficients(both, rest, near)
    diag_part, left_split, weights = prepare(diag_tile, cols, left_rows, table, index, halves)
    gots += send_near(coeffs, near, [gots[0], diag_part])
    first = rows(offsets, ranks, gots, messages, left_split, diag_part, slots, halves, False)
    mixed = mix(first, weights)
    coeffs, cols, both = mixed_coefficients(mixed, split_far, far, rank)
    gots = [send(value, message) for value, message in zip(coeffs, far)]
    coeffs = next_coefficients(both, split_near, near, rank)
    diag_part = diagonal(diag_tile, cols)
    gots += send_near(coeffs, near, [gots[0], diag_part])
    return rows(offsets, ranks, gots, messages, left_split, diag_part, slots, halves, True)[None]


def solution(mesh):
    in_specs = (
        P("kern", "tile", None, None),
        P("kern", "tile", None, None, None),
        P("kern", "tile", None, None, None),
        P("kern", "tile", None),
        P("kern", "tile", None),
        P(),
        P("tile"),
        P("kern", "tile", None),
    )
    out_specs = P("kern", "tile", None)
    return jax.shard_map(local, mesh=mesh, in_specs=in_specs, out_specs=out_specs, check_vma=False)
```

```python
import functools

import jax
import jax.numpy as jnp
from jax import lax
from jax.experimental import pallas as pl
from jax.experimental.pallas import tpu as pltpu
from jax.sharding import PartitionSpec as P

f32 = jnp.float32
bf16 = jnp.bfloat16
VMEM_BYTES = 24 * 1024 * 1024
in_vmem = pl.BlockSpec(memory_space=pltpu.VMEM)
in_smem = pl.BlockSpec(memory_space=pltpu.SMEM)
in_hbm = pl.BlockSpec(memory_space=pltpu.HBM)
in_any = pl.BlockSpec(memory_space=pl.ANY)


def to_hbm(value):
    return pltpu.with_memory_space_constraint(value, pltpu.HBM)


def struct(*shape, dtype=f32):
    return jax.ShapeDtypeStruct(shape, dtype)


def split(value):
    hi = value.astype(bf16)
    return hi, (value - hi.astype(f32)).astype(bf16)


def side_by_side(value):
    return jnp.concatenate(split(value), axis=1)


def dot(left, right):
    return jnp.dot(left, right, preferred_element_type=f32)


def fold(value):
    width = value.shape[1] // 2
    return value[:, :width] + value[:, width:]


def call(kernel, outs, out_specs, in_specs, scratch=(), flops=0, moved=0):
    return pl.pallas_call(
        kernel,
        out_shape=outs,
        in_specs=in_specs,
        out_specs=out_specs,
        scratch_shapes=list(scratch),
        compiler_params=pltpu.CompilerParams(vmem_limit_bytes=VMEM_BYTES),
        cost_estimate=pl.CostEstimate(flops=flops, bytes_accessed=moved, transcendentals=0),
    )


class Message:
    def __init__(self, pairs, slots, odd_slots=None):
        self.pairs = pairs
        self.slots = slots
        self.odd_slots = odd_slots
        self.width = len(slots)
        half = len(pairs) // 2
        self.across = self.width * sum((a < half) != (b < half) for a, b in pairs)


def message_sets_of(count, slots):
    reach = slots // 2
    groups = {}
    for slot in range(slots):
        offset = slot - reach if slot < reach else slot - reach + 1
        groups.setdefault(offset % count, []).append(slot)
    messages = []
    below, above = reach - 1, reach
    if groups.get(1) == [above] and groups.get(count - 1) == [below] and count % 2 == 0:
        del groups[1], groups[count - 1]
        for turn, (even, odd) in enumerate(((below, above), (above, below))):
            pairs = [(at, (at + (1, -1)[(at + turn) % 2]) % count) for at in range(count)]
            messages.append(Message(pairs, [even], [odd]))
    for ahead, group in groups.items():
        messages.append(Message([(at, (at - ahead) % count) for at in range(count)], group))
    messages.sort(key=lambda message: -message.across)
    return [messages[: len(messages) // 2], messages[len(messages) // 2 :]]


def slots_of(messages):
    return sorted({slot for m in messages for slot in m.slots + (m.odd_slots or [])})


def copy_runs(slots, source, target, sems):
    copies, at = [], 0
    while at < len(slots):
        count = 1
        while at + count < len(slots) and slots[at + count] == slots[at] + count:
            count += 1
        copies.append(
            pltpu.make_async_copy(
                source.at[pl.ds(slots[at], count)], target.at[pl.ds(at, count)], sems.at[at]
            )
        )
        copies[-1].start()
        at += count
    return copies


def store_coefficients(split_ref, both, messages, rank, outs):
    slots = slots_of(messages)
    size = len(slots) * rank
    got = fold(dot(split_ref[...], both))
    got = got[:size] + got[size:]

    def piece(slot):
        row = slots.index(slot) * rank
        return got[row : row + rank]

    odd = jnp.full((rank, got.shape[1]), lax.axis_index("tile") & 1, jnp.int32) == 1
    for message, out in zip(messages, outs):
        for w, slot in enumerate(message.slots):
            value = piece(slot)
            if message.odd_slots is not None:
                value = jnp.where(odd, piece(message.odd_slots[w]), value)
            out[w] = value


def split_rows(right, split_ref):
    count, rank, size = right.shape
    rows = count * rank
    hi, lo = split(right[...].reshape(rows, size))
    split_ref[:rows] = hi
    split_ref[rows:] = lo


def first_coeff_kernel(messages, others, cols_ref, right_ref, *refs):
    outs, refs = refs[: len(messages)], refs[len(messages) :]
    split_ref, both_ref, rest_ref, cols, right, cols_sem, sems, rest_sems = refs
    cols_copy = pltpu.make_async_copy(cols_ref, cols, cols_sem)
    cols_copy.start()
    copies = copy_runs(slots_of(messages), right_ref, right, sems)
    rest = copy_runs(slots_of(others), right_ref, rest_ref, rest_sems)
    cols_copy.wait()
    both_ref[...] = side_by_side(cols[...])
    for copy in copies:
        copy.wait()
    split_rows(right, split_ref)
    store_coefficients(split_ref, both_ref[...], messages, right.shape[1], outs)
    for copy in rest:
        copy.wait()


def first_coefficients(cols, right_tile, messages, others):
    _, rank, size = right_tile.shape
    width = cols.shape[1]
    count, rest = len(slots_of(messages)), len(slots_of(others))
    outs = [struct(message.width, rank, width) for message in messages]
    outs += [
        struct(2 * count * rank, size, dtype=bf16),
        struct(size, 2 * width, dtype=bf16),
        struct(rest, rank, size),
    ]
    got = call(
        functools.partial(first_coeff_kernel, messages, others),
        outs,
        [in_vmem] * len(outs),
        [in_hbm, in_hbm],
        [
            pltpu.VMEM(cols.shape, f32),
            pltpu.VMEM((count, rank, size), f32),
            pltpu.SemaphoreType.DMA,
            pltpu.SemaphoreType.DMA((count,)),
            pltpu.SemaphoreType.DMA((rest,)),
        ],
        flops=8 * count * rank * size * width,
        moved=4 * (count + rest) * rank * size,
    )(to_hbm(cols), to_hbm(right_tile))
    return got[:-3], got[-3], got[-2], got[-1]


def rest_coeff_kernel(messages, both_ref, right_ref, *refs):
    outs, split_ref = refs[:-1], refs[-1]
    split_rows(right_ref, split_ref)
    store_coefficients(split_ref, both_ref[...], messages, right_ref.shape[1], outs)


def rest_coefficients(both, right, messages):
    count, rank, size = right.shape
    width = both.shape[1] // 2
    outs = [struct(message.width, rank, width) for message in messages]
    outs.append(struct(2 * count * rank, size, dtype=bf16))
    got = call(
        functools.partial(rest_coeff_kernel, messages),
        outs,
        [in_vmem] * len(outs),
        [in_vmem] * 2,
        flops=8 * count * rank * size * width,
        moved=8 * count * rank * size,
    )(both, right)
    return got[:-1], got[-1]


def halve_kernel(base, own_ref, got_ref, weights_ref, keep_ref, send_ref):
    own, got = own_ref[...], got_ref[...]
    keep_ref[...] = own * weights_ref[base] + got * weights_ref[base + 1]
    send_ref[...] = own * weights_ref[base + 2] + got * weights_ref[base + 3]


def halve(own, got, weights, half):
    part, width = own.shape
    return call(
        functools.partial(halve_kernel, 4 * half),
        [struct(part, width)] * 2,
        [in_vmem] * 2,
        [in_vmem] * 3,
        flops=6 * part * width,
        moved=32 * part * width,
    )(own, got, weights)


def mix(first, weights):
    groups = lax.axis_size("kern")
    if groups != 4:
        fields = [lax.all_gather(part, "kern") for part in first]
        mixed = jnp.sum(jnp.concatenate(fields, axis=1) * weights, axis=0)
        return [(mixed, jnp.zeros_like(mixed))]
    count = lax.axis_size("tile")
    steps = ([], [])
    for group in range(groups):
        for tile in range(count):
            for turn, pairs in enumerate(steps):
                dest = group ^ (1 + (turn + tile) % 2)
                pairs.append((group * count + tile, dest * count + tile))
    axes = ("kern", "tile")
    came = [lax.ppermute(part, axes, pairs) for part, pairs in zip(first, steps)]
    sums = [
        halve(part, got, weights, half)
        for half, (part, got) in enumerate(zip(first, came))
    ]
    return [
        (keep, lax.ppermute(send, axes, pairs)) for (keep, send), pairs in zip(sums, steps[::-1])
    ]


def mixed_coeff_kernel(messages, terms, *refs):
    fields, split_ref = refs[:terms], refs[terms]
    outs, cols_ref, both_ref = refs[terms + 1 : -2], refs[-2], refs[-1]
    part = fields[0].shape[0]
    for at in range(0, terms, 2):
        rows_of = pl.ds(at // 2 * part, part)
        total = fields[at][...] + fields[at + 1][...]
        cols_ref[rows_of] = total
        both_ref[rows_of] = side_by_side(total)
    store_coefficients(split_ref, both_ref[...], messages, outs[0].shape[1], outs)


def mixed_coefficients(mixed, split_right, messages, rank):
    flat = [term for pair in mixed for term in pair]
    part, width = flat[0].shape
    size = part * len(mixed)
    total = split_right.shape[0]
    outs = [struct(message.width, rank, width) for message in messages]
    outs += [struct(size, width), struct(size, 2 * width, dtype=bf16)]
    got = call(
        functools.partial(mixed_coeff_kernel, messages, len(flat)),
        outs,
        [in_vmem] * len(outs),
        [in_vmem] * (len(flat) + 1),
        flops=4 * total * size * width,
        moved=2 * total * (size + width),
    )(*flat, split_right)
    return got[:-2], got[-2], got[-1]


def next_coeff_kernel(messages, both_ref, split_ref, *outs):
    store_coefficients(split_ref, both_ref[...], messages, outs[0].shape[1], outs)


def next_coefficients(both, split_right, messages, rank):
    size, width = both.shape[0], both.shape[1] // 2
    total = split_right.shape[0]
    return call(
        functools.partial(next_coeff_kernel, messages),
        [struct(message.width, rank, width) for message in messages],
        [in_vmem] * len(messages),
        [in_vmem] * 2,
        flops=4 * total * size * width,
        moved=2 * total * (size + width),
    )(both, split_right)


def times_diag(diag_ref, cols_ref):
    both = side_by_side(cols_ref[...])
    hi, lo = split(diag_ref[...])
    return fold(dot(hi, both) + dot(lo, both))


def relay_kernel(count, *refs):
    for source, target in zip(refs[:count], refs[-count:]):
        target[...] = source[...]


def relay(values, after):
    return call(
        functools.partial(relay_kernel, len(values)),
        [struct(*value.shape) for value in values],
        [in_vmem] * len(values),
        [in_vmem] * len(values) + [in_any] * len(after),
        moved=8 * sum(value.size for value in values),
    )(*values, *after)


def diag_kernel(diag_ref, cols_ref, out_ref):
    out_ref[...] = times_diag(diag_ref, cols_ref)


def diagonal(diag_tile, cols):
    size, width = cols.shape
    return call(
        diag_kernel,
        struct(size, width),
        in_vmem,
        [in_vmem, in_vmem],
        flops=8 * size * size * width,
        moved=4 * size * (size + 2 * width),
    )(diag_tile, cols)


def weight_rows(size):
    groups = lax.axis_size("kern")
    me = lax.axis_index("kern")
    if groups != 4:
        return [(me * groups + b, slice(0, size)) for b in range(groups)]
    rows_of = []
    odd = lax.axis_index("tile") & 1
    one, two = me ^ (1 + odd), me ^ (2 - odd)
    for half, (first, second) in enumerate(((one, two), (two, one))):
        lanes = slice(half * (size // 2), (half + 1) * (size // 2))
        for a in (me, second):
            for b in (me, first):
                rows_of.append((a * groups + b, lanes))
    return rows_of


def prepare_kernel(
    halves, diag_hbm, cols_hbm, left_hbm, table_ref, index_ref,
    diag_out, left_out, weights_ref, diag_ref, cols_ref, left_ref, full_ref, sems,
):
    copies = []
    for at, (source, target) in enumerate(
        ((diag_hbm, diag_ref), (cols_hbm, cols_ref), (left_hbm, left_ref))
    ):
        copies.append(pltpu.make_async_copy(source, target, sems.at[at]))
        copies[-1].start()
    entries = table_ref.shape[1]
    size = index_ref.shape[1]
    hot = (lax.broadcasted_iota(jnp.int32, (entries, size), 0) == index_ref[...]).astype(f32)
    full_ref[...] = jnp.dot(
        table_ref[...], hot, precision=lax.Precision.HIGHEST, preferred_element_type=f32
    )
    width = weights_ref.shape[2]
    for at, (row, lanes) in enumerate(weight_rows(size)):
        piece = full_ref[pl.ds(row, 1), lanes]
        weights_ref[at] = jnp.broadcast_to(piece, (width, piece.shape[1])).T
    copies[0].wait()
    copies[1].wait()
    diag_out[...] = times_diag(diag_ref, cols_ref)
    copies[2].wait()
    total = left_ref.shape[0]
    step = 128 if total % 128 == 0 else total
    part = size // halves
    for at in range(0, total, step):
        span = slice(at, at + step)
        hi, lo = split(left_ref[span].T)
        for half in range(halves):
            base = 2 * half * part
            rows_of = slice(half * part, (half + 1) * part)
            left_out[base : base + part, span] = hi[rows_of]
            left_out[base + part : base + 2 * part, span] = lo[rows_of]


def prepare(diag_tile, cols, left_rows, table, index, halves):
    size, width = cols.shape
    total = left_rows.shape[0]
    weights = weight_rows(size)
    part = weights[0][1].stop
    return call(
        functools.partial(prepare_kernel, halves),
        [
            struct(size, width),
            struct(2 * size, total, dtype=bf16),
            struct(len(weights), part, width),
        ],
        [in_vmem] * 3,
        [in_hbm] * 3 + [in_vmem] * 2,
        [
            pltpu.VMEM(diag_tile.shape, f32),
            pltpu.VMEM(cols.shape, f32),
            pltpu.VMEM(left_rows.shape, f32),
            pltpu.VMEM((table.shape[0], size), f32),
            pltpu.SemaphoreType.DMA((3,)),
        ],
        flops=8 * size * size * width,
        moved=8 * total * size + 4 * size * (size + 2 * width),
    )(to_hbm(diag_tile), to_hbm(cols), to_hbm(left_rows), table, index)


def row_kernel(messages, halves, final, offs_ref, ranks_ref, *refs):
    gots = refs[: len(messages)]
    left_ref, diag_ref = refs[len(messages) : len(messages) + 2]
    outs = refs[len(messages) + 2 :]
    if final:
        outs, (picked, term_of, stage, sems) = outs[:-4], outs[-4:]
    else:
        outs, (picked, term_of) = outs[:-2], outs[-2:]
    terms = offs_ref.shape[1]
    rank, width = gots[0].shape[1:]
    slots = term_of.shape[0]
    reach = slots // 2
    for slot in range(slots):
        term_of[slot] = -1
    for k in range(terms):
        offset = offs_ref[0, k]
        term_of[jnp.where(offset < 0, offset + reach, offset + reach - 1)] = k
    line = lax.broadcasted_iota(jnp.int32, (rank, width), 0)

    def pick(got, w, term):
        @pl.when(term >= 0)
        def _():
            kept = jnp.where(line < ranks_ref[0, term], got[w], 0.0)
            picked[pl.ds(pl.multiple_of(term * rank, rank), rank)] = kept

    for got, message in zip(gots, messages):
        for w, slot in enumerate(message.slots):
            if message.odd_slots is not None:
                slot = jnp.where((lax.axis_index("tile") & 1) == 1, slot, message.odd_slots[w])
            pick(got, w, term_of[slot])
    both = side_by_side(picked[...])
    part = diag_ref.shape[0] // halves
    sent = []
    got = fold(dot(left_ref[...], both))
    for half in range(halves):
        rows_of = pl.ds(half * part, part)
        base = 2 * half * part
        total = got[base : base + part] + got[base + part : base + 2 * part] + diag_ref[rows_of]
        if final:
            stage[rows_of] = total
            sent.append(
                pltpu.make_async_copy(stage.at[rows_of], outs[0].at[rows_of], sems.at[half])
            )
            sent[-1].start()
        else:
            outs[half][...] = total
    for copy in sent:
        copy.wait()


def rows(offsets, ranks, gots, messages, left_split, diag_part, slots, halves, final):
    size, width = diag_part.shape
    total = left_split.shape[1]
    scratch = [pltpu.VMEM((total, width), f32), pltpu.SMEM((slots,), jnp.int32)]
    if final:
        scratch += [pltpu.VMEM((size, width), f32), pltpu.SemaphoreType.DMA((halves,))]
    return call(
        functools.partial(row_kernel, messages, halves, final),
        pltpu.HBM((size, width), f32) if final else [struct(size // halves, width)] * halves,
        in_hbm if final else [in_vmem] * halves,
        [in_smem, in_smem] + [in_vmem] * (len(messages) + 2),
        scratch,
        flops=8 * total * size * width,
        moved=4 * total * (size + width),
    )(offsets, ranks, *gots, left_split, diag_part)


def send(value, message):
    return lax.ppermute(value, "tile", message.pairs)


def send_near(coeffs, messages, after=None):
    gots = []
    for value, message in zip(coeffs, messages):
        if after is not None and message.odd_slots is not None and message.across:
            value = relay([value], after)[0]
        gots.append(send(value, message))
    return gots


def local(
    diag_tiles,
    left_factors,
    right_factors,
    tile_offsets,
    tile_ranks,
    mixing,
    block_index,
    rhs_field,
):
    diag_tile = diag_tiles[0, 0]
    right_tile = right_factors[0, 0]
    offsets = tile_offsets[0]
    ranks = tile_ranks[0]
    slots, rank, size = right_tile.shape
    halves = 2 if size % 32 == 0 else 1
    left_rows = left_factors.reshape(-1, size)
    groups = lax.axis_size("kern")
    table = mixing.reshape(mixing.shape[0], groups * groups).T
    index = block_index[None]
    cols = rhs_field[0]

    far, near = message_sets_of(lax.axis_size("tile"), slots)
    messages = far + near
    coeffs, split_far, both, rest = first_coefficients(cols, right_tile, far, near)
    gots = [send(value, message) for value, message in zip(coeffs, far)]
    coeffs, split_near = rest_coefficients(both, rest, near)
    gots += send_near(coeffs, near)
    diag_part, left_split, weights = prepare(diag_tile, cols, left_rows, table, index, halves)
    first = rows(offsets, ranks, gots, messages, left_split, diag_part, slots, halves, False)
    mixed = mix(first, weights)
    coeffs, cols, both = mixed_coefficients(mixed, split_far, far, rank)
    gots = [send(value, message) for value, message in zip(coeffs, far)]
    coeffs = next_coefficients(both, split_near, near, rank)
    diag_part = diagonal(diag_tile, cols)
    gots += send_near(coeffs, near, [gots[0], diag_part])
    return rows(offsets, ranks, gots, messages, left_split, diag_part, slots, halves, True)[None]


def solution(mesh):
    in_specs = (
        P("kern", "tile", None, None),
        P("kern", "tile", None, None, None),
        P("kern", "tile", None, None, None),
        P("kern", "tile", None),
        P("kern", "tile", None),
        P(),
        P("tile"),
        P("kern", "tile", None),
    )
    out_specs = P("kern", "tile", None)
    return jax.shard_map(local, mesh=mesh, in_specs=in_specs, out_specs=out_specs, check_vma=False)
```

```python
import functools

import jax
import jax.numpy as jnp
from jax import lax
from jax.experimental import pallas as pl
from jax.experimental.pallas import tpu as pltpu
from jax.sharding import PartitionSpec as P

f32 = jnp.float32
bf16 = jnp.bfloat16
VMEM_BYTES = 24 * 1024 * 1024
in_vmem = pl.BlockSpec(memory_space=pltpu.VMEM)
in_smem = pl.BlockSpec(memory_space=pltpu.SMEM)
in_hbm = pl.BlockSpec(memory_space=pltpu.HBM)
in_any = pl.BlockSpec(memory_space=pl.ANY)


def to_hbm(value):
    return pltpu.with_memory_space_constraint(value, pltpu.HBM)


def struct(*shape, dtype=f32):
    return jax.ShapeDtypeStruct(shape, dtype)


def split(value):
    hi = value.astype(bf16)
    return hi, (value - hi.astype(f32)).astype(bf16)


def side_by_side(value):
    return jnp.concatenate(split(value), axis=1)


def dot(left, right):
    return jnp.dot(left, right, preferred_element_type=f32)


def fold(value):
    width = value.shape[1] // 2
    return value[:, :width] + value[:, width:]


def call(kernel, outs, out_specs, in_specs, scratch=(), flops=0, moved=0):
    return pl.pallas_call(
        kernel,
        out_shape=outs,
        in_specs=in_specs,
        out_specs=out_specs,
        scratch_shapes=list(scratch),
        compiler_params=pltpu.CompilerParams(vmem_limit_bytes=VMEM_BYTES),
        cost_estimate=pl.CostEstimate(flops=flops, bytes_accessed=moved, transcendentals=0),
    )


class Message:
    def __init__(self, pairs, slots, odd_slots=None):
        self.pairs = pairs
        self.slots = slots
        self.odd_slots = odd_slots
        self.width = len(slots)
        half = len(pairs) // 2
        self.across = self.width * sum((a < half) != (b < half) for a, b in pairs)


def message_sets_of(count, slots):
    reach = slots // 2
    groups = {}
    for slot in range(slots):
        offset = slot - reach if slot < reach else slot - reach + 1
        groups.setdefault(offset % count, []).append(slot)
    messages = []
    below, above = reach - 1, reach
    if groups.get(1) == [above] and groups.get(count - 1) == [below] and count % 2 == 0:
        del groups[1], groups[count - 1]
        for turn, (even, odd) in enumerate(((below, above), (above, below))):
            pairs = [(at, (at + (1, -1)[(at + turn) % 2]) % count) for at in range(count)]
            messages.append(Message(pairs, [even], [odd]))
    for ahead, group in groups.items():
        messages.append(Message([(at, (at - ahead) % count) for at in range(count)], group))
    messages.sort(key=lambda message: -message.across)
    first = messages[:1] + [m for m in messages[1:] if m.odd_slots is not None]
    return [first, [message for message in messages if message not in first]]


def slots_of(messages):
    return sorted({slot for m in messages for slot in m.slots + (m.odd_slots or [])})


def copy_runs(slots, source, target, sems):
    copies, at = [], 0
    while at < len(slots):
        count = 1
        while at + count < len(slots) and slots[at + count] == slots[at] + count:
            count += 1
        copies.append(
            pltpu.make_async_copy(
                source.at[pl.ds(slots[at], count)], target.at[pl.ds(at, count)], sems.at[at]
            )
        )
        copies[-1].start()
        at += count
    return copies


def store_coefficients(split_ref, both, messages, rank, outs):
    slots = slots_of(messages)
    size = len(slots) * rank
    got = fold(dot(split_ref[...], both))
    got = got[:size] + got[size:]

    def piece(slot):
        row = slots.index(slot) * rank
        return got[row : row + rank]

    odd = jnp.full((rank, got.shape[1]), lax.axis_index("tile") & 1, jnp.int32) == 1
    for message, out in zip(messages, outs):
        for w, slot in enumerate(message.slots):
            value = piece(slot)
            if message.odd_slots is not None:
                value = jnp.where(odd, piece(message.odd_slots[w]), value)
            out[w] = value


def split_rows(right, split_ref):
    count, rank, size = right.shape
    rows = count * rank
    hi, lo = split(right[...].reshape(rows, size))
    split_ref[:rows] = hi
    split_ref[rows:] = lo


def first_coeff_kernel(messages, others, cols_ref, right_ref, *refs):
    outs, refs = refs[: len(messages)], refs[len(messages) :]
    split_ref, both_ref, rest_ref, cols, right, cols_sem, sems, rest_sems = refs
    cols_copy = pltpu.make_async_copy(cols_ref, cols, cols_sem)
    cols_copy.start()
    copies = copy_runs(slots_of(messages), right_ref, right, sems)
    rest = copy_runs(slots_of(others), right_ref, rest_ref, rest_sems)
    cols_copy.wait()
    both_ref[...] = side_by_side(cols[...])
    for copy in copies:
        copy.wait()
    split_rows(right, split_ref)
    store_coefficients(split_ref, both_ref[...], messages, right.shape[1], outs)
    for copy in rest:
        copy.wait()


def first_coefficients(cols, right_tile, messages, others):
    _, rank, size = right_tile.shape
    width = cols.shape[1]
    count, rest = len(slots_of(messages)), len(slots_of(others))
    outs = [struct(message.width, rank, width) for message in messages]
    outs += [
        struct(2 * count * rank, size, dtype=bf16),
        struct(size, 2 * width, dtype=bf16),
        struct(rest, rank, size),
    ]
    got = call(
        functools.partial(first_coeff_kernel, messages, others),
        outs,
        [in_vmem] * len(outs),
        [in_hbm, in_hbm],
        [
            pltpu.VMEM(cols.shape, f32),
            pltpu.VMEM((count, rank, size), f32),
            pltpu.SemaphoreType.DMA,
            pltpu.SemaphoreType.DMA((count,)),
            pltpu.SemaphoreType.DMA((rest,)),
        ],
        flops=8 * count * rank * size * width,
        moved=4 * (count + rest) * rank * size,
    )(to_hbm(cols), to_hbm(right_tile))
    return got[:-3], got[-3], got[-2], got[-1]


def rest_coeff_kernel(messages, both_ref, right_ref, *refs):
    outs, split_ref = refs[:-1], refs[-1]
    split_rows(right_ref, split_ref)
    store_coefficients(split_ref, both_ref[...], messages, right_ref.shape[1], outs)


def rest_coefficients(both, right, messages):
    count, rank, size = right.shape
    width = both.shape[1] // 2
    outs = [struct(message.width, rank, width) for message in messages]
    outs.append(struct(2 * count * rank, size, dtype=bf16))
    got = call(
        functools.partial(rest_coeff_kernel, messages),
        outs,
        [in_vmem] * len(outs),
        [in_vmem] * 2,
        flops=8 * count * rank * size * width,
        moved=8 * count * rank * size,
    )(both, right)
    return got[:-1], got[-1]


def halve_kernel(base, own_ref, got_ref, weights_ref, keep_ref, send_ref):
    own, got = own_ref[...], got_ref[...]
    keep_ref[...] = own * weights_ref[base] + got * weights_ref[base + 1]
    send_ref[...] = own * weights_ref[base + 2] + got * weights_ref[base + 3]


def halve(own, got, weights, half):
    part, width = own.shape
    return call(
        functools.partial(halve_kernel, 4 * half),
        [struct(part, width)] * 2,
        [in_vmem] * 2,
        [in_vmem] * 3,
        flops=6 * part * width,
        moved=32 * part * width,
    )(own, got, weights)


def mix(first, weights):
    groups = lax.axis_size("kern")
    if groups != 4:
        fields = [lax.all_gather(part, "kern") for part in first]
        mixed = jnp.sum(jnp.concatenate(fields, axis=1) * weights, axis=0)
        return [(mixed, jnp.zeros_like(mixed))]
    count = lax.axis_size("tile")
    steps = ([], [])
    for group in range(groups):
        for tile in range(count):
            for turn, pairs in enumerate(steps):
                dest = group ^ (1 + (turn + tile) % 2)
                pairs.append((group * count + tile, dest * count + tile))
    axes = ("kern", "tile")
    came = [lax.ppermute(part, axes, pairs) for part, pairs in zip(first, steps)]
    sums = [
        halve(part, got, weights, half)
        for half, (part, got) in enumerate(zip(first, came))
    ]
    return [
        (keep, lax.ppermute(send, axes, pairs)) for (keep, send), pairs in zip(sums, steps[::-1])
    ]


def mixed_coeff_kernel(messages, terms, *refs):
    fields, split_ref = refs[:terms], refs[terms]
    outs, cols_ref, both_ref = refs[terms + 1 : -2], refs[-2], refs[-1]
    part = fields[0].shape[0]
    for at in range(0, terms, 2):
        rows_of = pl.ds(at // 2 * part, part)
        total = fields[at][...] + fields[at + 1][...]
        cols_ref[rows_of] = total
        both_ref[rows_of] = side_by_side(total)
    store_coefficients(split_ref, both_ref[...], messages, outs[0].shape[1], outs)


def mixed_coefficients(mixed, split_right, messages, rank):
    flat = [term for pair in mixed for term in pair]
    part, width = flat[0].shape
    size = part * len(mixed)
    total = split_right.shape[0]
    outs = [struct(message.width, rank, width) for message in messages]
    outs += [struct(size, width), struct(size, 2 * width, dtype=bf16)]
    got = call(
        functools.partial(mixed_coeff_kernel, messages, len(flat)),
        outs,
        [in_vmem] * len(outs),
        [in_vmem] * (len(flat) + 1),
        flops=4 * total * size * width,
        moved=2 * total * (size + width),
    )(*flat, split_right)
    return got[:-2], got[-2], got[-1]


def next_coeff_kernel(messages, both_ref, split_ref, *outs):
    store_coefficients(split_ref, both_ref[...], messages, outs[0].shape[1], outs)


def next_coefficients(both, split_right, messages, rank):
    size, width = both.shape[0], both.shape[1] // 2
    total = split_right.shape[0]
    return call(
        functools.partial(next_coeff_kernel, messages),
        [struct(message.width, rank, width) for message in messages],
        [in_vmem] * len(messages),
        [in_vmem] * 2,
        flops=4 * total * size * width,
        moved=2 * total * (size + width),
    )(both, split_right)


def times_diag(diag_ref, cols_ref):
    both = side_by_side(cols_ref[...])
    hi, lo = split(diag_ref[...])
    return fold(dot(hi, both) + dot(lo, both))


def relay_kernel(count, *refs):
    for source, target in zip(refs[:count], refs[-count:]):
        target[...] = source[...]


def relay(values, after):
    return call(
        functools.partial(relay_kernel, len(values)),
        [struct(*value.shape) for value in values],
        [in_vmem] * len(values),
        [in_vmem] * len(values) + [in_any] * len(after),
        moved=8 * sum(value.size for value in values),
    )(*values, *after)


def diag_kernel(diag_ref, cols_ref, out_ref):
    out_ref[...] = times_diag(diag_ref, cols_ref)


def diagonal(diag_tile, cols):
    size, width = cols.shape
    return call(
        diag_kernel,
        struct(size, width),
        in_vmem,
        [in_vmem, in_vmem],
        flops=8 * size * size * width,
        moved=4 * size * (size + 2 * width),
    )(diag_tile, cols)


def weight_rows(size):
    groups = lax.axis_size("kern")
    me = lax.axis_index("kern")
    if groups != 4:
        return [(me * groups + b, slice(0, size)) for b in range(groups)]
    rows_of = []
    odd = lax.axis_index("tile") & 1
    one, two = me ^ (1 + odd), me ^ (2 - odd)
    for half, (first, second) in enumerate(((one, two), (two, one))):
        lanes = slice(half * (size // 2), (half + 1) * (size // 2))
        for a in (me, second):
            for b in (me, first):
                rows_of.append((a * groups + b, lanes))
    return rows_of


def prepare_kernel(
    halves, diag_hbm, cols_hbm, left_hbm, table_ref, index_ref,
    diag_out, left_out, weights_ref, diag_ref, cols_ref, left_ref, full_ref, sems,
):
    copies = []
    for at, (source, target) in enumerate(
        ((diag_hbm, diag_ref), (cols_hbm, cols_ref), (left_hbm, left_ref))
    ):
        copies.append(pltpu.make_async_copy(source, target, sems.at[at]))
        copies[-1].start()
    entries = table_ref.shape[1]
    size = index_ref.shape[1]
    hot = (lax.broadcasted_iota(jnp.int32, (entries, size), 0) == index_ref[...]).astype(f32)
    full_ref[...] = jnp.dot(
        table_ref[...], hot, precision=lax.Precision.HIGHEST, preferred_element_type=f32
    )
    width = weights_ref.shape[2]
    for at, (row, lanes) in enumerate(weight_rows(size)):
        piece = full_ref[pl.ds(row, 1), lanes]
        weights_ref[at] = jnp.broadcast_to(piece, (width, piece.shape[1])).T
    copies[0].wait()
    copies[1].wait()
    diag_out[...] = times_diag(diag_ref, cols_ref)
    copies[2].wait()
    total = left_ref.shape[0]
    step = 128 if total % 128 == 0 else total
    part = size // halves
    for at in range(0, total, step):
        span = slice(at, at + step)
        hi, lo = split(left_ref[span].T)
        for half in range(halves):
            base = 2 * half * part
            rows_of = slice(half * part, (half + 1) * part)
            left_out[base : base + part, span] = hi[rows_of]
            left_out[base + part : base + 2 * part, span] = lo[rows_of]


def prepare(diag_tile, cols, left_rows, table, index, halves):
    size, width = cols.shape
    total = left_rows.shape[0]
    weights = weight_rows(size)
    part = weights[0][1].stop
    return call(
        functools.partial(prepare_kernel, halves),
        [
            struct(size, width),
            struct(2 * size, total, dtype=bf16),
            struct(len(weights), part, width),
        ],
        [in_vmem] * 3,
        [in_hbm] * 3 + [in_vmem] * 2,
        [
            pltpu.VMEM(diag_tile.shape, f32),
            pltpu.VMEM(cols.shape, f32),
            pltpu.VMEM(left_rows.shape, f32),
            pltpu.VMEM((table.shape[0], size), f32),
            pltpu.SemaphoreType.DMA((3,)),
        ],
        flops=8 * size * size * width,
        moved=8 * total * size + 4 * size * (size + 2 * width),
    )(to_hbm(diag_tile), to_hbm(cols), to_hbm(left_rows), table, index)


def row_kernel(messages, halves, final, offs_ref, ranks_ref, *refs):
    gots = refs[: len(messages)]
    left_ref, diag_ref = refs[len(messages) : len(messages) + 2]
    outs = refs[len(messages) + 2 :]
    if final:
        outs, (picked, term_of, stage, sems) = outs[:-4], outs[-4:]
    else:
        outs, (picked, term_of) = outs[:-2], outs[-2:]
    terms = offs_ref.shape[1]
    rank, width = gots[0].shape[1:]
    slots = term_of.shape[0]
    reach = slots // 2
    for slot in range(slots):
        term_of[slot] = -1
    for k in range(terms):
        offset = offs_ref[0, k]
        term_of[jnp.where(offset < 0, offset + reach, offset + reach - 1)] = k
    line = lax.broadcasted_iota(jnp.int32, (rank, width), 0)

    def pick(got, w, term):
        @pl.when(term >= 0)
        def _():
            kept = jnp.where(line < ranks_ref[0, term], got[w], 0.0)
            picked[pl.ds(pl.multiple_of(term * rank, rank), rank)] = kept

    for got, message in zip(gots, messages):
        for w, slot in enumerate(message.slots):
            if message.odd_slots is not None:
                slot = jnp.where((lax.axis_index("tile") & 1) == 1, slot, message.odd_slots[w])
            pick(got, w, term_of[slot])
    both = side_by_side(picked[...])
    part = diag_ref.shape[0] // halves
    sent = []
    got = fold(dot(left_ref[...], both))
    for half in range(halves):
        rows_of = pl.ds(half * part, part)
        base = 2 * half * part
        total = got[base : base + part] + got[base + part : base + 2 * part] + diag_ref[rows_of]
        if final:
            stage[rows_of] = total
            sent.append(
                pltpu.make_async_copy(stage.at[rows_of], outs[0].at[rows_of], sems.at[half])
            )
            sent[-1].start()
        else:
            outs[half][...] = total
    for copy in sent:
        copy.wait()


def rows(offsets, ranks, gots, messages, left_split, diag_part, slots, halves, final):
    size, width = diag_part.shape
    total = left_split.shape[1]
    scratch = [pltpu.VMEM((total, width), f32), pltpu.SMEM((slots,), jnp.int32)]
    if final:
        scratch += [pltpu.VMEM((size, width), f32), pltpu.SemaphoreType.DMA((halves,))]
    return call(
        functools.partial(row_kernel, messages, halves, final),
        pltpu.HBM((size, width), f32) if final else [struct(size // halves, width)] * halves,
        in_hbm if final else [in_vmem] * halves,
        [in_smem, in_smem] + [in_vmem] * (len(messages) + 2),
        scratch,
        flops=8 * total * size * width,
        moved=4 * total * (size + width),
    )(offsets, ranks, *gots, left_split, diag_part)


def send(value, message):
    return lax.ppermute(value, "tile", message.pairs)


def send_all(coeffs, messages, after=None):
    gots = []
    for value, message in zip(coeffs, messages):
        if after is not None and message.odd_slots is not None and message.across:
            value = relay([value], [gots[0], after])[0]
        gots.append(send(value, message))
    return gots


def local(
    diag_tiles,
    left_factors,
    right_factors,
    tile_offsets,
    tile_ranks,
    mixing,
    block_index,
    rhs_field,
):
    diag_tile = diag_tiles[0, 0]
    right_tile = right_factors[0, 0]
    offsets = tile_offsets[0]
    ranks = tile_ranks[0]
    slots, rank, size = right_tile.shape
    halves = 2 if size % 32 == 0 else 1
    left_rows = left_factors.reshape(-1, size)
    groups = lax.axis_size("kern")
    table = mixing.reshape(mixing.shape[0], groups * groups).T
    index = block_index[None]
    cols = rhs_field[0]

    one, two = message_sets_of(lax.axis_size("tile"), slots)
    messages = one + two
    coeffs, split_one, both, rest = first_coefficients(cols, right_tile, one, two)
    gots = send_all(coeffs, one)
    coeffs, split_two = rest_coefficients(both, rest, two)
    gots += send_all(coeffs, two)
    diag_part, left_split, weights = prepare(diag_tile, cols, left_rows, table, index, halves)
    first = rows(offsets, ranks, gots, messages, left_split, diag_part, slots, halves, False)
    mixed = mix(first, weights)
    coeffs, cols, both = mixed_coefficients(mixed, split_one, one, rank)
    diag_part = diagonal(diag_tile, cols)
    gots = send_all(coeffs, one, diag_part)
    gots += send_all(next_coefficients(both, split_two, two, rank), two)
    return rows(offsets, ranks, gots, messages, left_split, diag_part, slots, halves, True)[None]


def solution(mesh):
    in_specs = (
        P("kern", "tile", None, None),
        P("kern", "tile", None, None, None),
        P("kern", "tile", None, None, None),
        P("kern", "tile", None),
        P("kern", "tile", None),
        P(),
        P("tile"),
        P("kern", "tile", None),
    )
    out_specs = P("kern", "tile", None)
    return jax.shard_map(local, mesh=mesh, in_specs=in_specs, out_specs=out_specs, check_vma=False)
```

```python
import functools

import jax
import jax.numpy as jnp
from jax import lax
from jax.experimental import pallas as pl
from jax.experimental.pallas import tpu as pltpu
from jax.sharding import PartitionSpec as P

f32 = jnp.float32
bf16 = jnp.bfloat16
VMEM_BYTES = 24 * 1024 * 1024
in_vmem = pl.BlockSpec(memory_space=pltpu.VMEM)
in_smem = pl.BlockSpec(memory_space=pltpu.SMEM)
in_hbm = pl.BlockSpec(memory_space=pltpu.HBM)
in_any = pl.BlockSpec(memory_space=pl.ANY)


def to_hbm(value):
    return pltpu.with_memory_space_constraint(value, pltpu.HBM)


def struct(*shape, dtype=f32):
    return jax.ShapeDtypeStruct(shape, dtype)


def split(value):
    hi = value.astype(bf16)
    return hi, (value - hi.astype(f32)).astype(bf16)


def side_by_side(value):
    return jnp.concatenate(split(value), axis=1)


def dot(left, right):
    return jnp.dot(left, right, preferred_element_type=f32)


def fold(value):
    width = value.shape[1] // 2
    return value[:, :width] + value[:, width:]


def call(kernel, outs, out_specs, in_specs, scratch=(), flops=0, moved=0):
    return pl.pallas_call(
        kernel,
        out_shape=outs,
        in_specs=in_specs,
        out_specs=out_specs,
        scratch_shapes=list(scratch),
        compiler_params=pltpu.CompilerParams(vmem_limit_bytes=VMEM_BYTES),
        cost_estimate=pl.CostEstimate(flops=flops, bytes_accessed=moved, transcendentals=0),
    )


class Message:
    def __init__(self, pairs, slots, odd_slots=None):
        self.pairs = pairs
        self.slots = slots
        self.odd_slots = odd_slots
        self.width = len(slots)
        half = len(pairs) // 2
        self.across = self.width * sum((a < half) != (b < half) for a, b in pairs)


def message_sets_of(count, slots):
    reach = slots // 2
    groups = {}
    for slot in range(slots):
        offset = slot - reach if slot < reach else slot - reach + 1
        groups.setdefault(offset % count, []).append(slot)
    messages = []
    below, above = reach - 1, reach
    if groups.get(1) == [above] and groups.get(count - 1) == [below] and count % 2 == 0:
        del groups[1], groups[count - 1]
        for turn, (even, odd) in enumerate(((below, above), (above, below))):
            pairs = [(at, (at + (1, -1)[(at + turn) % 2]) % count) for at in range(count)]
            messages.append(Message(pairs, [even], [odd]))
    for ahead, group in groups.items():
        messages.append(Message([(at, (at - ahead) % count) for at in range(count)], group))
    messages.sort(key=lambda message: -message.across)
    first = messages[:1] + [m for m in messages[1:] if m.odd_slots is not None]
    return [first, [message for message in messages if message not in first]]


def slots_of(messages):
    return sorted({slot for m in messages for slot in m.slots + (m.odd_slots or [])})


def copy_runs(slots, source, target, sems):
    copies, at = [], 0
    while at < len(slots):
        count = 1
        while at + count < len(slots) and slots[at + count] == slots[at] + count:
            count += 1
        copies.append(
            pltpu.make_async_copy(
                source.at[pl.ds(slots[at], count)], target.at[pl.ds(at, count)], sems.at[at]
            )
        )
        copies[-1].start()
        at += count
    return copies


def store_coefficients(split_ref, both, messages, rank, outs):
    slots = slots_of(messages)
    size = len(slots) * rank
    got = fold(dot(split_ref[...], both))
    got = got[:size] + got[size:]

    def piece(slot):
        row = slots.index(slot) * rank
        return got[row : row + rank]

    odd = jnp.full((rank, got.shape[1]), lax.axis_index("tile") & 1, jnp.int32) == 1
    for message, out in zip(messages, outs):
        for w, slot in enumerate(message.slots):
            value = piece(slot)
            if message.odd_slots is not None:
                value = jnp.where(odd, piece(message.odd_slots[w]), value)
            out[w] = value


def split_rows(right, split_ref):
    count, rank, size = right.shape
    rows = count * rank
    hi, lo = split(right[...].reshape(rows, size))
    split_ref[:rows] = hi
    split_ref[rows:] = lo


def first_coeff_kernel(messages, others, cols_ref, right_ref, *refs):
    outs, refs = refs[: len(messages)], refs[len(messages) :]
    split_ref, both_ref, rest_ref, cols, right, cols_sem, sems, rest_sems = refs
    cols_copy = pltpu.make_async_copy(cols_ref, cols, cols_sem)
    cols_copy.start()
    copies = copy_runs(slots_of(messages), right_ref, right, sems)
    rest = copy_runs(slots_of(others), right_ref, rest_ref, rest_sems)
    cols_copy.wait()
    both_ref[...] = side_by_side(cols[...])
    for copy in copies:
        copy.wait()
    split_rows(right, split_ref)
    store_coefficients(split_ref, both_ref[...], messages, right.shape[1], outs)
    for copy in rest:
        copy.wait()


def first_coefficients(cols, right_tile, messages, others):
    _, rank, size = right_tile.shape
    width = cols.shape[1]
    count, rest = len(slots_of(messages)), len(slots_of(others))
    outs = [struct(message.width, rank, width) for message in messages]
    outs += [
        struct(2 * count * rank, size, dtype=bf16),
        struct(size, 2 * width, dtype=bf16),
        struct(rest, rank, size),
    ]
    got = call(
        functools.partial(first_coeff_kernel, messages, others),
        outs,
        [in_vmem] * len(outs),
        [in_hbm, in_hbm],
        [
            pltpu.VMEM(cols.shape, f32),
            pltpu.VMEM((count, rank, size), f32),
            pltpu.SemaphoreType.DMA,
            pltpu.SemaphoreType.DMA((count,)),
            pltpu.SemaphoreType.DMA((rest,)),
        ],
        flops=8 * count * rank * size * width,
        moved=4 * (count + rest) * rank * size,
    )(to_hbm(cols), to_hbm(right_tile))
    return got[:-3], got[-3], got[-2], got[-1]


def rest_coeff_kernel(messages, both_ref, right_ref, *refs):
    outs, split_ref = refs[:-1], refs[-1]
    split_rows(right_ref, split_ref)
    store_coefficients(split_ref, both_ref[...], messages, right_ref.shape[1], outs)


def rest_coefficients(both, right, messages):
    count, rank, size = right.shape
    width = both.shape[1] // 2
    outs = [struct(message.width, rank, width) for message in messages]
    outs.append(struct(2 * count * rank, size, dtype=bf16))
    got = call(
        functools.partial(rest_coeff_kernel, messages),
        outs,
        [in_vmem] * len(outs),
        [in_vmem] * 2,
        flops=8 * count * rank * size * width,
        moved=8 * count * rank * size,
    )(both, right)
    return got[:-1], got[-1]


def halve_kernel(base, own_ref, got_ref, weights_ref, keep_ref, send_ref):
    own, got = own_ref[...], got_ref[...]
    keep_ref[...] = own * weights_ref[base] + got * weights_ref[base + 1]
    send_ref[...] = own * weights_ref[base + 2] + got * weights_ref[base + 3]


def halve(own, got, weights, half):
    part, width = own.shape
    return call(
        functools.partial(halve_kernel, 4 * half),
        [struct(part, width)] * 2,
        [in_vmem] * 2,
        [in_vmem] * 3,
        flops=6 * part * width,
        moved=32 * part * width,
    )(own, got, weights)


def mix(first, weights):
    groups = lax.axis_size("kern")
    if groups != 4:
        fields = [lax.all_gather(part, "kern") for part in first]
        mixed = jnp.sum(jnp.concatenate(fields, axis=1) * weights, axis=0)
        return [(mixed, jnp.zeros_like(mixed))]
    count = lax.axis_size("tile")
    steps = ([], [])
    for group in range(groups):
        for tile in range(count):
            for turn, pairs in enumerate(steps):
                dest = group ^ (1 + (turn + tile) % 2)
                pairs.append((group * count + tile, dest * count + tile))
    axes = ("kern", "tile")
    came = [lax.ppermute(part, axes, pairs) for part, pairs in zip(first, steps)]
    sums = [
        halve(part, got, weights, half)
        for half, (part, got) in enumerate(zip(first, came))
    ]
    return [
        (keep, lax.ppermute(send, axes, pairs)) for (keep, send), pairs in zip(sums, steps[::-1])
    ]


def mixed_coeff_kernel(messages, terms, *refs):
    fields, split_ref = refs[:terms], refs[terms]
    outs, cols_ref, both_ref = refs[terms + 1 : -2], refs[-2], refs[-1]
    part = fields[0].shape[0]
    for at in range(0, terms, 2):
        rows_of = pl.ds(at // 2 * part, part)
        total = fields[at][...] + fields[at + 1][...]
        cols_ref[rows_of] = total
        both_ref[rows_of] = side_by_side(total)
    store_coefficients(split_ref, both_ref[...], messages, outs[0].shape[1], outs)


def mixed_coefficients(mixed, split_right, messages, rank):
    flat = [term for pair in mixed for term in pair]
    part, width = flat[0].shape
    size = part * len(mixed)
    total = split_right.shape[0]
    outs = [struct(message.width, rank, width) for message in messages]
    outs += [struct(size, width), struct(size, 2 * width, dtype=bf16)]
    got = call(
        functools.partial(mixed_coeff_kernel, messages, len(flat)),
        outs,
        [in_vmem] * len(outs),
        [in_vmem] * (len(flat) + 1),
        flops=4 * total * size * width,
        moved=2 * total * (size + width),
    )(*flat, split_right)
    return got[:-2], got[-2], got[-1]


def next_coeff_kernel(messages, both_ref, split_ref, *outs):
    store_coefficients(split_ref, both_ref[...], messages, outs[0].shape[1], outs)


def next_coefficients(both, split_right, messages, rank):
    size, width = both.shape[0], both.shape[1] // 2
    total = split_right.shape[0]
    return call(
        functools.partial(next_coeff_kernel, messages),
        [struct(message.width, rank, width) for message in messages],
        [in_vmem] * len(messages),
        [in_vmem] * 2,
        flops=4 * total * size * width,
        moved=2 * total * (size + width),
    )(both, split_right)


def times_diag(diag_ref, cols_ref):
    both = side_by_side(cols_ref[...])
    hi, lo = split(diag_ref[...])
    return fold(dot(hi, both) + dot(lo, both))


def relay_kernel(count, *refs):
    for source, target in zip(refs[:count], refs[-count:]):
        target[...] = source[...]


def relay(values, after):
    return call(
        functools.partial(relay_kernel, len(values)),
        [struct(*value.shape) for value in values],
        [in_vmem] * len(values),
        [in_vmem] * len(values) + [in_any] * len(after),
        moved=8 * sum(value.size for value in values),
    )(*values, *after)


def diag_kernel(diag_ref, cols_ref, out_ref):
    out_ref[...] = times_diag(diag_ref, cols_ref)


def diagonal(diag_tile, cols):
    size, width = cols.shape
    return call(
        diag_kernel,
        struct(size, width),
        in_vmem,
        [in_vmem, in_vmem],
        flops=8 * size * size * width,
        moved=4 * size * (size + 2 * width),
    )(diag_tile, cols)


def weight_rows(size):
    groups = lax.axis_size("kern")
    me = lax.axis_index("kern")
    if groups != 4:
        return [(me * groups + b, slice(0, size)) for b in range(groups)]
    rows_of = []
    odd = lax.axis_index("tile") & 1
    one, two = me ^ (1 + odd), me ^ (2 - odd)
    for half, (first, second) in enumerate(((one, two), (two, one))):
        lanes = slice(half * (size // 2), (half + 1) * (size // 2))
        for a in (me, second):
            for b in (me, first):
                rows_of.append((a * groups + b, lanes))
    return rows_of


def prepare_kernel(
    halves, diag_hbm, cols_hbm, left_hbm, table_ref, index_ref,
    diag_out, left_out, weights_ref, diag_ref, cols_ref, left_ref, full_ref, sems,
):
    copies = []
    for at, (source, target) in enumerate(
        ((diag_hbm, diag_ref), (cols_hbm, cols_ref), (left_hbm, left_ref))
    ):
        copies.append(pltpu.make_async_copy(source, target, sems.at[at]))
        copies[-1].start()
    entries = table_ref.shape[1]
    size = index_ref.shape[1]
    hot = (lax.broadcasted_iota(jnp.int32, (entries, size), 0) == index_ref[...]).astype(f32)
    full_ref[...] = jnp.dot(
        table_ref[...], hot, precision=lax.Precision.HIGHEST, preferred_element_type=f32
    )
    width = weights_ref.shape[2]
    for at, (row, lanes) in enumerate(weight_rows(size)):
        piece = full_ref[pl.ds(row, 1), lanes]
        weights_ref[at] = jnp.broadcast_to(piece, (width, piece.shape[1])).T
    copies[0].wait()
    copies[1].wait()
    diag_out[...] = times_diag(diag_ref, cols_ref)
    copies[2].wait()
    total = left_ref.shape[0]
    step = 128 if total % 128 == 0 else total
    part = size // halves
    for at in range(0, total, step):
        span = slice(at, at + step)
        hi, lo = split(left_ref[span].T)
        for half in range(halves):
            base = 2 * half * part
            rows_of = slice(half * part, (half + 1) * part)
            left_out[base : base + part, span] = hi[rows_of]
            left_out[base + part : base + 2 * part, span] = lo[rows_of]


def prepare(diag_tile, cols, left_rows, table, index, halves):
    size, width = cols.shape
    total = left_rows.shape[0]
    weights = weight_rows(size)
    part = weights[0][1].stop
    return call(
        functools.partial(prepare_kernel, halves),
        [
            struct(size, width),
            struct(2 * size, total, dtype=bf16),
            struct(len(weights), part, width),
        ],
        [in_vmem] * 3,
        [in_hbm] * 3 + [in_vmem] * 2,
        [
            pltpu.VMEM(diag_tile.shape, f32),
            pltpu.VMEM(cols.shape, f32),
            pltpu.VMEM(left_rows.shape, f32),
            pltpu.VMEM((table.shape[0], size), f32),
            pltpu.SemaphoreType.DMA((3,)),
        ],
        flops=8 * size * size * width,
        moved=8 * total * size + 4 * size * (size + 2 * width),
    )(to_hbm(diag_tile), to_hbm(cols), to_hbm(left_rows), table, index)


def row_kernel(messages, halves, final, offs_ref, ranks_ref, *refs):
    gots = refs[: len(messages)]
    left_ref, diag_ref = refs[len(messages) : len(messages) + 2]
    outs = refs[len(messages) + 2 :]
    if final:
        outs, (picked, term_of, stage, sems) = outs[:-4], outs[-4:]
    else:
        outs, (picked, term_of) = outs[:-2], outs[-2:]
    terms = offs_ref.shape[1]
    rank, width = gots[0].shape[1:]
    slots = term_of.shape[0]
    reach = slots // 2
    for slot in range(slots):
        term_of[slot] = terms
    for k in range(terms):
        offset = offs_ref[0, k]
        term_of[jnp.where(offset < 0, offset + reach, offset + reach - 1)] = k
    line = lax.broadcasted_iota(jnp.int32, (rank, width), 0)

    def pick(got, w, term):
        last = ranks_ref[0, jnp.minimum(term, terms - 1)]
        kept = jnp.where(line < last, got[w], 0.0)
        picked[pl.ds(pl.multiple_of(term * rank, rank), rank)] = kept

    for got, message in zip(gots, messages):
        for w, slot in enumerate(message.slots):
            if message.odd_slots is not None:
                slot = jnp.where((lax.axis_index("tile") & 1) == 1, slot, message.odd_slots[w])
            pick(got, w, term_of[slot])
    both = side_by_side(picked[: terms * rank])
    part = diag_ref.shape[0] // halves
    sent = []
    got = fold(dot(left_ref[...], both))
    for half in range(halves):
        rows_of = pl.ds(half * part, part)
        base = 2 * half * part
        total = got[base : base + part] + got[base + part : base + 2 * part] + diag_ref[rows_of]
        if final:
            stage[rows_of] = total
            sent.append(
                pltpu.make_async_copy(stage.at[rows_of], outs[0].at[rows_of], sems.at[half])
            )
            sent[-1].start()
        else:
            outs[half][...] = total
    for copy in sent:
        copy.wait()


def rows(offsets, ranks, gots, messages, left_split, diag_part, slots, halves, final):
    size, width = diag_part.shape
    total = left_split.shape[1]
    rank = gots[0].shape[1]
    scratch = [pltpu.VMEM((total + rank, width), f32), pltpu.SMEM((slots,), jnp.int32)]
    if final:
        scratch += [pltpu.VMEM((size, width), f32), pltpu.SemaphoreType.DMA((halves,))]
    return call(
        functools.partial(row_kernel, messages, halves, final),
        pltpu.HBM((size, width), f32) if final else [struct(size // halves, width)] * halves,
        in_hbm if final else [in_vmem] * halves,
        [in_smem, in_smem] + [in_vmem] * (len(messages) + 2),
        scratch,
        flops=8 * total * size * width,
        moved=4 * total * (size + width),
    )(offsets, ranks, *gots, left_split, diag_part)


def send(value, message):
    return lax.ppermute(value, "tile", message.pairs)


def send_all(coeffs, messages, after=None):
    gots = []
    for value, message in zip(coeffs, messages):
        if after is not None and message.odd_slots is not None and message.across:
            value = relay([value], [gots[0], after])[0]
        gots.append(send(value, message))
    return gots


def local(
    diag_tiles,
    left_factors,
    right_factors,
    tile_offsets,
    tile_ranks,
    mixing,
    block_index,
    rhs_field,
):
    diag_tile = diag_tiles[0, 0]
    right_tile = right_factors[0, 0]
    offsets = tile_offsets[0]
    ranks = tile_ranks[0]
    slots, rank, size = right_tile.shape
    halves = 2 if size % 32 == 0 else 1
    left_rows = left_factors.reshape(-1, size)
    groups = lax.axis_size("kern")
    table = mixing.reshape(mixing.shape[0], groups * groups).T
    index = block_index[None]
    cols = rhs_field[0]

    one, two = message_sets_of(lax.axis_size("tile"), slots)
    messages = one + two
    coeffs, split_one, both, rest = first_coefficients(cols, right_tile, one, two)
    gots = send_all(coeffs, one)
    coeffs, split_two = rest_coefficients(both, rest, two)
    gots += send_all(coeffs, two)
    diag_part, left_split, weights = prepare(diag_tile, cols, left_rows, table, index, halves)
    first = rows(offsets, ranks, gots, messages, left_split, diag_part, slots, halves, False)
    mixed = mix(first, weights)
    coeffs, cols, both = mixed_coefficients(mixed, split_one, one, rank)
    diag_part = diagonal(diag_tile, cols)
    gots = send_all(coeffs, one, diag_part)
    gots += send_all(next_coefficients(both, split_two, two, rank), two)
    return rows(offsets, ranks, gots, messages, left_split, diag_part, slots, halves, True)[None]


def solution(mesh):
    in_specs = (
        P("kern", "tile", None, None),
        P("kern", "tile", None, None, None),
        P("kern", "tile", None, None, None),
        P("kern", "tile", None),
        P("kern", "tile", None),
        P(),
        P("tile"),
        P("kern", "tile", None),
    )
    out_specs = P("kern", "tile", None)
    return jax.shard_map(local, mesh=mesh, in_specs=in_specs, out_specs=out_specs, check_vma=False)
```

```python
import functools

import jax
import jax.numpy as jnp
from jax import lax
from jax.experimental import pallas as pl
from jax.experimental.pallas import tpu as pltpu
from jax.sharding import PartitionSpec as P

f32 = jnp.float32
bf16 = jnp.bfloat16
VMEM_BYTES = 24 * 1024 * 1024
in_vmem = pl.BlockSpec(memory_space=pltpu.VMEM)
in_smem = pl.BlockSpec(memory_space=pltpu.SMEM)
in_hbm = pl.BlockSpec(memory_space=pltpu.HBM)
in_any = pl.BlockSpec(memory_space=pl.ANY)


def to_hbm(value):
    return pltpu.with_memory_space_constraint(value, pltpu.HBM)


def struct(*shape, dtype=f32):
    return jax.ShapeDtypeStruct(shape, dtype)


def split(value):
    hi = value.astype(bf16)
    return hi, (value - hi.astype(f32)).astype(bf16)


def side_by_side(value):
    return jnp.concatenate(split(value), axis=1)


def dot(left, right):
    return jnp.dot(left, right, preferred_element_type=f32)


def fold(value):
    width = value.shape[1] // 2
    return value[:, :width] + value[:, width:]


def call(kernel, outs, out_specs, in_specs, scratch=(), flops=0, moved=0):
    return pl.pallas_call(
        kernel,
        out_shape=outs,
        in_specs=in_specs,
        out_specs=out_specs,
        scratch_shapes=list(scratch),
        compiler_params=pltpu.CompilerParams(vmem_limit_bytes=VMEM_BYTES),
        cost_estimate=pl.CostEstimate(flops=flops, bytes_accessed=moved, transcendentals=0),
    )


class Message:
    def __init__(self, pairs, slots, odd_slots=None):
        self.pairs = pairs
        self.slots = slots
        self.odd_slots = odd_slots
        self.width = len(slots)
        half = len(pairs) // 2
        self.across = self.width * sum((a < half) != (b < half) for a, b in pairs)


def message_sets_of(count, slots):
    reach = slots // 2
    groups = {}
    for slot in range(slots):
        offset = slot - reach if slot < reach else slot - reach + 1
        groups.setdefault(offset % count, []).append(slot)
    messages = []
    below, above = reach - 1, reach
    if groups.get(1) == [above] and groups.get(count - 1) == [below] and count % 2 == 0:
        del groups[1], groups[count - 1]
        for turn, (even, odd) in enumerate(((below, above), (above, below))):
            pairs = [(at, (at + (1, -1)[(at + turn) % 2]) % count) for at in range(count)]
            messages.append(Message(pairs, [even], [odd]))
    for ahead, group in groups.items():
        messages.append(Message([(at, (at - ahead) % count) for at in range(count)], group))
    messages.sort(key=lambda message: -message.across)
    first = messages[:1] + [m for m in messages[1:] if m.odd_slots is not None]
    return [first, [message for message in messages if message not in first]]


def slots_of(messages):
    return sorted({slot for m in messages for slot in m.slots + (m.odd_slots or [])})


def copy_runs(slots, source, target, sems):
    copies, at = [], 0
    while at < len(slots):
        count = 1
        while at + count < len(slots) and slots[at + count] == slots[at] + count:
            count += 1
        copies.append(
            pltpu.make_async_copy(
                source.at[pl.ds(slots[at], count)], target.at[pl.ds(at, count)], sems.at[at]
            )
        )
        copies[-1].start()
        at += count
    return copies


def store_coefficients(split_ref, both, messages, rank, outs):
    slots = slots_of(messages)
    size = len(slots) * rank
    got = fold(dot(split_ref[...], both))
    got = got[:size] + got[size:]

    def piece(slot):
        row = slots.index(slot) * rank
        return got[row : row + rank]

    odd = jnp.full((rank, got.shape[1]), lax.axis_index("tile") & 1, jnp.int32) == 1
    for message, out in zip(messages, outs):
        for w, slot in enumerate(message.slots):
            value = piece(slot)
            if message.odd_slots is not None:
                value = jnp.where(odd, piece(message.odd_slots[w]), value)
            out[w] = value


def split_rows(right, split_ref):
    count, rank, size = right.shape
    rows = count * rank
    hi, lo = split(right[...].reshape(rows, size))
    split_ref[:rows] = hi
    split_ref[rows:] = lo


def first_coeff_kernel(messages, others, cols_ref, right_ref, *refs):
    outs, refs = refs[: len(messages)], refs[len(messages) :]
    split_ref, both_ref, rest_ref, cols, right, cols_sem, sems, rest_sems = refs
    cols_copy = pltpu.make_async_copy(cols_ref, cols, cols_sem)
    cols_copy.start()
    copies = copy_runs(slots_of(messages), right_ref, right, sems)
    rest = copy_runs(slots_of(others), right_ref, rest_ref, rest_sems)
    cols_copy.wait()
    both_ref[...] = side_by_side(cols[...])
    for copy in copies:
        copy.wait()
    split_rows(right, split_ref)
    store_coefficients(split_ref, both_ref[...], messages, right.shape[1], outs)
    for copy in rest:
        copy.wait()


def first_coefficients(cols, right_tile, messages, others):
    _, rank, size = right_tile.shape
    width = cols.shape[1]
    count, rest = len(slots_of(messages)), len(slots_of(others))
    outs = [struct(message.width, rank, width) for message in messages]
    outs += [
        struct(2 * count * rank, size, dtype=bf16),
        struct(size, 2 * width, dtype=bf16),
        struct(rest, rank, size),
    ]
    got = call(
        functools.partial(first_coeff_kernel, messages, others),
        outs,
        [in_vmem] * len(outs),
        [in_hbm, in_hbm],
        [
            pltpu.VMEM(cols.shape, f32),
            pltpu.VMEM((count, rank, size), f32),
            pltpu.SemaphoreType.DMA,
            pltpu.SemaphoreType.DMA((count,)),
            pltpu.SemaphoreType.DMA((rest,)),
        ],
        flops=8 * count * rank * size * width,
        moved=4 * (count + rest) * rank * size,
    )(to_hbm(cols), to_hbm(right_tile))
    return got[:-3], got[-3], got[-2], got[-1]


def rest_coeff_kernel(messages, both_ref, right_ref, *refs):
    outs, split_ref = refs[:-1], refs[-1]
    split_rows(right_ref, split_ref)
    store_coefficients(split_ref, both_ref[...], messages, right_ref.shape[1], outs)


def rest_coefficients(both, right, messages):
    count, rank, size = right.shape
    width = both.shape[1] // 2
    outs = [struct(message.width, rank, width) for message in messages]
    outs.append(struct(2 * count * rank, size, dtype=bf16))
    got = call(
        functools.partial(rest_coeff_kernel, messages),
        outs,
        [in_vmem] * len(outs),
        [in_vmem] * 2,
        flops=8 * count * rank * size * width,
        moved=8 * count * rank * size,
    )(both, right)
    return got[:-1], got[-1]


def halve_kernel(base, own_ref, got_ref, weights_ref, keep_ref, send_ref):
    own, got = own_ref[...], got_ref[...]
    keep_ref[...] = own * weights_ref[base] + got * weights_ref[base + 1]
    send_ref[...] = own * weights_ref[base + 2] + got * weights_ref[base + 3]


def halve(own, got, weights, half):
    part, width = own.shape
    return call(
        functools.partial(halve_kernel, 4 * half),
        [struct(part, width)] * 2,
        [in_vmem] * 2,
        [in_vmem] * 3,
        flops=6 * part * width,
        moved=32 * part * width,
    )(own, got, weights)


def mix(first, weights):
    groups = lax.axis_size("kern")
    if groups != 4:
        fields = [lax.all_gather(part, "kern") for part in first]
        mixed = jnp.sum(jnp.concatenate(fields, axis=1) * weights, axis=0)
        return [(mixed, jnp.zeros_like(mixed))]
    count = lax.axis_size("tile")
    steps = ([], [])
    for group in range(groups):
        for tile in range(count):
            for turn, pairs in enumerate(steps):
                dest = group ^ (1 + (turn + tile) % 2)
                pairs.append((group * count + tile, dest * count + tile))
    axes = ("kern", "tile")
    came = [lax.ppermute(part, axes, pairs) for part, pairs in zip(first, steps)]
    sums = [
        halve(part, got, weights, half)
        for half, (part, got) in enumerate(zip(first, came))
    ]
    return [
        (keep, lax.ppermute(send, axes, pairs)) for (keep, send), pairs in zip(sums, steps[::-1])
    ]


def mixed_coeff_kernel(messages, terms, *refs):
    fields, split_ref = refs[:terms], refs[terms]
    outs, cols_ref, both_ref = refs[terms + 1 : -2], refs[-2], refs[-1]
    part = fields[0].shape[0]
    for at in range(0, terms, 2):
        rows_of = pl.ds(at // 2 * part, part)
        total = fields[at][...] + fields[at + 1][...]
        cols_ref[rows_of] = total
        both_ref[rows_of] = side_by_side(total)
    store_coefficients(split_ref, both_ref[...], messages, outs[0].shape[1], outs)


def mixed_coefficients(mixed, split_right, messages, rank):
    flat = [term for pair in mixed for term in pair]
    part, width = flat[0].shape
    size = part * len(mixed)
    total = split_right.shape[0]
    outs = [struct(message.width, rank, width) for message in messages]
    outs += [struct(size, width), struct(size, 2 * width, dtype=bf16)]
    got = call(
        functools.partial(mixed_coeff_kernel, messages, len(flat)),
        outs,
        [in_vmem] * len(outs),
        [in_vmem] * (len(flat) + 1),
        flops=4 * total * size * width,
        moved=2 * total * (size + width),
    )(*flat, split_right)
    return got[:-2], got[-2], got[-1]


def next_coeff_kernel(messages, both_ref, split_ref, *outs):
    store_coefficients(split_ref, both_ref[...], messages, outs[0].shape[1], outs)


def next_coefficients(both, split_right, messages, rank):
    size, width = both.shape[0], both.shape[1] // 2
    total = split_right.shape[0]
    return call(
        functools.partial(next_coeff_kernel, messages),
        [struct(message.width, rank, width) for message in messages],
        [in_vmem] * len(messages),
        [in_vmem] * 2,
        flops=4 * total * size * width,
        moved=2 * total * (size + width),
    )(both, split_right)


def times_diag(diag_ref, cols_ref):
    both = side_by_side(cols_ref[...])
    hi, lo = split(diag_ref[...])
    return fold(dot(hi, both) + dot(lo, both))


def relay_kernel(count, *refs):
    for source, target in zip(refs[:count], refs[-count:]):
        target[...] = source[...]


def relay(values, after):
    return call(
        functools.partial(relay_kernel, len(values)),
        [struct(*value.shape) for value in values],
        [in_vmem] * len(values),
        [in_vmem] * len(values) + [in_any] * len(after),
        moved=8 * sum(value.size for value in values),
    )(*values, *after)


def diag_kernel(diag_ref, cols_ref, out_ref):
    out_ref[...] = times_diag(diag_ref, cols_ref)


def diagonal(diag_tile, cols):
    size, width = cols.shape
    return call(
        diag_kernel,
        struct(size, width),
        in_vmem,
        [in_vmem, in_vmem],
        flops=8 * size * size * width,
        moved=4 * size * (size + 2 * width),
    )(diag_tile, cols)


def weight_rows(size):
    groups = lax.axis_size("kern")
    me = lax.axis_index("kern")
    if groups != 4:
        return [(me * groups + b, slice(0, size)) for b in range(groups)]
    rows_of = []
    odd = lax.axis_index("tile") & 1
    one, two = me ^ (1 + odd), me ^ (2 - odd)
    for half, (first, second) in enumerate(((one, two), (two, one))):
        lanes = slice(half * (size // 2), (half + 1) * (size // 2))
        for a in (me, second):
            for b in (me, first):
                rows_of.append((a * groups + b, lanes))
    return rows_of


def prepare_kernel(
    halves, diag_hbm, cols_hbm, left_hbm, diag_out, left_out, diag_ref, cols_ref, left_ref, sems
):
    copies = []
    for at, (source, target) in enumerate(
        ((diag_hbm, diag_ref), (cols_hbm, cols_ref), (left_hbm, left_ref))
    ):
        copies.append(pltpu.make_async_copy(source, target, sems.at[at]))
        copies[-1].start()
    copies[0].wait()
    copies[1].wait()
    diag_out[...] = times_diag(diag_ref, cols_ref)
    copies[2].wait()
    total, size = left_ref.shape
    step = 128 if total % 128 == 0 else total
    part = size // halves
    for at in range(0, total, step):
        span = slice(at, at + step)
        hi, lo = split(left_ref[span].T)
        for half in range(halves):
            base = 2 * half * part
            rows_of = slice(half * part, (half + 1) * part)
            left_out[base : base + part, span] = hi[rows_of]
            left_out[base + part : base + 2 * part, span] = lo[rows_of]


def prepare(diag_tile, cols, left_rows, halves):
    size, width = cols.shape
    total = left_rows.shape[0]
    return call(
        functools.partial(prepare_kernel, halves),
        [struct(size, width), struct(2 * size, total, dtype=bf16)],
        [in_vmem] * 2,
        [in_hbm] * 3,
        [
            pltpu.VMEM(diag_tile.shape, f32),
            pltpu.VMEM(cols.shape, f32),
            pltpu.VMEM(left_rows.shape, f32),
            pltpu.SemaphoreType.DMA((3,)),
        ],
        flops=8 * size * size * width,
        moved=8 * total * size + 4 * size * (size + 2 * width),
    )(to_hbm(diag_tile), to_hbm(cols), to_hbm(left_rows))


def weights_kernel(table_ref, index_ref, after_ref, weights_ref, full_ref):
    entries = table_ref.shape[1]
    size = index_ref.shape[1]
    hot = (lax.broadcasted_iota(jnp.int32, (entries, size), 0) == index_ref[...]).astype(f32)
    full_ref[...] = jnp.dot(
        table_ref[...], hot, precision=lax.Precision.HIGHEST, preferred_element_type=f32
    )
    width = weights_ref.shape[2]
    for at, (row, lanes) in enumerate(weight_rows(size)):
        piece = full_ref[pl.ds(row, 1), lanes]
        weights_ref[at] = jnp.broadcast_to(piece, (width, piece.shape[1])).T


def spread_weights(table, index, width, after):
    size = index.shape[1]
    rows_of = weight_rows(size)
    part = rows_of[0][1].stop
    return call(
        weights_kernel,
        struct(len(rows_of), part, width),
        in_vmem,
        [in_vmem, in_vmem, in_any],
        [pltpu.VMEM((table.shape[0], size), f32)],
        flops=12 * table.size * size,
        moved=4 * len(rows_of) * part * width,
    )(table, index, after)


def row_kernel(messages, halves, final, offs_ref, ranks_ref, *refs):
    gots = refs[: len(messages)]
    left_ref, diag_ref = refs[len(messages) : len(messages) + 2]
    outs = refs[len(messages) + 2 :]
    if final:
        outs, (picked, term_of, stage, sems) = outs[:-4], outs[-4:]
    else:
        outs, (picked, term_of) = outs[:-2], outs[-2:]
    terms = offs_ref.shape[1]
    rank, width = gots[0].shape[1:]
    slots = term_of.shape[0]
    reach = slots // 2
    for slot in range(slots):
        term_of[slot] = terms
    for k in range(terms):
        offset = offs_ref[0, k]
        term_of[jnp.where(offset < 0, offset + reach, offset + reach - 1)] = k
    line = lax.broadcasted_iota(jnp.int32, (rank, width), 0)

    def pick(got, w, term):
        last = ranks_ref[0, jnp.minimum(term, terms - 1)]
        kept = jnp.where(line < last, got[w], 0.0)
        picked[pl.ds(pl.multiple_of(term * rank, rank), rank)] = kept

    for got, message in zip(gots, messages):
        for w, slot in enumerate(message.slots):
            if message.odd_slots is not None:
                slot = jnp.where((lax.axis_index("tile") & 1) == 1, slot, message.odd_slots[w])
            pick(got, w, term_of[slot])
    both = side_by_side(picked[: terms * rank])
    part = diag_ref.shape[0] // halves
    sent = []
    got = fold(dot(left_ref[...], both))
    for half in range(halves):
        rows_of = pl.ds(half * part, part)
        base = 2 * half * part
        total = got[base : base + part] + got[base + part : base + 2 * part] + diag_ref[rows_of]
        if final:
            stage[rows_of] = total
            sent.append(
                pltpu.make_async_copy(stage.at[rows_of], outs[0].at[rows_of], sems.at[half])
            )
            sent[-1].start()
        else:
            outs[half][...] = total
    for copy in sent:
        copy.wait()


def rows(offsets, ranks, gots, messages, left_split, diag_part, slots, halves, final):
    size, width = diag_part.shape
    total = left_split.shape[1]
    rank = gots[0].shape[1]
    scratch = [pltpu.VMEM((total + rank, width), f32), pltpu.SMEM((slots,), jnp.int32)]
    if final:
        scratch += [pltpu.VMEM((size, width), f32), pltpu.SemaphoreType.DMA((halves,))]
    return call(
        functools.partial(row_kernel, messages, halves, final),
        pltpu.HBM((size, width), f32) if final else [struct(size // halves, width)] * halves,
        in_hbm if final else [in_vmem] * halves,
        [in_smem, in_smem] + [in_vmem] * (len(messages) + 2),
        scratch,
        flops=8 * total * size * width,
        moved=4 * total * (size + width),
    )(offsets, ranks, *gots, left_split, diag_part)


def send(value, message):
    return lax.ppermute(value, "tile", message.pairs)


def send_all(coeffs, messages, after=None):
    gots = []
    for value, message in zip(coeffs, messages):
        if after is not None and message.odd_slots is not None and message.across:
            value = relay([value], [gots[0], after])[0]
        gots.append(send(value, message))
    return gots


def local(
    diag_tiles,
    left_factors,
    right_factors,
    tile_offsets,
    tile_ranks,
    mixing,
    block_index,
    rhs_field,
):
    diag_tile = diag_tiles[0, 0]
    right_tile = right_factors[0, 0]
    offsets = tile_offsets[0]
    ranks = tile_ranks[0]
    slots, rank, size = right_tile.shape
    halves = 2 if size % 32 == 0 else 1
    left_rows = left_factors.reshape(-1, size)
    groups = lax.axis_size("kern")
    table = mixing.reshape(mixing.shape[0], groups * groups).T
    index = block_index[None]
    cols = rhs_field[0]

    one, two = message_sets_of(lax.axis_size("tile"), slots)
    messages = one + two
    coeffs, split_one, both, rest = first_coefficients(cols, right_tile, one, two)
    diag_part, left_split = prepare(diag_tile, cols, left_rows, halves)
    gots = send_all(coeffs, one, diag_part)
    coeffs, split_two = rest_coefficients(both, rest, two)
    gots += send_all(coeffs, two)
    first = rows(offsets, ranks, gots, messages, left_split, diag_part, slots, halves, False)
    weights = spread_weights(table, index, cols.shape[1], first[0])
    mixed = mix(first, weights)
    coeffs, cols, both = mixed_coefficients(mixed, split_one, one, rank)
    diag_part = diagonal(diag_tile, cols)
    gots = send_all(coeffs, one, diag_part)
    gots += send_all(next_coefficients(both, split_two, two, rank), two)
    return rows(offsets, ranks, gots, messages, left_split, diag_part, slots, halves, True)[None]


def solution(mesh):
    in_specs = (
        P("kern", "tile", None, None),
        P("kern", "tile", None, None, None),
        P("kern", "tile", None, None, None),
        P("kern", "tile", None),
        P("kern", "tile", None),
        P(),
        P("tile"),
        P("kern", "tile", None),
    )
    out_specs = P("kern", "tile", None)
    return jax.shard_map(local, mesh=mesh, in_specs=in_specs, out_specs=out_specs, check_vma=False)
```

```python
import functools

import jax
import jax.numpy as jnp
from jax import lax
from jax.experimental import pallas as pl
from jax.experimental.pallas import tpu as pltpu
from jax.sharding import PartitionSpec as P

f32 = jnp.float32
bf16 = jnp.bfloat16
VMEM_BYTES = 24 * 1024 * 1024
in_vmem = pl.BlockSpec(memory_space=pltpu.VMEM)
in_smem = pl.BlockSpec(memory_space=pltpu.SMEM)
in_hbm = pl.BlockSpec(memory_space=pltpu.HBM)
in_any = pl.BlockSpec(memory_space=pl.ANY)


def to_hbm(value):
    return pltpu.with_memory_space_constraint(value, pltpu.HBM)


def struct(*shape, dtype=f32):
    return jax.ShapeDtypeStruct(shape, dtype)


def split(value):
    hi = value.astype(bf16)
    return hi, (value - hi.astype(f32)).astype(bf16)


def side_by_side(value):
    return jnp.concatenate(split(value), axis=1)


def dot(left, right):
    return jnp.dot(left, right, preferred_element_type=f32)


def fold(value):
    width = value.shape[1] // 2
    return value[:, :width] + value[:, width:]


def call(kernel, outs, out_specs, in_specs, scratch=(), flops=0, moved=0):
    return pl.pallas_call(
        kernel,
        out_shape=outs,
        in_specs=in_specs,
        out_specs=out_specs,
        scratch_shapes=list(scratch),
        compiler_params=pltpu.CompilerParams(vmem_limit_bytes=VMEM_BYTES),
        cost_estimate=pl.CostEstimate(flops=flops, bytes_accessed=moved, transcendentals=0),
    )


class Message:
    def __init__(self, pairs, slots, odd_slots=None):
        self.pairs = pairs
        self.slots = slots
        self.odd_slots = odd_slots
        self.width = len(slots)
        half = len(pairs) // 2
        self.across = self.width * sum((a < half) != (b < half) for a, b in pairs)


def message_sets_of(count, slots):
    reach = slots // 2
    groups = {}
    for slot in range(slots):
        offset = slot - reach if slot < reach else slot - reach + 1
        groups.setdefault(offset % count, []).append(slot)
    messages = []
    below, above = reach - 1, reach
    if groups.get(1) == [above] and groups.get(count - 1) == [below] and count % 2 == 0:
        del groups[1], groups[count - 1]
        for turn, (even, odd) in enumerate(((below, above), (above, below))):
            pairs = [(at, (at + (1, -1)[(at + turn) % 2]) % count) for at in range(count)]
            messages.append(Message(pairs, [even], [odd]))
    for ahead, group in groups.items():
        messages.append(Message([(at, (at - ahead) % count) for at in range(count)], group))
    messages.sort(key=lambda message: -message.across)
    first = messages[:1] + [m for m in messages[:0:-1] if m.odd_slots is not None]
    return [first, [message for message in messages if message not in first]]


def slots_of(messages):
    return sorted({slot for m in messages for slot in m.slots + (m.odd_slots or [])})


def copy_runs(slots, source, target, sems):
    copies, at = [], 0
    while at < len(slots):
        count = 1
        while at + count < len(slots) and slots[at + count] == slots[at] + count:
            count += 1
        copies.append(
            pltpu.make_async_copy(
                source.at[pl.ds(slots[at], count)], target.at[pl.ds(at, count)], sems.at[at]
            )
        )
        copies[-1].start()
        at += count
    return copies


def store_coefficients(split_ref, both, messages, rank, outs):
    slots = slots_of(messages)
    size = len(slots) * rank
    got = fold(dot(split_ref[...], both))
    got = got[:size] + got[size:]

    def piece(slot):
        row = slots.index(slot) * rank
        return got[row : row + rank]

    odd = jnp.full((rank, got.shape[1]), lax.axis_index("tile") & 1, jnp.int32) == 1
    for message, out in zip(messages, outs):
        for w, slot in enumerate(message.slots):
            value = piece(slot)
            if message.odd_slots is not None:
                value = jnp.where(odd, piece(message.odd_slots[w]), value)
            out[w] = value


def split_rows(right, split_ref):
    count, rank, size = right.shape
    rows = count * rank
    hi, lo = split(right[...].reshape(rows, size))
    split_ref[:rows] = hi
    split_ref[rows:] = lo


def first_coeff_kernel(messages, others, cols_ref, right_ref, *refs):
    outs, refs = refs[: len(messages)], refs[len(messages) :]
    split_ref, both_ref, rest_ref, cols, right, cols_sem, sems, rest_sems = refs
    cols_copy = pltpu.make_async_copy(cols_ref, cols, cols_sem)
    cols_copy.start()
    copies = copy_runs(slots_of(messages), right_ref, right, sems)
    rest = copy_runs(slots_of(others), right_ref, rest_ref, rest_sems)
    cols_copy.wait()
    both_ref[...] = side_by_side(cols[...])
    for copy in copies:
        copy.wait()
    split_rows(right, split_ref)
    store_coefficients(split_ref, both_ref[...], messages, right.shape[1], outs)
    for copy in rest:
        copy.wait()


def first_coefficients(cols, right_tile, messages, others):
    _, rank, size = right_tile.shape
    width = cols.shape[1]
    count, rest = len(slots_of(messages)), len(slots_of(others))
    outs = [struct(message.width, rank, width) for message in messages]
    outs += [
        struct(2 * count * rank, size, dtype=bf16),
        struct(size, 2 * width, dtype=bf16),
        struct(rest, rank, size),
    ]
    got = call(
        functools.partial(first_coeff_kernel, messages, others),
        outs,
        [in_vmem] * len(outs),
        [in_hbm, in_hbm],
        [
            pltpu.VMEM(cols.shape, f32),
            pltpu.VMEM((count, rank, size), f32),
            pltpu.SemaphoreType.DMA,
            pltpu.SemaphoreType.DMA((count,)),
            pltpu.SemaphoreType.DMA((rest,)),
        ],
        flops=8 * count * rank * size * width,
        moved=4 * (count + rest) * rank * size,
    )(to_hbm(cols), to_hbm(right_tile))
    return got[:-3], got[-3], got[-2], got[-1]


def rest_coeff_kernel(messages, both_ref, right_ref, *refs):
    outs, split_ref = refs[:-1], refs[-1]
    split_rows(right_ref, split_ref)
    store_coefficients(split_ref, both_ref[...], messages, right_ref.shape[1], outs)


def rest_coefficients(both, right, messages):
    count, rank, size = right.shape
    width = both.shape[1] // 2
    outs = [struct(message.width, rank, width) for message in messages]
    outs.append(struct(2 * count * rank, size, dtype=bf16))
    got = call(
        functools.partial(rest_coeff_kernel, messages),
        outs,
        [in_vmem] * len(outs),
        [in_vmem] * 2,
        flops=8 * count * rank * size * width,
        moved=8 * count * rank * size,
    )(both, right)
    return got[:-1], got[-1]


def halve_kernel(base, own_ref, got_ref, weights_ref, keep_ref, send_ref):
    own, got = own_ref[...], got_ref[...]
    keep_ref[...] = own * weights_ref[base] + got * weights_ref[base + 1]
    send_ref[...] = own * weights_ref[base + 2] + got * weights_ref[base + 3]


def halve(own, got, weights, half):
    part, width = own.shape
    return call(
        functools.partial(halve_kernel, 4 * half),
        [struct(part, width)] * 2,
        [in_vmem] * 2,
        [in_vmem] * 3,
        flops=6 * part * width,
        moved=32 * part * width,
    )(own, got, weights)


def mix(first, weights):
    groups = lax.axis_size("kern")
    if groups != 4:
        fields = [lax.all_gather(part, "kern") for part in first]
        mixed = jnp.sum(jnp.concatenate(fields, axis=1) * weights, axis=0)
        return [(mixed, jnp.zeros_like(mixed))]
    count = lax.axis_size("tile")
    steps = ([], [])
    for group in range(groups):
        for tile in range(count):
            for turn, pairs in enumerate(steps):
                dest = group ^ (1 + (turn + tile) % 2)
                pairs.append((group * count + tile, dest * count + tile))
    axes = ("kern", "tile")
    came = [lax.ppermute(part, axes, pairs) for part, pairs in zip(first, steps)]
    sums = [
        halve(part, got, weights, half)
        for half, (part, got) in enumerate(zip(first, came))
    ]
    return [
        (keep, lax.ppermute(send, axes, pairs)) for (keep, send), pairs in zip(sums, steps[::-1])
    ]


def mixed_coeff_kernel(messages, terms, *refs):
    fields, split_ref = refs[:terms], refs[terms]
    outs, cols_ref, both_ref = refs[terms + 1 : -2], refs[-2], refs[-1]
    part = fields[0].shape[0]
    for at in range(0, terms, 2):
        rows_of = pl.ds(at // 2 * part, part)
        total = fields[at][...] + fields[at + 1][...]
        cols_ref[rows_of] = total
        both_ref[rows_of] = side_by_side(total)
    store_coefficients(split_ref, both_ref[...], messages, outs[0].shape[1], outs)


def mixed_coefficients(mixed, split_right, messages, rank):
    flat = [term for pair in mixed for term in pair]
    part, width = flat[0].shape
    size = part * len(mixed)
    total = split_right.shape[0]
    outs = [struct(message.width, rank, width) for message in messages]
    outs += [struct(size, width), struct(size, 2 * width, dtype=bf16)]
    got = call(
        functools.partial(mixed_coeff_kernel, messages, len(flat)),
        outs,
        [in_vmem] * len(outs),
        [in_vmem] * (len(flat) + 1),
        flops=4 * total * size * width,
        moved=2 * total * (size + width),
    )(*flat, split_right)
    return got[:-2], got[-2], got[-1]


def next_coeff_kernel(messages, both_ref, split_ref, *outs):
    store_coefficients(split_ref, both_ref[...], messages, outs[0].shape[1], outs)


def next_coefficients(both, split_right, messages, rank):
    size, width = both.shape[0], both.shape[1] // 2
    total = split_right.shape[0]
    return call(
        functools.partial(next_coeff_kernel, messages),
        [struct(message.width, rank, width) for message in messages],
        [in_vmem] * len(messages),
        [in_vmem] * 2,
        flops=4 * total * size * width,
        moved=2 * total * (size + width),
    )(both, split_right)


def times_diag(diag_ref, cols_ref):
    both = side_by_side(cols_ref[...])
    hi, lo = split(diag_ref[...])
    return fold(dot(hi, both) + dot(lo, both))


def relay_kernel(count, *refs):
    for source, target in zip(refs[:count], refs[-count:]):
        target[...] = source[...]


def relay(values, after):
    return call(
        functools.partial(relay_kernel, len(values)),
        [struct(*value.shape) for value in values],
        [in_vmem] * len(values),
        [in_vmem] * len(values) + [in_any] * len(after),
        moved=8 * sum(value.size for value in values),
    )(*values, *after)


def diag_kernel(diag_ref, cols_ref, out_ref):
    out_ref[...] = times_diag(diag_ref, cols_ref)


def diagonal(diag_tile, cols):
    size, width = cols.shape
    return call(
        diag_kernel,
        struct(size, width),
        in_vmem,
        [in_vmem, in_vmem],
        flops=8 * size * size * width,
        moved=4 * size * (size + 2 * width),
    )(diag_tile, cols)


def weight_rows(size):
    groups = lax.axis_size("kern")
    me = lax.axis_index("kern")
    if groups != 4:
        return [(me * groups + b, slice(0, size)) for b in range(groups)]
    rows_of = []
    odd = lax.axis_index("tile") & 1
    one, two = me ^ (1 + odd), me ^ (2 - odd)
    for half, (first, second) in enumerate(((one, two), (two, one))):
        lanes = slice(half * (size // 2), (half + 1) * (size // 2))
        for a in (me, second):
            for b in (me, first):
                rows_of.append((a * groups + b, lanes))
    return rows_of


def prepare_kernel(
    halves, diag_hbm, cols_hbm, left_hbm, table_ref, index_ref,
    diag_out, left_out, weights_ref, diag_ref, cols_ref, left_ref, full_ref, sems,
):
    copies = []
    for at, (source, target) in enumerate(
        ((diag_hbm, diag_ref), (cols_hbm, cols_ref), (left_hbm, left_ref))
    ):
        copies.append(pltpu.make_async_copy(source, target, sems.at[at]))
        copies[-1].start()
    entries = table_ref.shape[1]
    size = index_ref.shape[1]
    hot = (lax.broadcasted_iota(jnp.int32, (entries, size), 0) == index_ref[...]).astype(f32)
    full_ref[...] = jnp.dot(
        table_ref[...], hot, precision=lax.Precision.HIGHEST, preferred_element_type=f32
    )
    width = weights_ref.shape[2]
    for at, (row, lanes) in enumerate(weight_rows(size)):
        piece = full_ref[pl.ds(row, 1), lanes]
        weights_ref[at] = jnp.broadcast_to(piece, (width, piece.shape[1])).T
    copies[0].wait()
    copies[1].wait()
    diag_out[...] = times_diag(diag_ref, cols_ref)
    copies[2].wait()
    total = left_ref.shape[0]
    step = 128 if total % 128 == 0 else total
    part = size // halves
    for at in range(0, total, step):
        span = slice(at, at + step)
        hi, lo = split(left_ref[span].T)
        for half in range(halves):
            base = 2 * half * part
            rows_of = slice(half * part, (half + 1) * part)
            left_out[base : base + part, span] = hi[rows_of]
            left_out[base + part : base + 2 * part, span] = lo[rows_of]


def prepare(diag_tile, cols, left_rows, table, index, halves):
    size, width = cols.shape
    total = left_rows.shape[0]
    weights = weight_rows(size)
    part = weights[0][1].stop
    return call(
        functools.partial(prepare_kernel, halves),
        [
            struct(size, width),
            struct(2 * size, total, dtype=bf16),
            struct(len(weights), part, width),
        ],
        [in_vmem] * 3,
        [in_hbm] * 3 + [in_vmem] * 2,
        [
            pltpu.VMEM(diag_tile.shape, f32),
            pltpu.VMEM(cols.shape, f32),
            pltpu.VMEM(left_rows.shape, f32),
            pltpu.VMEM((table.shape[0], size), f32),
            pltpu.SemaphoreType.DMA((3,)),
        ],
        flops=8 * size * size * width,
        moved=8 * total * size + 4 * size * (size + 2 * width),
    )(to_hbm(diag_tile), to_hbm(cols), to_hbm(left_rows), table, index)


def row_kernel(messages, halves, final, offs_ref, ranks_ref, *refs):
    gots = refs[: len(messages)]
    left_ref, diag_ref = refs[len(messages) : len(messages) + 2]
    outs = refs[len(messages) + 2 :]
    if final:
        outs, (picked, term_of, stage, sems) = outs[:-4], outs[-4:]
    else:
        outs, (picked, term_of) = outs[:-2], outs[-2:]
    terms = offs_ref.shape[1]
    rank, width = gots[0].shape[1:]
    slots = term_of.shape[0]
    reach = slots // 2
    for slot in range(slots):
        term_of[slot] = terms
    for k in range(terms):
        offset = offs_ref[0, k]
        term_of[jnp.where(offset < 0, offset + reach, offset + reach - 1)] = k
    line = lax.broadcasted_iota(jnp.int32, (rank, width), 0)

    def pick(got, w, term):
        last = ranks_ref[0, jnp.minimum(term, terms - 1)]
        kept = jnp.where(line < last, got[w], 0.0)
        picked[pl.ds(pl.multiple_of(term * rank, rank), rank)] = kept

    for got, message in zip(gots, messages):
        for w, slot in enumerate(message.slots):
            if message.odd_slots is not None:
                slot = jnp.where((lax.axis_index("tile") & 1) == 1, slot, message.odd_slots[w])
            pick(got, w, term_of[slot])
    both = side_by_side(picked[: terms * rank])
    part = diag_ref.shape[0] // halves
    sent = []
    got = fold(dot(left_ref[...], both))
    for half in range(halves):
        rows_of = pl.ds(half * part, part)
        base = 2 * half * part
        total = got[base : base + part] + got[base + part : base + 2 * part] + diag_ref[rows_of]
        if final:
            stage[rows_of] = total
            sent.append(
                pltpu.make_async_copy(stage.at[rows_of], outs[0].at[rows_of], sems.at[half])
            )
            sent[-1].start()
        else:
            outs[half][...] = total
    for copy in sent:
        copy.wait()


def rows(offsets, ranks, gots, messages, left_split, diag_part, slots, halves, final):
    size, width = diag_part.shape
    total = left_split.shape[1]
    rank = gots[0].shape[1]
    scratch = [pltpu.VMEM((total + rank, width), f32), pltpu.SMEM((slots,), jnp.int32)]
    if final:
        scratch += [pltpu.VMEM((size, width), f32), pltpu.SemaphoreType.DMA((halves,))]
    return call(
        functools.partial(row_kernel, messages, halves, final),
        pltpu.HBM((size, width), f32) if final else [struct(size // halves, width)] * halves,
        in_hbm if final else [in_vmem] * halves,
        [in_smem, in_smem] + [in_vmem] * (len(messages) + 2),
        scratch,
        flops=8 * total * size * width,
        moved=4 * total * (size + width),
    )(offsets, ranks, *gots, left_split, diag_part)


def send(value, message):
    return lax.ppermute(value, "tile", message.pairs)


def send_all(one, two, coeffs, more, waited, beside):
    gots = []
    for value, message in zip(coeffs, one):
        if message.odd_slots is not None and message.across:
            value = relay([value], [gots[waited], more[0], beside])[0]
        gots.append(send(value, message))
    return gots + [send(value, message) for value, message in zip(more, two)]


def local(
    diag_tiles,
    left_factors,
    right_factors,
    tile_offsets,
    tile_ranks,
    mixing,
    block_index,
    rhs_field,
):
    diag_tile = diag_tiles[0, 0]
    right_tile = right_factors[0, 0]
    offsets = tile_offsets[0]
    ranks = tile_ranks[0]
    slots, rank, size = right_tile.shape
    halves = 2 if size % 32 == 0 else 1
    left_rows = left_factors.reshape(-1, size)
    groups = lax.axis_size("kern")
    table = mixing.reshape(mixing.shape[0], groups * groups).T
    index = block_index[None]
    cols = rhs_field[0]

    one, two = message_sets_of(lax.axis_size("tile"), slots)
    messages = one + two
    coeffs, split_one, both, rest = first_coefficients(cols, right_tile, one, two)
    more, split_two = rest_coefficients(both, rest, two)
    diag_part, left_split, weights = prepare(diag_tile, cols, left_rows, table, index, halves)
    gots = send_all(one, two, coeffs, more, -1, diag_part)
    first = rows(offsets, ranks, gots, messages, left_split, diag_part, slots, halves, False)
    mixed = mix(first, weights)
    coeffs, cols, both = mixed_coefficients(mixed, split_one, one, rank)
    more = next_coefficients(both, split_two, two, rank)
    diag_part = diagonal(diag_tile, cols)
    gots = send_all(one, two, coeffs, more, 0, diag_part)
    return rows(offsets, ranks, gots, messages, left_split, diag_part, slots, halves, True)[None]


def solution(mesh):
    in_specs = (
        P("kern", "tile", None, None),
        P("kern", "tile", None, None, None),
        P("kern", "tile", None, None, None),
        P("kern", "tile", None),
        P("kern", "tile", None),
        P(),
        P("tile"),
        P("kern", "tile", None),
    )
    out_specs = P("kern", "tile", None)
    return jax.shard_map(local, mesh=mesh, in_specs=in_specs, out_specs=out_specs, check_vma=False)
```

```python
import functools

import jax
import jax.numpy as jnp
from jax import lax
from jax.experimental import pallas as pl
from jax.experimental.pallas import tpu as pltpu
from jax.sharding import PartitionSpec as P

f32 = jnp.float32
bf16 = jnp.bfloat16
VMEM_BYTES = 24 * 1024 * 1024
in_vmem = pl.BlockSpec(memory_space=pltpu.VMEM)
in_smem = pl.BlockSpec(memory_space=pltpu.SMEM)
in_hbm = pl.BlockSpec(memory_space=pltpu.HBM)
in_any = pl.BlockSpec(memory_space=pl.ANY)


def to_hbm(value):
    return pltpu.with_memory_space_constraint(value, pltpu.HBM)


def struct(*shape, dtype=f32):
    return jax.ShapeDtypeStruct(shape, dtype)


def split(value):
    hi = value.astype(bf16)
    return hi, (value - hi.astype(f32)).astype(bf16)


def side_by_side(value):
    return jnp.concatenate(split(value), axis=1)


def dot(left, right):
    return jnp.dot(left, right, preferred_element_type=f32)


def fold(value):
    width = value.shape[1] // 2
    return value[:, :width] + value[:, width:]


def call(kernel, outs, out_specs, in_specs, scratch=(), flops=0, moved=0):
    return pl.pallas_call(
        kernel,
        out_shape=outs,
        in_specs=in_specs,
        out_specs=out_specs,
        scratch_shapes=list(scratch),
        compiler_params=pltpu.CompilerParams(vmem_limit_bytes=VMEM_BYTES),
        cost_estimate=pl.CostEstimate(flops=flops, bytes_accessed=moved, transcendentals=0),
    )


class Message:
    def __init__(self, pairs, slots, odd_slots=None):
        self.pairs = pairs
        self.slots = slots
        self.odd_slots = odd_slots
        self.width = len(slots)
        half = len(pairs) // 2
        self.across = self.width * sum((a < half) != (b < half) for a, b in pairs)


def message_sets_of(count, slots):
    reach = slots // 2
    groups = {}
    for slot in range(slots):
        offset = slot - reach if slot < reach else slot - reach + 1
        groups.setdefault(offset % count, []).append(slot)
    messages = []
    below, above = reach - 1, reach
    if groups.get(1) == [above] and groups.get(count - 1) == [below] and count % 2 == 0:
        del groups[1], groups[count - 1]
        for turn, (even, odd) in enumerate(((below, above), (above, below))):
            pairs = [(at, (at + (1, -1)[(at + turn) % 2]) % count) for at in range(count)]
            messages.append(Message(pairs, [even], [odd]))
    for ahead, group in groups.items():
        messages.append(Message([(at, (at - ahead) % count) for at in range(count)], group))
    messages.sort(key=lambda message: -message.across)
    first = messages[:1] + [m for m in messages[:0:-1] if m.odd_slots is not None]
    return [first, [message for message in messages if message not in first]]


def slots_of(messages):
    return sorted({slot for m in messages for slot in m.slots + (m.odd_slots or [])})


def copy_runs(slots, source, target, sems):
    copies, at = [], 0
    while at < len(slots):
        count = 1
        while at + count < len(slots) and slots[at + count] == slots[at] + count:
            count += 1
        copies.append(
            pltpu.make_async_copy(
                source.at[pl.ds(slots[at], count)], target.at[pl.ds(at, count)], sems.at[at]
            )
        )
        copies[-1].start()
        at += count
    return copies


def store_coefficients(split_ref, both, messages, rank, outs):
    slots = slots_of(messages)
    size = len(slots) * rank
    got = fold(dot(split_ref[...], both))
    got = got[:size] + got[size:]

    def piece(slot):
        row = slots.index(slot) * rank
        return got[row : row + rank]

    odd = jnp.full((rank, got.shape[1]), lax.axis_index("tile") & 1, jnp.int32) == 1
    for message, out in zip(messages, outs):
        for w, slot in enumerate(message.slots):
            value = piece(slot)
            if message.odd_slots is not None:
                value = jnp.where(odd, piece(message.odd_slots[w]), value)
            out[w] = value


def split_rows(right, split_ref):
    count, rank, size = right.shape
    rows = count * rank
    hi, lo = split(right[...].reshape(rows, size))
    split_ref[:rows] = hi
    split_ref[rows:] = lo


def first_coeff_kernel(messages, others, cols_ref, right_ref, *refs):
    outs, refs = refs[: len(messages)], refs[len(messages) :]
    split_ref, both_ref, rest_ref, cols, right, cols_sem, sems, rest_sems = refs
    cols_copy = pltpu.make_async_copy(cols_ref, cols, cols_sem)
    cols_copy.start()
    copies = copy_runs(slots_of(messages), right_ref, right, sems)
    rest = copy_runs(slots_of(others), right_ref, rest_ref, rest_sems)
    cols_copy.wait()
    both_ref[...] = side_by_side(cols[...])
    for copy in copies:
        copy.wait()
    split_rows(right, split_ref)
    store_coefficients(split_ref, both_ref[...], messages, right.shape[1], outs)
    for copy in rest:
        copy.wait()


def first_coefficients(cols, right_tile, messages, others):
    _, rank, size = right_tile.shape
    width = cols.shape[1]
    count, rest = len(slots_of(messages)), len(slots_of(others))
    outs = [struct(message.width, rank, width) for message in messages]
    outs += [
        struct(2 * count * rank, size, dtype=bf16),
        struct(size, 2 * width, dtype=bf16),
        struct(rest, rank, size),
    ]
    got = call(
        functools.partial(first_coeff_kernel, messages, others),
        outs,
        [in_vmem] * len(outs),
        [in_hbm, in_hbm],
        [
            pltpu.VMEM(cols.shape, f32),
            pltpu.VMEM((count, rank, size), f32),
            pltpu.SemaphoreType.DMA,
            pltpu.SemaphoreType.DMA((count,)),
            pltpu.SemaphoreType.DMA((rest,)),
        ],
        flops=8 * count * rank * size * width,
        moved=4 * (count + rest) * rank * size,
    )(to_hbm(cols), to_hbm(right_tile))
    return got[:-3], got[-3], got[-2], got[-1]


def rest_coeff_kernel(messages, both_ref, right_ref, *refs):
    outs, split_ref = refs[:-1], refs[-1]
    split_rows(right_ref, split_ref)
    store_coefficients(split_ref, both_ref[...], messages, right_ref.shape[1], outs)


def rest_coefficients(both, right, messages):
    count, rank, size = right.shape
    width = both.shape[1] // 2
    outs = [struct(message.width, rank, width) for message in messages]
    outs.append(struct(2 * count * rank, size, dtype=bf16))
    got = call(
        functools.partial(rest_coeff_kernel, messages),
        outs,
        [in_vmem] * len(outs),
        [in_vmem] * 2,
        flops=8 * count * rank * size * width,
        moved=8 * count * rank * size,
    )(both, right)
    return got[:-1], got[-1]


def halve_kernel(base, own_ref, got_ref, weights_ref, keep_ref, send_ref):
    own, got = own_ref[...], got_ref[...]
    keep_ref[...] = own * weights_ref[base] + got * weights_ref[base + 1]
    send_ref[...] = own * weights_ref[base + 2] + got * weights_ref[base + 3]


def halve(own, got, weights, half):
    part, width = own.shape
    return call(
        functools.partial(halve_kernel, 4 * half),
        [struct(part, width)] * 2,
        [in_vmem] * 2,
        [in_vmem] * 3,
        flops=6 * part * width,
        moved=32 * part * width,
    )(own, got, weights)


def mix(first, weights):
    groups = lax.axis_size("kern")
    if groups != 4:
        fields = [lax.all_gather(part, "kern") for part in first]
        mixed = jnp.sum(jnp.concatenate(fields, axis=1) * weights, axis=0)
        return [(mixed, jnp.zeros_like(mixed))]
    count = lax.axis_size("tile")
    steps = ([], [])
    for group in range(groups):
        for tile in range(count):
            for turn, pairs in enumerate(steps):
                dest = group ^ (1 + (turn + tile) % 2)
                pairs.append((group * count + tile, dest * count + tile))
    axes = ("kern", "tile")
    came = [lax.ppermute(part, axes, pairs) for part, pairs in zip(first, steps)]
    sums = [
        halve(part, got, weights, half)
        for half, (part, got) in enumerate(zip(first, came))
    ]
    return [
        (keep, lax.ppermute(send, axes, pairs)) for (keep, send), pairs in zip(sums, steps[::-1])
    ]


def mixed_coeff_kernel(messages, terms, *refs):
    fields, split_ref = refs[:terms], refs[terms]
    outs, cols_ref, both_ref = refs[terms + 1 : -2], refs[-2], refs[-1]
    part = fields[0].shape[0]
    for at in range(0, terms, 2):
        rows_of = pl.ds(at // 2 * part, part)
        total = fields[at][...] + fields[at + 1][...]
        cols_ref[rows_of] = total
        both_ref[rows_of] = side_by_side(total)
    store_coefficients(split_ref, both_ref[...], messages, outs[0].shape[1], outs)


def mixed_coefficients(mixed, split_right, messages, rank):
    flat = [term for pair in mixed for term in pair]
    part, width = flat[0].shape
    size = part * len(mixed)
    total = split_right.shape[0]
    outs = [struct(message.width, rank, width) for message in messages]
    outs += [struct(size, width), struct(size, 2 * width, dtype=bf16)]
    got = call(
        functools.partial(mixed_coeff_kernel, messages, len(flat)),
        outs,
        [in_vmem] * len(outs),
        [in_vmem] * (len(flat) + 1),
        flops=4 * total * size * width,
        moved=2 * total * (size + width),
    )(*flat, split_right)
    return got[:-2], got[-2], got[-1]


def next_coeff_kernel(messages, both_ref, split_ref, *outs):
    store_coefficients(split_ref, both_ref[...], messages, outs[0].shape[1], outs)


def next_coefficients(both, split_right, messages, rank):
    size, width = both.shape[0], both.shape[1] // 2
    total = split_right.shape[0]
    return call(
        functools.partial(next_coeff_kernel, messages),
        [struct(message.width, rank, width) for message in messages],
        [in_vmem] * len(messages),
        [in_vmem] * 2,
        flops=4 * total * size * width,
        moved=2 * total * (size + width),
    )(both, split_right)


def times_diag(diag_ref, cols_ref):
    both = side_by_side(cols_ref[...])
    hi, lo = split(diag_ref[...])
    return fold(dot(hi, both) + dot(lo, both))


def relay_kernel(count, *refs):
    for source, target in zip(refs[:count], refs[-count:]):
        target[...] = source[...]


def relay(values, after):
    return call(
        functools.partial(relay_kernel, len(values)),
        [struct(*value.shape) for value in values],
        [in_vmem] * len(values),
        [in_vmem] * len(values) + [in_any] * len(after),
        moved=8 * sum(value.size for value in values),
    )(*values, *after)


def diag_kernel(diag_ref, cols_ref, out_ref):
    out_ref[...] = times_diag(diag_ref, cols_ref)


def diagonal(diag_tile, cols):
    size, width = cols.shape
    return call(
        diag_kernel,
        struct(size, width),
        in_vmem,
        [in_vmem, in_vmem],
        flops=8 * size * size * width,
        moved=4 * size * (size + 2 * width),
    )(diag_tile, cols)


def weight_rows(size):
    groups = lax.axis_size("kern")
    me = lax.axis_index("kern")
    if groups != 4:
        return [(me * groups + b, slice(0, size)) for b in range(groups)]
    rows_of = []
    odd = lax.axis_index("tile") & 1
    one, two = me ^ (1 + odd), me ^ (2 - odd)
    for half, (first, second) in enumerate(((one, two), (two, one))):
        lanes = slice(half * (size // 2), (half + 1) * (size // 2))
        for a in (me, second):
            for b in (me, first):
                rows_of.append((a * groups + b, lanes))
    return rows_of


def prepare_kernel(
    halves, diag_hbm, cols_hbm, left_hbm, table_ref, index_ref,
    diag_out, left_out, weights_ref, diag_ref, cols_ref, left_ref, full_ref, sems,
):
    copies = []
    for at, (source, target) in enumerate(
        ((diag_hbm, diag_ref), (cols_hbm, cols_ref), (left_hbm, left_ref))
    ):
        copies.append(pltpu.make_async_copy(source, target, sems.at[at]))
        copies[-1].start()
    entries = table_ref.shape[1]
    size = index_ref.shape[1]
    hot = (lax.broadcasted_iota(jnp.int32, (entries, size), 0) == index_ref[...]).astype(f32)
    full_ref[...] = jnp.dot(
        table_ref[...], hot, precision=lax.Precision.HIGHEST, preferred_element_type=f32
    )
    width = weights_ref.shape[2]
    for at, (row, lanes) in enumerate(weight_rows(size)):
        piece = full_ref[pl.ds(row, 1), lanes]
        weights_ref[at] = jnp.broadcast_to(piece, (width, piece.shape[1])).T
    copies[0].wait()
    copies[1].wait()
    diag_out[...] = times_diag(diag_ref, cols_ref)
    copies[2].wait()
    total = left_ref.shape[0]
    step = 128 if total % 128 == 0 else total
    part = size // halves
    for at in range(0, total, step):
        span = slice(at, at + step)
        hi, lo = split(left_ref[span].T)
        for half in range(halves):
            base = 2 * half * part
            rows_of = slice(half * part, (half + 1) * part)
            left_out[base : base + part, span] = hi[rows_of]
            left_out[base + part : base + 2 * part, span] = lo[rows_of]


def prepare(diag_tile, cols, left_rows, table, index, halves):
    size, width = cols.shape
    total = left_rows.shape[0]
    weights = weight_rows(size)
    part = weights[0][1].stop
    return call(
        functools.partial(prepare_kernel, halves),
        [
            struct(size, width),
            struct(2 * size, total, dtype=bf16),
            struct(len(weights), part, width),
        ],
        [in_vmem] * 3,
        [in_hbm] * 3 + [in_vmem] * 2,
        [
            pltpu.VMEM(diag_tile.shape, f32),
            pltpu.VMEM(cols.shape, f32),
            pltpu.VMEM(left_rows.shape, f32),
            pltpu.VMEM((table.shape[0], size), f32),
            pltpu.SemaphoreType.DMA((3,)),
        ],
        flops=8 * size * size * width,
        moved=8 * total * size + 4 * size * (size + 2 * width),
    )(to_hbm(diag_tile), to_hbm(cols), to_hbm(left_rows), table, index)


def row_kernel(messages, halves, final, offs_ref, ranks_ref, *refs):
    gots = refs[: len(messages)]
    left_ref, diag_ref = refs[len(messages) : len(messages) + 2]
    outs = refs[len(messages) + 2 :]
    if final:
        outs, (picked, term_of, stage, sems) = outs[:-4], outs[-4:]
    else:
        outs, (picked, term_of) = outs[:-2], outs[-2:]
    terms = offs_ref.shape[1]
    rank, width = gots[0].shape[1:]
    slots = term_of.shape[0]
    reach = slots // 2
    for slot in range(slots):
        term_of[slot] = terms
    for k in range(terms):
        offset = offs_ref[0, k]
        term_of[jnp.where(offset < 0, offset + reach, offset + reach - 1)] = k
    line = lax.broadcasted_iota(jnp.int32, (rank, width), 0)

    def pick(got, w, term):
        last = ranks_ref[0, jnp.minimum(term, terms - 1)]
        kept = jnp.where(line < last, got[w], 0.0)
        picked[pl.ds(pl.multiple_of(term * rank, rank), rank)] = kept

    for got, message in zip(gots, messages):
        for w, slot in enumerate(message.slots):
            if message.odd_slots is not None:
                slot = jnp.where((lax.axis_index("tile") & 1) == 1, slot, message.odd_slots[w])
            pick(got, w, term_of[slot])
    both = side_by_side(picked[: terms * rank])
    part = diag_ref.shape[0] // halves
    sent = []
    got = fold(dot(left_ref[...], both))
    for half in range(halves):
        rows_of = pl.ds(half * part, part)
        base = 2 * half * part
        total = got[base : base + part] + got[base + part : base + 2 * part] + diag_ref[rows_of]
        if final:
            stage[rows_of] = total
            sent.append(
                pltpu.make_async_copy(stage.at[rows_of], outs[0].at[rows_of], sems.at[half])
            )
            sent[-1].start()
        else:
            outs[half][...] = total
    for copy in sent:
        copy.wait()


def rows(offsets, ranks, gots, messages, left_split, diag_part, slots, halves, final):
    size, width = diag_part.shape
    total = left_split.shape[1]
    rank = gots[0].shape[1]
    scratch = [pltpu.VMEM((total + rank, width), f32), pltpu.SMEM((slots,), jnp.int32)]
    if final:
        scratch += [pltpu.VMEM((size, width), f32), pltpu.SemaphoreType.DMA((halves,))]
    return call(
        functools.partial(row_kernel, messages, halves, final),
        pltpu.HBM((size, width), f32) if final else [struct(size // halves, width)] * halves,
        in_hbm if final else [in_vmem] * halves,
        [in_smem, in_smem] + [in_vmem] * (len(messages) + 2),
        scratch,
        flops=8 * total * size * width,
        moved=4 * total * (size + width),
    )(offsets, ranks, *gots, left_split, diag_part)


def send(value, message):
    return lax.ppermute(value, "tile", message.pairs)


def send_all(one, two, coeffs, more, beside):
    gots = []
    for value, message in zip(coeffs, one):
        if message.odd_slots is not None and message.across:
            value = relay([value], [gots[-1], more[0], beside])[0]
        gots.append(send(value, message))
    return gots + [send(value, message) for value, message in zip(more, two)]


def local(
    diag_tiles,
    left_factors,
    right_factors,
    tile_offsets,
    tile_ranks,
    mixing,
    block_index,
    rhs_field,
):
    diag_tile = diag_tiles[0, 0]
    right_tile = right_factors[0, 0]
    offsets = tile_offsets[0]
    ranks = tile_ranks[0]
    slots, rank, size = right_tile.shape
    halves = 2 if size % 32 == 0 else 1
    left_rows = left_factors.reshape(-1, size)
    groups = lax.axis_size("kern")
    table = mixing.reshape(mixing.shape[0], groups * groups).T
    index = block_index[None]
    cols = rhs_field[0]

    one, two = message_sets_of(lax.axis_size("tile"), slots)
    messages = one + two
    coeffs, split_one, both, rest = first_coefficients(cols, right_tile, one, two)
    more, split_two = rest_coefficients(both, rest, two)
    diag_part, left_split, weights = prepare(diag_tile, cols, left_rows, table, index, halves)
    gots = send_all(one, two, coeffs, more, diag_part)
    first = rows(offsets, ranks, gots, messages, left_split, diag_part, slots, halves, False)
    mixed = mix(first, weights)
    coeffs, cols, both = mixed_coefficients(mixed, split_one, one, rank)
    more = next_coefficients(both, split_two, two, rank)
    diag_part = diagonal(diag_tile, cols)
    gots = send_all(one, two, coeffs, more, diag_part)
    return rows(offsets, ranks, gots, messages, left_split, diag_part, slots, halves, True)[None]


def solution(mesh):
    in_specs = (
        P("kern", "tile", None, None),
        P("kern", "tile", None, None, None),
        P("kern", "tile", None, None, None),
        P("kern", "tile", None),
        P("kern", "tile", None),
        P(),
        P("tile"),
        P("kern", "tile", None),
    )
    out_specs = P("kern", "tile", None)
    return jax.shard_map(local, mesh=mesh, in_specs=in_specs, out_specs=out_specs, check_vma=False)
```

```python
import functools

import jax
import jax.numpy as jnp
from jax import lax
from jax.experimental import pallas as pl
from jax.experimental.pallas import tpu as pltpu
from jax.sharding import PartitionSpec as P

f32 = jnp.float32
bf16 = jnp.bfloat16
VMEM_BYTES = 24 * 1024 * 1024
in_vmem = pl.BlockSpec(memory_space=pltpu.VMEM)
in_smem = pl.BlockSpec(memory_space=pltpu.SMEM)
in_hbm = pl.BlockSpec(memory_space=pltpu.HBM)
in_any = pl.BlockSpec(memory_space=pl.ANY)


def to_hbm(value):
    return pltpu.with_memory_space_constraint(value, pltpu.HBM)


def struct(*shape, dtype=f32):
    return jax.ShapeDtypeStruct(shape, dtype)


def split(value):
    hi = value.astype(bf16)
    return hi, (value - hi.astype(f32)).astype(bf16)


def side_by_side(value):
    return jnp.concatenate(split(value), axis=1)


def dot(left, right):
    return jnp.dot(left, right, preferred_element_type=f32)


def fold(value):
    width = value.shape[1] // 2
    return value[:, :width] + value[:, width:]


def call(kernel, outs, out_specs, in_specs, scratch=(), flops=0, moved=0):
    return pl.pallas_call(
        kernel,
        out_shape=outs,
        in_specs=in_specs,
        out_specs=out_specs,
        scratch_shapes=list(scratch),
        compiler_params=pltpu.CompilerParams(vmem_limit_bytes=VMEM_BYTES),
        cost_estimate=pl.CostEstimate(flops=flops, bytes_accessed=moved, transcendentals=0),
    )


class Message:
    def __init__(self, pairs, slots, odd_slots=None):
        self.pairs = pairs
        self.slots = slots
        self.odd_slots = odd_slots
        self.width = len(slots)
        half = len(pairs) // 2
        self.across = self.width * sum((a < half) != (b < half) for a, b in pairs)


def message_sets_of(count, slots):
    reach = slots // 2
    groups = {}
    for slot in range(slots):
        offset = slot - reach if slot < reach else slot - reach + 1
        groups.setdefault(offset % count, []).append(slot)
    messages = []
    below, above = reach - 1, reach
    if groups.get(1) == [above] and groups.get(count - 1) == [below] and count % 2 == 0:
        del groups[1], groups[count - 1]
        for turn, (even, odd) in enumerate(((below, above), (above, below))):
            pairs = [(at, (at + (1, -1)[(at + turn) % 2]) % count) for at in range(count)]
            messages.append(Message(pairs, [even], [odd]))
    for ahead, group in groups.items():
        messages.append(Message([(at, (at - ahead) % count) for at in range(count)], group))
    messages.sort(key=lambda message: -message.across)
    first = messages[:1] + [m for m in messages[:0:-1] if m.odd_slots is not None]
    rest = [message for message in messages if message not in first]
    return [first, rest[-1:] + rest[:-1]]


def slots_of(messages):
    return sorted({slot for m in messages for slot in m.slots + (m.odd_slots or [])})


def copy_runs(slots, source, target, sems):
    copies, at = [], 0
    while at < len(slots):
        count = 1
        while at + count < len(slots) and slots[at + count] == slots[at] + count:
            count += 1
        copies.append(
            pltpu.make_async_copy(
                source.at[pl.ds(slots[at], count)], target.at[pl.ds(at, count)], sems.at[at]
            )
        )
        copies[-1].start()
        at += count
    return copies


def store_coefficients(split_ref, both, messages, rank, outs):
    slots = slots_of(messages)
    size = len(slots) * rank
    got = fold(dot(split_ref[...], both))
    got = got[:size] + got[size:]

    def piece(slot):
        row = slots.index(slot) * rank
        return got[row : row + rank]

    odd = jnp.full((rank, got.shape[1]), lax.axis_index("tile") & 1, jnp.int32) == 1
    for message, out in zip(messages, outs):
        for w, slot in enumerate(message.slots):
            value = piece(slot)
            if message.odd_slots is not None:
                value = jnp.where(odd, piece(message.odd_slots[w]), value)
            out[w] = value


def split_rows(right, split_ref):
    count, rank, size = right.shape
    rows = count * rank
    hi, lo = split(right[...].reshape(rows, size))
    split_ref[:rows] = hi
    split_ref[rows:] = lo


def first_coeff_kernel(messages, others, cols_ref, right_ref, *refs):
    outs, refs = refs[: len(messages)], refs[len(messages) :]
    split_ref, both_ref, rest_ref, cols, right, cols_sem, sems, rest_sems = refs
    cols_copy = pltpu.make_async_copy(cols_ref, cols, cols_sem)
    cols_copy.start()
    copies = copy_runs(slots_of(messages), right_ref, right, sems)
    rest = copy_runs(slots_of(others), right_ref, rest_ref, rest_sems)
    cols_copy.wait()
    both_ref[...] = side_by_side(cols[...])
    for copy in copies:
        copy.wait()
    split_rows(right, split_ref)
    store_coefficients(split_ref, both_ref[...], messages, right.shape[1], outs)
    for copy in rest:
        copy.wait()


def first_coefficients(cols, right_tile, messages, others):
    _, rank, size = right_tile.shape
    width = cols.shape[1]
    count, rest = len(slots_of(messages)), len(slots_of(others))
    outs = [struct(message.width, rank, width) for message in messages]
    outs += [
        struct(2 * count * rank, size, dtype=bf16),
        struct(size, 2 * width, dtype=bf16),
        struct(rest, rank, size),
    ]
    got = call(
        functools.partial(first_coeff_kernel, messages, others),
        outs,
        [in_vmem] * len(outs),
        [in_hbm, in_hbm],
        [
            pltpu.VMEM(cols.shape, f32),
            pltpu.VMEM((count, rank, size), f32),
            pltpu.SemaphoreType.DMA,
            pltpu.SemaphoreType.DMA((count,)),
            pltpu.SemaphoreType.DMA((rest,)),
        ],
        flops=8 * count * rank * size * width,
        moved=4 * (count + rest) * rank * size,
    )(to_hbm(cols), to_hbm(right_tile))
    return got[:-3], got[-3], got[-2], got[-1]


def rest_coeff_kernel(messages, both_ref, right_ref, *refs):
    outs, split_ref = refs[:-1], refs[-1]
    split_rows(right_ref, split_ref)
    store_coefficients(split_ref, both_ref[...], messages, right_ref.shape[1], outs)


def rest_coefficients(both, right, messages):
    count, rank, size = right.shape
    width = both.shape[1] // 2
    outs = [struct(message.width, rank, width) for message in messages]
    outs.append(struct(2 * count * rank, size, dtype=bf16))
    got = call(
        functools.partial(rest_coeff_kernel, messages),
        outs,
        [in_vmem] * len(outs),
        [in_vmem] * 2,
        flops=8 * count * rank * size * width,
        moved=8 * count * rank * size,
    )(both, right)
    return got[:-1], got[-1]


def halve_kernel(base, own_ref, got_ref, weights_ref, keep_ref, send_ref):
    own, got = own_ref[...], got_ref[...]
    keep_ref[...] = own * weights_ref[base] + got * weights_ref[base + 1]
    send_ref[...] = own * weights_ref[base + 2] + got * weights_ref[base + 3]


def halve(own, got, weights, half):
    part, width = own.shape
    return call(
        functools.partial(halve_kernel, 4 * half),
        [struct(part, width)] * 2,
        [in_vmem] * 2,
        [in_vmem] * 3,
        flops=6 * part * width,
        moved=32 * part * width,
    )(own, got, weights)


def mix(first, weights):
    groups = lax.axis_size("kern")
    if groups != 4:
        fields = [lax.all_gather(part, "kern") for part in first]
        mixed = jnp.sum(jnp.concatenate(fields, axis=1) * weights, axis=0)
        return [(mixed, jnp.zeros_like(mixed))]
    count = lax.axis_size("tile")
    steps = ([], [])
    for group in range(groups):
        for tile in range(count):
            for turn, pairs in enumerate(steps):
                dest = group ^ (1 + (turn + tile) % 2)
                pairs.append((group * count + tile, dest * count + tile))
    axes = ("kern", "tile")
    came = [lax.ppermute(part, axes, pairs) for part, pairs in zip(first, steps)]
    sums = [
        halve(part, got, weights, half)
        for half, (part, got) in enumerate(zip(first, came))
    ]
    return [
        (keep, lax.ppermute(send, axes, pairs)) for (keep, send), pairs in zip(sums, steps[::-1])
    ]


def mixed_coeff_kernel(messages, terms, *refs):
    fields, split_ref = refs[:terms], refs[terms]
    outs, cols_ref, both_ref = refs[terms + 1 : -2], refs[-2], refs[-1]
    part = fields[0].shape[0]
    for at in range(0, terms, 2):
        rows_of = pl.ds(at // 2 * part, part)
        total = fields[at][...] + fields[at + 1][...]
        cols_ref[rows_of] = total
        both_ref[rows_of] = side_by_side(total)
    store_coefficients(split_ref, both_ref[...], messages, outs[0].shape[1], outs)


def mixed_coefficients(mixed, split_right, messages, rank):
    flat = [term for pair in mixed for term in pair]
    part, width = flat[0].shape
    size = part * len(mixed)
    total = split_right.shape[0]
    outs = [struct(message.width, rank, width) for message in messages]
    outs += [struct(size, width), struct(size, 2 * width, dtype=bf16)]
    got = call(
        functools.partial(mixed_coeff_kernel, messages, len(flat)),
        outs,
        [in_vmem] * len(outs),
        [in_vmem] * (len(flat) + 1),
        flops=4 * total * size * width,
        moved=2 * total * (size + width),
    )(*flat, split_right)
    return got[:-2], got[-2], got[-1]


def next_coeff_kernel(messages, both_ref, split_ref, *outs):
    store_coefficients(split_ref, both_ref[...], messages, outs[0].shape[1], outs)


def next_coefficients(both, split_right, messages, rank):
    size, width = both.shape[0], both.shape[1] // 2
    total = split_right.shape[0]
    return call(
        functools.partial(next_coeff_kernel, messages),
        [struct(message.width, rank, width) for message in messages],
        [in_vmem] * len(messages),
        [in_vmem] * 2,
        flops=4 * total * size * width,
        moved=2 * total * (size + width),
    )(both, split_right)


def times_diag(diag_ref, cols_ref):
    both = side_by_side(cols_ref[...])
    hi, lo = split(diag_ref[...])
    return fold(dot(hi, both) + dot(lo, both))


def relay_kernel(count, *refs):
    for source, target in zip(refs[:count], refs[-count:]):
        target[...] = source[...]


def relay(values, after):
    return call(
        functools.partial(relay_kernel, len(values)),
        [struct(*value.shape) for value in values],
        [in_vmem] * len(values),
        [in_vmem] * len(values) + [in_any] * len(after),
        moved=8 * sum(value.size for value in values),
    )(*values, *after)


def diag_kernel(diag_ref, cols_ref, out_ref):
    out_ref[...] = times_diag(diag_ref, cols_ref)


def diagonal(diag_tile, cols):
    size, width = cols.shape
    return call(
        diag_kernel,
        struct(size, width),
        in_vmem,
        [in_vmem, in_vmem],
        flops=8 * size * size * width,
        moved=4 * size * (size + 2 * width),
    )(diag_tile, cols)


def weight_rows(size):
    groups = lax.axis_size("kern")
    me = lax.axis_index("kern")
    if groups != 4:
        return [(me * groups + b, slice(0, size)) for b in range(groups)]
    rows_of = []
    odd = lax.axis_index("tile") & 1
    one, two = me ^ (1 + odd), me ^ (2 - odd)
    for half, (first, second) in enumerate(((one, two), (two, one))):
        lanes = slice(half * (size // 2), (half + 1) * (size // 2))
        for a in (me, second):
            for b in (me, first):
                rows_of.append((a * groups + b, lanes))
    return rows_of


def prepare_kernel(
    halves, diag_hbm, cols_hbm, left_hbm, table_ref, index_ref,
    diag_out, left_out, weights_ref, diag_ref, cols_ref, left_ref, full_ref, sems,
):
    copies = []
    for at, (source, target) in enumerate(
        ((diag_hbm, diag_ref), (cols_hbm, cols_ref), (left_hbm, left_ref))
    ):
        copies.append(pltpu.make_async_copy(source, target, sems.at[at]))
        copies[-1].start()
    entries = table_ref.shape[1]
    size = index_ref.shape[1]
    hot = (lax.broadcasted_iota(jnp.int32, (entries, size), 0) == index_ref[...]).astype(f32)
    full_ref[...] = jnp.dot(
        table_ref[...], hot, precision=lax.Precision.HIGHEST, preferred_element_type=f32
    )
    width = weights_ref.shape[2]
    for at, (row, lanes) in enumerate(weight_rows(size)):
        piece = full_ref[pl.ds(row, 1), lanes]
        weights_ref[at] = jnp.broadcast_to(piece, (width, piece.shape[1])).T
    copies[0].wait()
    copies[1].wait()
    diag_out[...] = times_diag(diag_ref, cols_ref)
    copies[2].wait()
    total = left_ref.shape[0]
    step = 128 if total % 128 == 0 else total
    part = size // halves
    for at in range(0, total, step):
        span = slice(at, at + step)
        hi, lo = split(left_ref[span].T)
        for half in range(halves):
            base = 2 * half * part
            rows_of = slice(half * part, (half + 1) * part)
            left_out[base : base + part, span] = hi[rows_of]
            left_out[base + part : base + 2 * part, span] = lo[rows_of]


def prepare(diag_tile, cols, left_rows, table, index, halves):
    size, width = cols.shape
    total = left_rows.shape[0]
    weights = weight_rows(size)
    part = weights[0][1].stop
    return call(
        functools.partial(prepare_kernel, halves),
        [
            struct(size, width),
            struct(2 * size, total, dtype=bf16),
            struct(len(weights), part, width),
        ],
        [in_vmem] * 3,
        [in_hbm] * 3 + [in_vmem] * 2,
        [
            pltpu.VMEM(diag_tile.shape, f32),
            pltpu.VMEM(cols.shape, f32),
            pltpu.VMEM(left_rows.shape, f32),
            pltpu.VMEM((table.shape[0], size), f32),
            pltpu.SemaphoreType.DMA((3,)),
        ],
        flops=8 * size * size * width,
        moved=8 * total * size + 4 * size * (size + 2 * width),
    )(to_hbm(diag_tile), to_hbm(cols), to_hbm(left_rows), table, index)


def row_kernel(messages, halves, final, offs_ref, ranks_ref, *refs):
    gots = refs[: len(messages)]
    left_ref, diag_ref = refs[len(messages) : len(messages) + 2]
    outs = refs[len(messages) + 2 :]
    if final:
        outs, (picked, term_of, stage, sems) = outs[:-4], outs[-4:]
    else:
        outs, (picked, term_of) = outs[:-2], outs[-2:]
    terms = offs_ref.shape[1]
    rank, width = gots[0].shape[1:]
    slots = term_of.shape[0]
    reach = slots // 2
    for slot in range(slots):
        term_of[slot] = terms
    for k in range(terms):
        offset = offs_ref[0, k]
        term_of[jnp.where(offset < 0, offset + reach, offset + reach - 1)] = k
    line = lax.broadcasted_iota(jnp.int32, (rank, width), 0)

    def pick(got, w, term):
        last = ranks_ref[0, jnp.minimum(term, terms - 1)]
        kept = jnp.where(line < last, got[w], 0.0)
        picked[pl.ds(pl.multiple_of(term * rank, rank), rank)] = kept

    for got, message in zip(gots, messages):
        for w, slot in enumerate(message.slots):
            if message.odd_slots is not None:
                slot = jnp.where((lax.axis_index("tile") & 1) == 1, slot, message.odd_slots[w])
            pick(got, w, term_of[slot])
    both = side_by_side(picked[: terms * rank])
    part = diag_ref.shape[0] // halves
    sent = []
    got = fold(dot(left_ref[...], both))
    for half in range(halves):
        rows_of = pl.ds(half * part, part)
        base = 2 * half * part
        total = got[base : base + part] + got[base + part : base + 2 * part] + diag_ref[rows_of]
        if final:
            stage[rows_of] = total
            sent.append(
                pltpu.make_async_copy(stage.at[rows_of], outs[0].at[rows_of], sems.at[half])
            )
            sent[-1].start()
        else:
            outs[half][...] = total
    for copy in sent:
        copy.wait()


def rows(offsets, ranks, gots, messages, left_split, diag_part, slots, halves, final):
    size, width = diag_part.shape
    total = left_split.shape[1]
    rank = gots[0].shape[1]
    scratch = [pltpu.VMEM((total + rank, width), f32), pltpu.SMEM((slots,), jnp.int32)]
    if final:
        scratch += [pltpu.VMEM((size, width), f32), pltpu.SemaphoreType.DMA((halves,))]
    return call(
        functools.partial(row_kernel, messages, halves, final),
        pltpu.HBM((size, width), f32) if final else [struct(size // halves, width)] * halves,
        in_hbm if final else [in_vmem] * halves,
        [in_smem, in_smem] + [in_vmem] * (len(messages) + 2),
        scratch,
        flops=8 * total * size * width,
        moved=4 * total * (size + width),
    )(offsets, ranks, *gots, left_split, diag_part)


def send(value, message):
    return lax.ppermute(value, "tile", message.pairs)


def send_all(one, two, coeffs, more, waited, beside):
    gots = []
    for value, message in zip(coeffs, one):
        if message.odd_slots is not None and message.across:
            value = relay([value], [gots[waited], more[0], beside])[0]
        gots.append(send(value, message))
    return gots + [send(value, message) for value, message in zip(more, two)]


def local(
    diag_tiles,
    left_factors,
    right_factors,
    tile_offsets,
    tile_ranks,
    mixing,
    block_index,
    rhs_field,
):
    diag_tile = diag_tiles[0, 0]
    right_tile = right_factors[0, 0]
    offsets = tile_offsets[0]
    ranks = tile_ranks[0]
    slots, rank, size = right_tile.shape
    halves = 2 if size % 32 == 0 else 1
    left_rows = left_factors.reshape(-1, size)
    groups = lax.axis_size("kern")
    table = mixing.reshape(mixing.shape[0], groups * groups).T
    index = block_index[None]
    cols = rhs_field[0]

    one, two = message_sets_of(lax.axis_size("tile"), slots)
    messages = one + two
    coeffs, split_one, both, rest = first_coefficients(cols, right_tile, one, two)
    more, split_two = rest_coefficients(both, rest, two)
    diag_part, left_split, weights = prepare(diag_tile, cols, left_rows, table, index, halves)
    gots = send_all(one, two, coeffs, more, -1, diag_part)
    first = rows(offsets, ranks, gots, messages, left_split, diag_part, slots, halves, False)
    mixed = mix(first, weights)
    coeffs, cols, both = mixed_coefficients(mixed, split_one, one, rank)
    more = next_coefficients(both, split_two, two, rank)
    diag_part = diagonal(diag_tile, cols)
    gots = send_all(one, two, coeffs, more, 0, diag_part)
    return rows(offsets, ranks, gots, messages, left_split, diag_part, slots, halves, True)[None]


def solution(mesh):
    in_specs = (
        P("kern", "tile", None, None),
        P("kern", "tile", None, None, None),
        P("kern", "tile", None, None, None),
        P("kern", "tile", None),
        P("kern", "tile", None),
        P(),
        P("tile"),
        P("kern", "tile", None),
    )
    out_specs = P("kern", "tile", None)
    return jax.shard_map(local, mesh=mesh, in_specs=in_specs, out_specs=out_specs, check_vma=False)
```

```python
import functools

import jax
import jax.numpy as jnp
from jax import lax
from jax.experimental import pallas as pl
from jax.experimental.pallas import tpu as pltpu
from jax.sharding import PartitionSpec as P

f32 = jnp.float32
bf16 = jnp.bfloat16
VMEM_BYTES = 24 * 1024 * 1024
in_vmem = pl.BlockSpec(memory_space=pltpu.VMEM)
in_smem = pl.BlockSpec(memory_space=pltpu.SMEM)
in_hbm = pl.BlockSpec(memory_space=pltpu.HBM)
in_any = pl.BlockSpec(memory_space=pl.ANY)


def to_hbm(value):
    return pltpu.with_memory_space_constraint(value, pltpu.HBM)


def struct(*shape, dtype=f32):
    return jax.ShapeDtypeStruct(shape, dtype)


def split(value):
    hi = value.astype(bf16)
    return hi, (value - hi.astype(f32)).astype(bf16)


def side_by_side(value):
    return jnp.concatenate(split(value), axis=1)


def dot(left, right):
    return jnp.dot(left, right, preferred_element_type=f32)


def fold(value):
    width = value.shape[1] // 2
    return value[:, :width] + value[:, width:]


def call(kernel, outs, out_specs, in_specs, scratch=(), flops=0, moved=0):
    return pl.pallas_call(
        kernel,
        out_shape=outs,
        in_specs=in_specs,
        out_specs=out_specs,
        scratch_shapes=list(scratch),
        compiler_params=pltpu.CompilerParams(vmem_limit_bytes=VMEM_BYTES),
        cost_estimate=pl.CostEstimate(flops=flops, bytes_accessed=moved, transcendentals=0),
    )


class Message:
    def __init__(self, pairs, slots, odd_slots=None):
        self.pairs = pairs
        self.slots = slots
        self.odd_slots = odd_slots
        self.width = len(slots)
        half = len(pairs) // 2
        self.across = self.width * sum((a < half) != (b < half) for a, b in pairs)


def message_sets_of(count, slots):
    reach = slots // 2
    groups = {}
    for slot in range(slots):
        offset = slot - reach if slot < reach else slot - reach + 1
        groups.setdefault(offset % count, []).append(slot)
    messages = []
    below, above = reach - 1, reach
    if groups.get(1) == [above] and groups.get(count - 1) == [below] and count % 2 == 0:
        del groups[1], groups[count - 1]
        for turn, (even, odd) in enumerate(((below, above), (above, below))):
            pairs = [(at, (at + (1, -1)[(at + turn) % 2]) % count) for at in range(count)]
            messages.append(Message(pairs, [even], [odd]))
    for ahead, group in groups.items():
        messages.append(Message([(at, (at - ahead) % count) for at in range(count)], group))
    messages.sort(key=lambda message: -message.across)
    first = messages[:1] + [m for m in messages[:0:-1] if m.odd_slots is not None]
    rest = [message for message in messages if message not in first]
    return [first, rest[-1:] + rest[:-1]]


def slots_of(messages):
    return sorted({slot for m in messages for slot in m.slots + (m.odd_slots or [])})


def copy_runs(slots, source, target, sems):
    copies, at = [], 0
    while at < len(slots):
        count = 1
        while at + count < len(slots) and slots[at + count] == slots[at] + count:
            count += 1
        copies.append(
            pltpu.make_async_copy(
                source.at[pl.ds(slots[at], count)], target.at[pl.ds(at, count)], sems.at[at]
            )
        )
        copies[-1].start()
        at += count
    return copies


def store_coefficients(split_ref, both, messages, rank, outs):
    slots = slots_of(messages)
    size = len(slots) * rank
    got = fold(dot(split_ref[...], both))
    got = got[:size] + got[size:]

    def piece(slot):
        row = slots.index(slot) * rank
        return got[row : row + rank]

    odd = jnp.full((rank, got.shape[1]), lax.axis_index("tile") & 1, jnp.int32) == 1
    for message, out in zip(messages, outs):
        for w, slot in enumerate(message.slots):
            value = piece(slot)
            if message.odd_slots is not None:
                value = jnp.where(odd, piece(message.odd_slots[w]), value)
            out[w] = value


def split_rows(right, split_ref):
    count, rank, size = right.shape
    rows = count * rank
    hi, lo = split(right[...].reshape(rows, size))
    split_ref[:rows] = hi
    split_ref[rows:] = lo


def first_coeff_kernel(messages, others, cols_ref, right_ref, *refs):
    outs, refs = refs[: len(messages)], refs[len(messages) :]
    split_ref, both_ref, rest_ref, cols, right, cols_sem, sems, rest_sems = refs
    cols_copy = pltpu.make_async_copy(cols_ref, cols, cols_sem)
    cols_copy.start()
    copies = copy_runs(slots_of(messages), right_ref, right, sems)
    rest = copy_runs(slots_of(others), right_ref, rest_ref, rest_sems)
    cols_copy.wait()
    both_ref[...] = side_by_side(cols[...])
    for copy in copies:
        copy.wait()
    split_rows(right, split_ref)
    store_coefficients(split_ref, both_ref[...], messages, right.shape[1], outs)
    for copy in rest:
        copy.wait()


def first_coefficients(cols, right_tile, messages, others):
    _, rank, size = right_tile.shape
    width = cols.shape[1]
    count, rest = len(slots_of(messages)), len(slots_of(others))
    outs = [struct(message.width, rank, width) for message in messages]
    outs += [
        struct(2 * count * rank, size, dtype=bf16),
        struct(size, 2 * width, dtype=bf16),
        struct(rest, rank, size),
    ]
    got = call(
        functools.partial(first_coeff_kernel, messages, others),
        outs,
        [in_vmem] * len(outs),
        [in_hbm, in_hbm],
        [
            pltpu.VMEM(cols.shape, f32),
            pltpu.VMEM((count, rank, size), f32),
            pltpu.SemaphoreType.DMA,
            pltpu.SemaphoreType.DMA((count,)),
            pltpu.SemaphoreType.DMA((rest,)),
        ],
        flops=8 * count * rank * size * width,
        moved=4 * (count + rest) * rank * size,
    )(to_hbm(cols), to_hbm(right_tile))
    return got[:-3], got[-3], got[-2], got[-1]


def rest_coeff_kernel(messages, both_ref, right_ref, *refs):
    outs, split_ref = refs[:-1], refs[-1]
    split_rows(right_ref, split_ref)
    store_coefficients(split_ref, both_ref[...], messages, right_ref.shape[1], outs)


def rest_coefficients(both, right, messages):
    count, rank, size = right.shape
    width = both.shape[1] // 2
    outs = [struct(message.width, rank, width) for message in messages]
    outs.append(struct(2 * count * rank, size, dtype=bf16))
    got = call(
        functools.partial(rest_coeff_kernel, messages),
        outs,
        [in_vmem] * len(outs),
        [in_vmem] * 2,
        flops=8 * count * rank * size * width,
        moved=8 * count * rank * size,
    )(both, right)
    return got[:-1], got[-1]


def halve_kernel(base, own_ref, got_ref, weights_ref, keep_ref, send_ref):
    own, got = own_ref[...], got_ref[...]
    keep_ref[...] = own * weights_ref[base] + got * weights_ref[base + 1]
    send_ref[...] = own * weights_ref[base + 2] + got * weights_ref[base + 3]


def halve(own, got, weights, half):
    part, width = own.shape
    return call(
        functools.partial(halve_kernel, 4 * half),
        [struct(part, width)] * 2,
        [in_vmem] * 2,
        [in_vmem] * 3,
        flops=6 * part * width,
        moved=32 * part * width,
    )(own, got, weights)


def mix(first, weights):
    groups = lax.axis_size("kern")
    if groups != 4:
        fields = [lax.all_gather(part, "kern") for part in first]
        mixed = jnp.sum(jnp.concatenate(fields, axis=1) * weights, axis=0)
        return [(mixed, jnp.zeros_like(mixed))]
    count = lax.axis_size("tile")
    steps = ([], [])
    for group in range(groups):
        for tile in range(count):
            for turn, pairs in enumerate(steps):
                dest = group ^ (2 - (turn + tile) % 2)
                pairs.append((group * count + tile, dest * count + tile))
    axes = ("kern", "tile")
    came = [lax.ppermute(part, axes, pairs) for part, pairs in zip(first, steps)]
    sums = [
        halve(part, got, weights, half)
        for half, (part, got) in enumerate(zip(first, came))
    ]
    return [
        (keep, lax.ppermute(send, axes, pairs)) for (keep, send), pairs in zip(sums, steps[::-1])
    ]


def mixed_coeff_kernel(messages, terms, *refs):
    fields, split_ref = refs[:terms], refs[terms]
    outs, cols_ref, both_ref = refs[terms + 1 : -2], refs[-2], refs[-1]
    part = fields[0].shape[0]
    for at in range(0, terms, 2):
        rows_of = pl.ds(at // 2 * part, part)
        total = fields[at][...] + fields[at + 1][...]
        cols_ref[rows_of] = total
        both_ref[rows_of] = side_by_side(total)
    store_coefficients(split_ref, both_ref[...], messages, outs[0].shape[1], outs)


def mixed_coefficients(mixed, split_right, messages, rank):
    flat = [term for pair in mixed for term in pair]
    part, width = flat[0].shape
    size = part * len(mixed)
    total = split_right.shape[0]
    outs = [struct(message.width, rank, width) for message in messages]
    outs += [struct(size, width), struct(size, 2 * width, dtype=bf16)]
    got = call(
        functools.partial(mixed_coeff_kernel, messages, len(flat)),
        outs,
        [in_vmem] * len(outs),
        [in_vmem] * (len(flat) + 1),
        flops=4 * total * size * width,
        moved=2 * total * (size + width),
    )(*flat, split_right)
    return got[:-2], got[-2], got[-1]


def next_coeff_kernel(messages, both_ref, split_ref, *outs):
    store_coefficients(split_ref, both_ref[...], messages, outs[0].shape[1], outs)


def next_coefficients(both, split_right, messages, rank):
    size, width = both.shape[0], both.shape[1] // 2
    total = split_right.shape[0]
    return call(
        functools.partial(next_coeff_kernel, messages),
        [struct(message.width, rank, width) for message in messages],
        [in_vmem] * len(messages),
        [in_vmem] * 2,
        flops=4 * total * size * width,
        moved=2 * total * (size + width),
    )(both, split_right)


def times_diag(diag_ref, cols_ref):
    both = side_by_side(cols_ref[...])
    hi, lo = split(diag_ref[...])
    return fold(dot(hi, both) + dot(lo, both))


def relay_kernel(count, *refs):
    for source, target in zip(refs[:count], refs[-count:]):
        target[...] = source[...]


def relay(values, after):
    return call(
        functools.partial(relay_kernel, len(values)),
        [struct(*value.shape) for value in values],
        [in_vmem] * len(values),
        [in_vmem] * len(values) + [in_any] * len(after),
        moved=8 * sum(value.size for value in values),
    )(*values, *after)


def diag_kernel(diag_ref, cols_ref, out_ref):
    out_ref[...] = times_diag(diag_ref, cols_ref)


def diagonal(diag_tile, cols):
    size, width = cols.shape
    return call(
        diag_kernel,
        struct(size, width),
        in_vmem,
        [in_vmem, in_vmem],
        flops=8 * size * size * width,
        moved=4 * size * (size + 2 * width),
    )(diag_tile, cols)


def weight_rows(size):
    groups = lax.axis_size("kern")
    me = lax.axis_index("kern")
    if groups != 4:
        return [(me * groups + b, slice(0, size)) for b in range(groups)]
    rows_of = []
    odd = lax.axis_index("tile") & 1
    one, two = me ^ (2 - odd), me ^ (1 + odd)
    for half, (first, second) in enumerate(((one, two), (two, one))):
        lanes = slice(half * (size // 2), (half + 1) * (size // 2))
        for a in (me, second):
            for b in (me, first):
                rows_of.append((a * groups + b, lanes))
    return rows_of


def prepare_kernel(
    halves, diag_hbm, cols_hbm, left_hbm, table_ref, index_ref,
    diag_out, left_out, weights_ref, diag_ref, cols_ref, left_ref, full_ref, sems,
):
    copies = []
    for at, (source, target) in enumerate(
        ((diag_hbm, diag_ref), (cols_hbm, cols_ref), (left_hbm, left_ref))
    ):
        copies.append(pltpu.make_async_copy(source, target, sems.at[at]))
        copies[-1].start()
    entries = table_ref.shape[1]
    size = index_ref.shape[1]
    hot = (lax.broadcasted_iota(jnp.int32, (entries, size), 0) == index_ref[...]).astype(f32)
    full_ref[...] = jnp.dot(
        table_ref[...], hot, precision=lax.Precision.HIGHEST, preferred_element_type=f32
    )
    width = weights_ref.shape[2]
    for at, (row, lanes) in enumerate(weight_rows(size)):
        piece = full_ref[pl.ds(row, 1), lanes]
        weights_ref[at] = jnp.broadcast_to(piece, (width, piece.shape[1])).T
    copies[0].wait()
    copies[1].wait()
    diag_out[...] = times_diag(diag_ref, cols_ref)
    copies[2].wait()
    total = left_ref.shape[0]
    step = 128 if total % 128 == 0 else total
    part = size // halves
    for at in range(0, total, step):
        span = slice(at, at + step)
        hi, lo = split(left_ref[span].T)
        for half in range(halves):
            base = 2 * half * part
            rows_of = slice(half * part, (half + 1) * part)
            left_out[base : base + part, span] = hi[rows_of]
            left_out[base + part : base + 2 * part, span] = lo[rows_of]


def prepare(diag_tile, cols, left_rows, table, index, halves):
    size, width = cols.shape
    total = left_rows.shape[0]
    weights = weight_rows(size)
    part = weights[0][1].stop
    return call(
        functools.partial(prepare_kernel, halves),
        [
            struct(size, width),
            struct(2 * size, total, dtype=bf16),
            struct(len(weights), part, width),
        ],
        [in_vmem] * 3,
        [in_hbm] * 3 + [in_vmem] * 2,
        [
            pltpu.VMEM(diag_tile.shape, f32),
            pltpu.VMEM(cols.shape, f32),
            pltpu.VMEM(left_rows.shape, f32),
            pltpu.VMEM((table.shape[0], size), f32),
            pltpu.SemaphoreType.DMA((3,)),
        ],
        flops=8 * size * size * width,
        moved=8 * total * size + 4 * size * (size + 2 * width),
    )(to_hbm(diag_tile), to_hbm(cols), to_hbm(left_rows), table, index)


def row_kernel(messages, halves, final, offs_ref, ranks_ref, *refs):
    gots = refs[: len(messages)]
    left_ref, diag_ref = refs[len(messages) : len(messages) + 2]
    outs = refs[len(messages) + 2 :]
    if final:
        outs, (picked, term_of, stage, sems) = outs[:-4], outs[-4:]
    else:
        outs, (picked, term_of) = outs[:-2], outs[-2:]
    terms = offs_ref.shape[1]
    rank, width = gots[0].shape[1:]
    slots = term_of.shape[0]
    reach = slots // 2
    for slot in range(slots):
        term_of[slot] = terms
    for k in range(terms):
        offset = offs_ref[0, k]
        term_of[jnp.where(offset < 0, offset + reach, offset + reach - 1)] = k
    line = lax.broadcasted_iota(jnp.int32, (rank, width), 0)

    def pick(got, w, term):
        last = ranks_ref[0, jnp.minimum(term, terms - 1)]
        kept = jnp.where(line < last, got[w], 0.0)
        picked[pl.ds(pl.multiple_of(term * rank, rank), rank)] = kept

    for got, message in zip(gots, messages):
        for w, slot in enumerate(message.slots):
            if message.odd_slots is not None:
                slot = jnp.where((lax.axis_index("tile") & 1) == 1, slot, message.odd_slots[w])
            pick(got, w, term_of[slot])
    both = side_by_side(picked[: terms * rank])
    part = diag_ref.shape[0] // halves
    sent = []
    got = fold(dot(left_ref[...], both))
    for half in range(halves):
        rows_of = pl.ds(half * part, part)
        base = 2 * half * part
        total = got[base : base + part] + got[base + part : base + 2 * part] + diag_ref[rows_of]
        if final:
            stage[rows_of] = total
            sent.append(
                pltpu.make_async_copy(stage.at[rows_of], outs[0].at[rows_of], sems.at[half])
            )
            sent[-1].start()
        else:
            outs[half][...] = total
    for copy in sent:
        copy.wait()


def rows(offsets, ranks, gots, messages, left_split, diag_part, slots, halves, final):
    size, width = diag_part.shape
    total = left_split.shape[1]
    rank = gots[0].shape[1]
    scratch = [pltpu.VMEM((total + rank, width), f32), pltpu.SMEM((slots,), jnp.int32)]
    if final:
        scratch += [pltpu.VMEM((size, width), f32), pltpu.SemaphoreType.DMA((halves,))]
    return call(
        functools.partial(row_kernel, messages, halves, final),
        pltpu.HBM((size, width), f32) if final else [struct(size // halves, width)] * halves,
        in_hbm if final else [in_vmem] * halves,
        [in_smem, in_smem] + [in_vmem] * (len(messages) + 2),
        scratch,
        flops=8 * total * size * width,
        moved=4 * total * (size + width),
    )(offsets, ranks, *gots, left_split, diag_part)


def send(value, message):
    return lax.ppermute(value, "tile", message.pairs)


def send_all(one, two, coeffs, more, waited, beside):
    gots = []
    for value, message in zip(coeffs, one):
        if message.odd_slots is not None and message.across:
            value = relay([value], [gots[waited], more[0], beside])[0]
        gots.append(send(value, message))
    return gots + [send(value, message) for value, message in zip(more, two)]


def local(
    diag_tiles,
    left_factors,
    right_factors,
    tile_offsets,
    tile_ranks,
    mixing,
    block_index,
    rhs_field,
):
    diag_tile = diag_tiles[0, 0]
    right_tile = right_factors[0, 0]
    offsets = tile_offsets[0]
    ranks = tile_ranks[0]
    slots, rank, size = right_tile.shape
    halves = 2 if size % 32 == 0 else 1
    left_rows = left_factors.reshape(-1, size)
    groups = lax.axis_size("kern")
    table = mixing.reshape(mixing.shape[0], groups * groups).T
    index = block_index[None]
    cols = rhs_field[0]

    one, two = message_sets_of(lax.axis_size("tile"), slots)
    messages = one + two
    coeffs, split_one, both, rest = first_coefficients(cols, right_tile, one, two)
    more, split_two = rest_coefficients(both, rest, two)
    diag_part, left_split, weights = prepare(diag_tile, cols, left_rows, table, index, halves)
    gots = send_all(one, two, coeffs, more, -1, diag_part)
    first = rows(offsets, ranks, gots, messages, left_split, diag_part, slots, halves, False)
    mixed = mix(first, weights)
    coeffs, cols, both = mixed_coefficients(mixed, split_one, one, rank)
    more = next_coefficients(both, split_two, two, rank)
    diag_part = diagonal(diag_tile, cols)
    gots = send_all(one, two, coeffs, more, 0, diag_part)
    return rows(offsets, ranks, gots, messages, left_split, diag_part, slots, halves, True)[None]


def solution(mesh):
    in_specs = (
        P("kern", "tile", None, None),
        P("kern", "tile", None, None, None),
        P("kern", "tile", None, None, None),
        P("kern", "tile", None),
        P("kern", "tile", None),
        P(),
        P("tile"),
        P("kern", "tile", None),
    )
    out_specs = P("kern", "tile", None)
    return jax.shard_map(local, mesh=mesh, in_specs=in_specs, out_specs=out_specs, check_vma=False)
```

```python
import functools

import jax
import jax.numpy as jnp
from jax import lax
from jax.experimental import pallas as pl
from jax.experimental.pallas import tpu as pltpu
from jax.sharding import PartitionSpec as P

f32 = jnp.float32
bf16 = jnp.bfloat16
VMEM_BYTES = 24 * 1024 * 1024
in_vmem = pl.BlockSpec(memory_space=pltpu.VMEM)
in_smem = pl.BlockSpec(memory_space=pltpu.SMEM)
in_hbm = pl.BlockSpec(memory_space=pltpu.HBM)
in_any = pl.BlockSpec(memory_space=pl.ANY)


def to_hbm(value):
    return pltpu.with_memory_space_constraint(value, pltpu.HBM)


def struct(*shape, dtype=f32):
    return jax.ShapeDtypeStruct(shape, dtype)


def split(value):
    hi = value.astype(bf16)
    return hi, (value - hi.astype(f32)).astype(bf16)


def side_by_side(value):
    return jnp.concatenate(split(value), axis=1)


def dot(left, right):
    return jnp.dot(left, right, preferred_element_type=f32)


def fold(value):
    width = value.shape[1] // 2
    return value[:, :width] + value[:, width:]


def call(kernel, outs, out_specs, in_specs, scratch=(), flops=0, moved=0):
    return pl.pallas_call(
        kernel,
        out_shape=outs,
        in_specs=in_specs,
        out_specs=out_specs,
        scratch_shapes=list(scratch),
        compiler_params=pltpu.CompilerParams(vmem_limit_bytes=VMEM_BYTES),
        cost_estimate=pl.CostEstimate(flops=flops, bytes_accessed=moved, transcendentals=0),
    )


class Message:
    def __init__(self, pairs, slots, odd_slots=None):
        self.pairs = pairs
        self.slots = slots
        self.odd_slots = odd_slots
        self.width = len(slots)
        half = len(pairs) // 2
        self.across = self.width * sum((a < half) != (b < half) for a, b in pairs)


def message_sets_of(count, slots):
    reach = slots // 2
    groups = {}
    for slot in range(slots):
        offset = slot - reach if slot < reach else slot - reach + 1
        groups.setdefault(offset % count, []).append(slot)
    messages = []
    below, above = reach - 1, reach
    if groups.get(1) == [above] and groups.get(count - 1) == [below] and count % 2 == 0:
        del groups[1], groups[count - 1]
        for turn, (even, odd) in enumerate(((below, above), (above, below))):
            pairs = [(at, (at + (1, -1)[(at + turn) % 2]) % count) for at in range(count)]
            messages.append(Message(pairs, [even], [odd]))
    for ahead, group in groups.items():
        messages.append(Message([(at, (at - ahead) % count) for at in range(count)], group))
    messages.sort(key=lambda message: -message.across)
    short = [message for message in messages[::-1] if message.odd_slots is not None]
    long = [message for message in messages if message.odd_slots is None]
    return [long[-1:] + short, long[-2:-1] + long[:-2]]


def slots_of(messages):
    return sorted({slot for m in messages for slot in m.slots + (m.odd_slots or [])})


def copy_runs(slots, source, target, sems):
    copies, at = [], 0
    while at < len(slots):
        count = 1
        while at + count < len(slots) and slots[at + count] == slots[at] + count:
            count += 1
        copies.append(
            pltpu.make_async_copy(
                source.at[pl.ds(slots[at], count)], target.at[pl.ds(at, count)], sems.at[at]
            )
        )
        copies[-1].start()
        at += count
    return copies


def store_coefficients(split_ref, both, messages, rank, outs):
    slots = slots_of(messages)
    size = len(slots) * rank
    got = fold(dot(split_ref[...], both))
    got = got[:size] + got[size:]

    def piece(slot):
        row = slots.index(slot) * rank
        return got[row : row + rank]

    odd = jnp.full((rank, got.shape[1]), lax.axis_index("tile") & 1, jnp.int32) == 1
    for message, out in zip(messages, outs):
        for w, slot in enumerate(message.slots):
            value = piece(slot)
            if message.odd_slots is not None:
                value = jnp.where(odd, piece(message.odd_slots[w]), value)
            out[w] = value


def split_rows(right, split_ref):
    count, rank, size = right.shape
    rows = count * rank
    hi, lo = split(right[...].reshape(rows, size))
    split_ref[:rows] = hi
    split_ref[rows:] = lo


def first_coeff_kernel(messages, others, cols_ref, right_ref, *refs):
    outs, refs = refs[: len(messages)], refs[len(messages) :]
    split_ref, both_ref, rest_ref, cols, right, cols_sem, sems, rest_sems = refs
    cols_copy = pltpu.make_async_copy(cols_ref, cols, cols_sem)
    cols_copy.start()
    copies = copy_runs(slots_of(messages), right_ref, right, sems)
    rest = copy_runs(slots_of(others), right_ref, rest_ref, rest_sems)
    cols_copy.wait()
    both_ref[...] = side_by_side(cols[...])
    for copy in copies:
        copy.wait()
    split_rows(right, split_ref)
    store_coefficients(split_ref, both_ref[...], messages, right.shape[1], outs)
    for copy in rest:
        copy.wait()


def first_coefficients(cols, right_tile, messages, others):
    _, rank, size = right_tile.shape
    width = cols.shape[1]
    count, rest = len(slots_of(messages)), len(slots_of(others))
    outs = [struct(message.width, rank, width) for message in messages]
    outs += [
        struct(2 * count * rank, size, dtype=bf16),
        struct(size, 2 * width, dtype=bf16),
        struct(rest, rank, size),
    ]
    got = call(
        functools.partial(first_coeff_kernel, messages, others),
        outs,
        [in_vmem] * len(outs),
        [in_hbm, in_hbm],
        [
            pltpu.VMEM(cols.shape, f32),
            pltpu.VMEM((count, rank, size), f32),
            pltpu.SemaphoreType.DMA,
            pltpu.SemaphoreType.DMA((count,)),
            pltpu.SemaphoreType.DMA((rest,)),
        ],
        flops=8 * count * rank * size * width,
        moved=4 * (count + rest) * rank * size,
    )(to_hbm(cols), to_hbm(right_tile))
    return got[:-3], got[-3], got[-2], got[-1]


def rest_coeff_kernel(messages, both_ref, right_ref, *refs):
    outs, split_ref = refs[:-1], refs[-1]
    split_rows(right_ref, split_ref)
    store_coefficients(split_ref, both_ref[...], messages, right_ref.shape[1], outs)


def rest_coefficients(both, right, messages):
    count, rank, size = right.shape
    width = both.shape[1] // 2
    outs = [struct(message.width, rank, width) for message in messages]
    outs.append(struct(2 * count * rank, size, dtype=bf16))
    got = call(
        functools.partial(rest_coeff_kernel, messages),
        outs,
        [in_vmem] * len(outs),
        [in_vmem] * 2,
        flops=8 * count * rank * size * width,
        moved=8 * count * rank * size,
    )(both, right)
    return got[:-1], got[-1]


def halve_kernel(base, own_ref, got_ref, weights_ref, keep_ref, send_ref):
    own, got = own_ref[...], got_ref[...]
    keep_ref[...] = own * weights_ref[base] + got * weights_ref[base + 1]
    send_ref[...] = own * weights_ref[base + 2] + got * weights_ref[base + 3]


def halve(own, got, weights, half):
    part, width = own.shape
    return call(
        functools.partial(halve_kernel, 4 * half),
        [struct(part, width)] * 2,
        [in_vmem] * 2,
        [in_vmem] * 3,
        flops=6 * part * width,
        moved=32 * part * width,
    )(own, got, weights)


def mix(first, weights):
    groups = lax.axis_size("kern")
    if groups != 4:
        fields = [lax.all_gather(part, "kern") for part in first]
        mixed = jnp.sum(jnp.concatenate(fields, axis=1) * weights, axis=0)
        return [(mixed, jnp.zeros_like(mixed))]
    count = lax.axis_size("tile")
    steps = ([], [])
    for group in range(groups):
        for tile in range(count):
            for turn, pairs in enumerate(steps):
                dest = group ^ (1 + (turn + tile) % 2)
                pairs.append((group * count + tile, dest * count + tile))
    axes = ("kern", "tile")
    came = [lax.ppermute(part, axes, pairs) for part, pairs in zip(first, steps)]
    sums = [
        halve(part, got, weights, half)
        for half, (part, got) in enumerate(zip(first, came))
    ]
    return [
        (keep, lax.ppermute(send, axes, pairs)) for (keep, send), pairs in zip(sums, steps[::-1])
    ]


def mixed_coeff_kernel(messages, terms, *refs):
    fields, split_ref = refs[:terms], refs[terms]
    outs, cols_ref, both_ref = refs[terms + 1 : -2], refs[-2], refs[-1]
    part = fields[0].shape[0]
    for at in range(0, terms, 2):
        rows_of = pl.ds(at // 2 * part, part)
        total = fields[at][...] + fields[at + 1][...]
        cols_ref[rows_of] = total
        both_ref[rows_of] = side_by_side(total)
    store_coefficients(split_ref, both_ref[...], messages, outs[0].shape[1], outs)


def mixed_coefficients(mixed, split_right, messages, rank):
    flat = [term for pair in mixed for term in pair]
    part, width = flat[0].shape
    size = part * len(mixed)
    total = split_right.shape[0]
    outs = [struct(message.width, rank, width) for message in messages]
    outs += [struct(size, width), struct(size, 2 * width, dtype=bf16)]
    got = call(
        functools.partial(mixed_coeff_kernel, messages, len(flat)),
        outs,
        [in_vmem] * len(outs),
        [in_vmem] * (len(flat) + 1),
        flops=4 * total * size * width,
        moved=2 * total * (size + width),
    )(*flat, split_right)
    return got[:-2], got[-2], got[-1]


def next_coeff_kernel(messages, both_ref, split_ref, *outs):
    store_coefficients(split_ref, both_ref[...], messages, outs[0].shape[1], outs)


def next_coefficients(both, split_right, messages, rank):
    size, width = both.shape[0], both.shape[1] // 2
    total = split_right.shape[0]
    return call(
        functools.partial(next_coeff_kernel, messages),
        [struct(message.width, rank, width) for message in messages],
        [in_vmem] * len(messages),
        [in_vmem] * 2,
        flops=4 * total * size * width,
        moved=2 * total * (size + width),
    )(both, split_right)


def times_diag(diag_ref, cols_ref):
    both = side_by_side(cols_ref[...])
    hi, lo = split(diag_ref[...])
    return fold(dot(hi, both) + dot(lo, both))


def relay_kernel(count, *refs):
    for source, target in zip(refs[:count], refs[-count:]):
        target[...] = source[...]


def relay(values, after):
    return call(
        functools.partial(relay_kernel, len(values)),
        [struct(*value.shape) for value in values],
        [in_vmem] * len(values),
        [in_vmem] * len(values) + [in_any] * len(after),
        moved=8 * sum(value.size for value in values),
    )(*values, *after)


def diag_kernel(diag_ref, cols_ref, out_ref):
    out_ref[...] = times_diag(diag_ref, cols_ref)


def diagonal(diag_tile, cols):
    size, width = cols.shape
    return call(
        diag_kernel,
        struct(size, width),
        in_vmem,
        [in_vmem, in_vmem],
        flops=8 * size * size * width,
        moved=4 * size * (size + 2 * width),
    )(diag_tile, cols)


def weight_rows(size):
    groups = lax.axis_size("kern")
    me = lax.axis_index("kern")
    if groups != 4:
        return [(me * groups + b, slice(0, size)) for b in range(groups)]
    rows_of = []
    odd = lax.axis_index("tile") & 1
    one, two = me ^ (1 + odd), me ^ (2 - odd)
    for half, (first, second) in enumerate(((one, two), (two, one))):
        lanes = slice(half * (size // 2), (half + 1) * (size // 2))
        for a in (me, second):
            for b in (me, first):
                rows_of.append((a * groups + b, lanes))
    return rows_of


def prepare_kernel(
    halves, diag_hbm, cols_hbm, left_hbm, table_ref, index_ref,
    diag_out, left_out, weights_ref, diag_ref, cols_ref, left_ref, full_ref, sems,
):
    copies = []
    for at, (source, target) in enumerate(
        ((diag_hbm, diag_ref), (cols_hbm, cols_ref), (left_hbm, left_ref))
    ):
        copies.append(pltpu.make_async_copy(source, target, sems.at[at]))
        copies[-1].start()
    entries = table_ref.shape[1]
    size = index_ref.shape[1]
    hot = (lax.broadcasted_iota(jnp.int32, (entries, size), 0) == index_ref[...]).astype(f32)
    full_ref[...] = jnp.dot(
        table_ref[...], hot, precision=lax.Precision.HIGHEST, preferred_element_type=f32
    )
    width = weights_ref.shape[2]
    for at, (row, lanes) in enumerate(weight_rows(size)):
        piece = full_ref[pl.ds(row, 1), lanes]
        weights_ref[at] = jnp.broadcast_to(piece, (width, piece.shape[1])).T
    copies[0].wait()
    copies[1].wait()
    diag_out[...] = times_diag(diag_ref, cols_ref)
    copies[2].wait()
    total = left_ref.shape[0]
    step = 128 if total % 128 == 0 else total
    part = size // halves
    for at in range(0, total, step):
        span = slice(at, at + step)
        hi, lo = split(left_ref[span].T)
        for half in range(halves):
            base = 2 * half * part
            rows_of = slice(half * part, (half + 1) * part)
            left_out[base : base + part, span] = hi[rows_of]
            left_out[base + part : base + 2 * part, span] = lo[rows_of]


def prepare(diag_tile, cols, left_rows, table, index, halves):
    size, width = cols.shape
    total = left_rows.shape[0]
    weights = weight_rows(size)
    part = weights[0][1].stop
    return call(
        functools.partial(prepare_kernel, halves),
        [
            struct(size, width),
            struct(2 * size, total, dtype=bf16),
            struct(len(weights), part, width),
        ],
        [in_vmem] * 3,
        [in_hbm] * 3 + [in_vmem] * 2,
        [
            pltpu.VMEM(diag_tile.shape, f32),
            pltpu.VMEM(cols.shape, f32),
            pltpu.VMEM(left_rows.shape, f32),
            pltpu.VMEM((table.shape[0], size), f32),
            pltpu.SemaphoreType.DMA((3,)),
        ],
        flops=8 * size * size * width,
        moved=8 * total * size + 4 * size * (size + 2 * width),
    )(to_hbm(diag_tile), to_hbm(cols), to_hbm(left_rows), table, index)


def row_kernel(messages, halves, final, offs_ref, ranks_ref, *refs):
    gots = refs[: len(messages)]
    left_ref, diag_ref = refs[len(messages) : len(messages) + 2]
    outs = refs[len(messages) + 2 :]
    if final:
        outs, (picked, term_of, stage, sems) = outs[:-4], outs[-4:]
    else:
        outs, (picked, term_of) = outs[:-2], outs[-2:]
    terms = offs_ref.shape[1]
    rank, width = gots[0].shape[1:]
    slots = term_of.shape[0]
    reach = slots // 2
    for slot in range(slots):
        term_of[slot] = terms
    for k in range(terms):
        offset = offs_ref[0, k]
        term_of[jnp.where(offset < 0, offset + reach, offset + reach - 1)] = k
    line = lax.broadcasted_iota(jnp.int32, (rank, width), 0)

    def pick(got, w, term):
        last = ranks_ref[0, jnp.minimum(term, terms - 1)]
        kept = jnp.where(line < last, got[w], 0.0)
        picked[pl.ds(pl.multiple_of(term * rank, rank), rank)] = kept

    for got, message in zip(gots, messages):
        for w, slot in enumerate(message.slots):
            if message.odd_slots is not None:
                slot = jnp.where((lax.axis_index("tile") & 1) == 1, slot, message.odd_slots[w])
            pick(got, w, term_of[slot])
    both = side_by_side(picked[: terms * rank])
    part = diag_ref.shape[0] // halves
    sent = []
    got = fold(dot(left_ref[...], both))
    for half in range(halves):
        rows_of = pl.ds(half * part, part)
        base = 2 * half * part
        total = got[base : base + part] + got[base + part : base + 2 * part] + diag_ref[rows_of]
        if final:
            stage[rows_of] = total
            sent.append(
                pltpu.make_async_copy(stage.at[rows_of], outs[0].at[rows_of], sems.at[half])
            )
            sent[-1].start()
        else:
            outs[half][...] = total
    for copy in sent:
        copy.wait()


def rows(offsets, ranks, gots, messages, left_split, diag_part, slots, halves, final):
    size, width = diag_part.shape
    total = left_split.shape[1]
    rank = gots[0].shape[1]
    scratch = [pltpu.VMEM((total + rank, width), f32), pltpu.SMEM((slots,), jnp.int32)]
    if final:
        scratch += [pltpu.VMEM((size, width), f32), pltpu.SemaphoreType.DMA((halves,))]
    return call(
        functools.partial(row_kernel, messages, halves, final),
        pltpu.HBM((size, width), f32) if final else [struct(size // halves, width)] * halves,
        in_hbm if final else [in_vmem] * halves,
        [in_smem, in_smem] + [in_vmem] * (len(messages) + 2),
        scratch,
        flops=8 * total * size * width,
        moved=4 * total * (size + width),
    )(offsets, ranks, *gots, left_split, diag_part)


def send(value, message):
    return lax.ppermute(value, "tile", message.pairs)


def send_all(one, two, coeffs, more, waited, beside):
    gots = []
    for value, message in zip(coeffs, one):
        if message.odd_slots is not None and message.across:
            value = relay([value], [gots[waited], more[0], beside])[0]
        gots.append(send(value, message))
    return gots + [send(value, message) for value, message in zip(more, two)]


def local(
    diag_tiles,
    left_factors,
    right_factors,
    tile_offsets,
    tile_ranks,
    mixing,
    block_index,
    rhs_field,
):
    diag_tile = diag_tiles[0, 0]
    right_tile = right_factors[0, 0]
    offsets = tile_offsets[0]
    ranks = tile_ranks[0]
    slots, rank, size = right_tile.shape
    halves = 2 if size % 32 == 0 else 1
    left_rows = left_factors.reshape(-1, size)
    groups = lax.axis_size("kern")
    table = mixing.reshape(mixing.shape[0], groups * groups).T
    index = block_index[None]
    cols = rhs_field[0]

    one, two = message_sets_of(lax.axis_size("tile"), slots)
    messages = one + two
    coeffs, split_one, both, rest = first_coefficients(cols, right_tile, one, two)
    more, split_two = rest_coefficients(both, rest, two)
    diag_part, left_split, weights = prepare(diag_tile, cols, left_rows, table, index, halves)
    gots = send_all(one, two, coeffs, more, -1, diag_part)
    first = rows(offsets, ranks, gots, messages, left_split, diag_part, slots, halves, False)
    mixed = mix(first, weights)
    coeffs, cols, both = mixed_coefficients(mixed, split_one, one, rank)
    more = next_coefficients(both, split_two, two, rank)
    diag_part = diagonal(diag_tile, cols)
    gots = send_all(one, two, coeffs, more, 0, diag_part)
    return rows(offsets, ranks, gots, messages, left_split, diag_part, slots, halves, True)[None]


def solution(mesh):
    in_specs = (
        P("kern", "tile", None, None),
        P("kern", "tile", None, None, None),
        P("kern", "tile", None, None, None),
        P("kern", "tile", None),
        P("kern", "tile", None),
        P(),
        P("tile"),
        P("kern", "tile", None),
    )
    out_specs = P("kern", "tile", None)
    return jax.shard_map(local, mesh=mesh, in_specs=in_specs, out_specs=out_specs, check_vma=False)
```

```python
import functools

import jax
import jax.numpy as jnp
from jax import lax
from jax.experimental import pallas as pl
from jax.experimental.pallas import tpu as pltpu
from jax.sharding import PartitionSpec as P

f32 = jnp.float32
bf16 = jnp.bfloat16
VMEM_BYTES = 24 * 1024 * 1024
in_vmem = pl.BlockSpec(memory_space=pltpu.VMEM)
in_smem = pl.BlockSpec(memory_space=pltpu.SMEM)
in_hbm = pl.BlockSpec(memory_space=pltpu.HBM)
in_any = pl.BlockSpec(memory_space=pl.ANY)


def to_hbm(value):
    return pltpu.with_memory_space_constraint(value, pltpu.HBM)


def struct(*shape, dtype=f32):
    return jax.ShapeDtypeStruct(shape, dtype)


def split(value):
    hi = value.astype(bf16)
    return hi, (value - hi.astype(f32)).astype(bf16)


def side_by_side(value):
    return jnp.concatenate(split(value), axis=1)


def dot(left, right):
    return jnp.dot(left, right, preferred_element_type=f32)


def fold(value):
    width = value.shape[1] // 2
    return value[:, :width] + value[:, width:]


def call(kernel, outs, out_specs, in_specs, scratch=(), flops=0, moved=0):
    return pl.pallas_call(
        kernel,
        out_shape=outs,
        in_specs=in_specs,
        out_specs=out_specs,
        scratch_shapes=list(scratch),
        compiler_params=pltpu.CompilerParams(vmem_limit_bytes=VMEM_BYTES),
        cost_estimate=pl.CostEstimate(flops=flops, bytes_accessed=moved, transcendentals=0),
    )


class Message:
    def __init__(self, pairs, slots, odd_slots=None):
        self.pairs = pairs
        self.slots = slots
        self.odd_slots = odd_slots
        self.width = len(slots)
        half = len(pairs) // 2
        self.across = self.width * sum((a < half) != (b < half) for a, b in pairs)


def message_sets_of(count, slots):
    reach = slots // 2
    groups = {}
    for slot in range(slots):
        offset = slot - reach if slot < reach else slot - reach + 1
        groups.setdefault(offset % count, []).append(slot)
    messages = []
    below, above = reach - 1, reach
    if groups.get(1) == [above] and groups.get(count - 1) == [below] and count % 2 == 0:
        del groups[1], groups[count - 1]
        for turn, (even, odd) in enumerate(((below, above), (above, below))):
            pairs = [(at, (at + (1, -1)[(at + turn) % 2]) % count) for at in range(count)]
            messages.append(Message(pairs, [even], [odd]))
    for ahead, group in groups.items():
        messages.append(Message([(at, (at - ahead) % count) for at in range(count)], group))
    messages.sort(key=lambda message: -message.across)
    first = messages[:1] + [m for m in messages[:0:-1] if m.odd_slots is not None]
    rest = [message for message in messages if message not in first]
    return [first, rest[-1:] + rest[:-1]]


def slots_of(messages):
    return sorted({slot for m in messages for slot in m.slots + (m.odd_slots or [])})


def copy_runs(slots, source, target, sems):
    copies, at = [], 0
    while at < len(slots):
        count = 1
        while at + count < len(slots) and slots[at + count] == slots[at] + count:
            count += 1
        copies.append(
            pltpu.make_async_copy(
                source.at[pl.ds(slots[at], count)], target.at[pl.ds(at, count)], sems.at[at]
            )
        )
        copies[-1].start()
        at += count
    return copies


def store_coefficients(split_ref, both, messages, rank, outs):
    slots = slots_of(messages)
    size = len(slots) * rank
    got = fold(dot(split_ref[...], both))
    got = got[:size] + got[size:]

    def piece(slot):
        row = slots.index(slot) * rank
        return got[row : row + rank]

    odd = jnp.full((rank, got.shape[1]), lax.axis_index("tile") & 1, jnp.int32) == 1
    for message, out in zip(messages, outs):
        for w, slot in enumerate(message.slots):
            value = piece(slot)
            if message.odd_slots is not None:
                value = jnp.where(odd, piece(message.odd_slots[w]), value)
            out[w] = value


def split_rows(right, slots, split_ref):
    rank = right.shape[1]
    rows = len(slots) * rank
    for at, slot in enumerate(slots):
        hi, lo = split(right[slot])
        split_ref[at * rank : (at + 1) * rank] = hi
        split_ref[rows + at * rank : rows + (at + 1) * rank] = lo


def first_coeff_kernel(messages, cols_ref, right_ref, *refs):
    outs, refs = refs[: len(messages)], refs[len(messages) :]
    split_ref, both_ref, cols, right, cols_sem, sems = refs
    cols_copy = pltpu.make_async_copy(cols_ref, cols, cols_sem)
    cols_copy.start()
    copies = copy_runs(slots_of(messages), right_ref, right, sems)
    cols_copy.wait()
    both_ref[...] = side_by_side(cols[...])
    for copy in copies:
        copy.wait()
    split_rows(right, range(right.shape[0]), split_ref)
    store_coefficients(split_ref, both_ref[...], messages, right.shape[1], outs)


def first_coefficients(cols, right_tile, messages):
    _, rank, size = right_tile.shape
    width = cols.shape[1]
    count = len(slots_of(messages))
    outs = [struct(message.width, rank, width) for message in messages]
    outs += [struct(2 * count * rank, size, dtype=bf16), struct(size, 2 * width, dtype=bf16)]
    got = call(
        functools.partial(first_coeff_kernel, messages),
        outs,
        [in_vmem] * len(outs),
        [in_hbm, in_hbm],
        [
            pltpu.VMEM(cols.shape, f32),
            pltpu.VMEM((count, rank, size), f32),
            pltpu.SemaphoreType.DMA,
            pltpu.SemaphoreType.DMA((count,)),
        ],
        flops=8 * count * rank * size * width,
        moved=4 * count * rank * size,
    )(to_hbm(cols), to_hbm(right_tile))
    return got[:-2], got[-2], got[-1]


def rest_coeff_kernel(messages, both_ref, right_ref, *refs):
    outs, split_ref = refs[:-1], refs[-1]
    split_rows(right_ref, slots_of(messages), split_ref)
    store_coefficients(split_ref, both_ref[...], messages, right_ref.shape[1], outs)


def rest_coefficients(both, right_tile, messages):
    _, rank, size = right_tile.shape
    count = len(slots_of(messages))
    width = both.shape[1] // 2
    outs = [struct(message.width, rank, width) for message in messages]
    outs.append(struct(2 * count * rank, size, dtype=bf16))
    got = call(
        functools.partial(rest_coeff_kernel, messages),
        outs,
        [in_vmem] * len(outs),
        [in_vmem] * 2,
        flops=8 * count * rank * size * width,
        moved=8 * count * rank * size,
    )(both, right_tile)
    return got[:-1], got[-1]


def halve_kernel(base, own_ref, got_ref, weights_ref, keep_ref, send_ref):
    own, got = own_ref[...], got_ref[...]
    keep_ref[...] = own * weights_ref[base] + got * weights_ref[base + 1]
    send_ref[...] = own * weights_ref[base + 2] + got * weights_ref[base + 3]


def halve(own, got, weights, half):
    part, width = own.shape
    return call(
        functools.partial(halve_kernel, 4 * half),
        [struct(part, width)] * 2,
        [in_vmem] * 2,
        [in_vmem] * 3,
        flops=6 * part * width,
        moved=32 * part * width,
    )(own, got, weights)


def mix(first, weights):
    groups = lax.axis_size("kern")
    if groups != 4:
        fields = [lax.all_gather(part, "kern") for part in first]
        mixed = jnp.sum(jnp.concatenate(fields, axis=1) * weights, axis=0)
        return [(mixed, jnp.zeros_like(mixed))]
    count = lax.axis_size("tile")
    steps = ([], [])
    for group in range(groups):
        for tile in range(count):
            for turn, pairs in enumerate(steps):
                dest = group ^ (1 + (turn + tile) % 2)
                pairs.append((group * count + tile, dest * count + tile))
    axes = ("kern", "tile")
    came = [lax.ppermute(part, axes, pairs) for part, pairs in zip(first, steps)]
    sums = [
        halve(part, got, weights, half)
        for half, (part, got) in enumerate(zip(first, came))
    ]
    return [
        (keep, lax.ppermute(send, axes, pairs)) for (keep, send), pairs in zip(sums, steps[::-1])
    ]


def mixed_coeff_kernel(messages, terms, *refs):
    fields, split_ref = refs[:terms], refs[terms]
    outs, cols_ref, both_ref = refs[terms + 1 : -2], refs[-2], refs[-1]
    part = fields[0].shape[0]
    for at in range(0, terms, 2):
        rows_of = pl.ds(at // 2 * part, part)
        total = fields[at][...] + fields[at + 1][...]
        cols_ref[rows_of] = total
        both_ref[rows_of] = side_by_side(total)
    store_coefficients(split_ref, both_ref[...], messages, outs[0].shape[1], outs)


def mixed_coefficients(mixed, split_right, messages, rank):
    flat = [term for pair in mixed for term in pair]
    part, width = flat[0].shape
    size = part * len(mixed)
    total = split_right.shape[0]
    outs = [struct(message.width, rank, width) for message in messages]
    outs += [struct(size, width), struct(size, 2 * width, dtype=bf16)]
    got = call(
        functools.partial(mixed_coeff_kernel, messages, len(flat)),
        outs,
        [in_vmem] * len(outs),
        [in_vmem] * (len(flat) + 1),
        flops=4 * total * size * width,
        moved=2 * total * (size + width),
    )(*flat, split_right)
    return got[:-2], got[-2], got[-1]


def next_coeff_kernel(messages, both_ref, split_ref, *outs):
    store_coefficients(split_ref, both_ref[...], messages, outs[0].shape[1], outs)


def next_coefficients(both, split_right, messages, rank):
    size, width = both.shape[0], both.shape[1] // 2
    total = split_right.shape[0]
    return call(
        functools.partial(next_coeff_kernel, messages),
        [struct(message.width, rank, width) for message in messages],
        [in_vmem] * len(messages),
        [in_vmem] * 2,
        flops=4 * total * size * width,
        moved=2 * total * (size + width),
    )(both, split_right)


def times_diag(diag_ref, cols_ref):
    both = side_by_side(cols_ref[...])
    hi, lo = split(diag_ref[...])
    return fold(dot(hi, both) + dot(lo, both))


def relay_kernel(count, *refs):
    for source, target in zip(refs[:count], refs[-count:]):
        target[...] = source[...]


def relay(values, after):
    return call(
        functools.partial(relay_kernel, len(values)),
        [struct(*value.shape) for value in values],
        [in_vmem] * len(values),
        [in_vmem] * len(values) + [in_any] * len(after),
        moved=8 * sum(value.size for value in values),
    )(*values, *after)


def diag_kernel(diag_ref, cols_ref, out_ref):
    out_ref[...] = times_diag(diag_ref, cols_ref)


def diagonal(diag_tile, cols):
    size, width = cols.shape
    return call(
        diag_kernel,
        struct(size, width),
        in_vmem,
        [in_vmem, in_vmem],
        flops=8 * size * size * width,
        moved=4 * size * (size + 2 * width),
    )(diag_tile, cols)


def weight_rows(size):
    groups = lax.axis_size("kern")
    me = lax.axis_index("kern")
    if groups != 4:
        return [(me * groups + b, slice(0, size)) for b in range(groups)]
    rows_of = []
    odd = lax.axis_index("tile") & 1
    one, two = me ^ (1 + odd), me ^ (2 - odd)
    for half, (first, second) in enumerate(((one, two), (two, one))):
        lanes = slice(half * (size // 2), (half + 1) * (size // 2))
        for a in (me, second):
            for b in (me, first):
                rows_of.append((a * groups + b, lanes))
    return rows_of


def prepare_kernel(
    halves, diag_hbm, cols_hbm, left_hbm, table_ref, index_ref,
    diag_out, left_out, weights_ref, diag_ref, cols_ref, left_ref, full_ref, sems,
):
    copies = []
    for at, (source, target) in enumerate(
        ((diag_hbm, diag_ref), (cols_hbm, cols_ref), (left_hbm, left_ref))
    ):
        copies.append(pltpu.make_async_copy(source, target, sems.at[at]))
        copies[-1].start()
    entries = table_ref.shape[1]
    size = index_ref.shape[1]
    hot = (lax.broadcasted_iota(jnp.int32, (entries, size), 0) == index_ref[...]).astype(f32)
    full_ref[...] = jnp.dot(
        table_ref[...], hot, precision=lax.Precision.HIGHEST, preferred_element_type=f32
    )
    width = weights_ref.shape[2]
    for at, (row, lanes) in enumerate(weight_rows(size)):
        piece = full_ref[pl.ds(row, 1), lanes]
        weights_ref[at] = jnp.broadcast_to(piece, (width, piece.shape[1])).T
    copies[0].wait()
    copies[1].wait()
    diag_out[...] = times_diag(diag_ref, cols_ref)
    copies[2].wait()
    total = left_ref.shape[0]
    step = 128 if total % 128 == 0 else total
    part = size // halves
    for at in range(0, total, step):
        span = slice(at, at + step)
        hi, lo = split(left_ref[span].T)
        for half in range(halves):
            base = 2 * half * part
            rows_of = slice(half * part, (half + 1) * part)
            left_out[base : base + part, span] = hi[rows_of]
            left_out[base + part : base + 2 * part, span] = lo[rows_of]


def prepare(diag_tile, cols, left_rows, table, index, halves):
    size, width = cols.shape
    total = left_rows.shape[0]
    weights = weight_rows(size)
    part = weights[0][1].stop
    return call(
        functools.partial(prepare_kernel, halves),
        [
            struct(size, width),
            struct(2 * size, total, dtype=bf16),
            struct(len(weights), part, width),
        ],
        [in_vmem] * 3,
        [in_hbm] * 3 + [in_vmem] * 2,
        [
            pltpu.VMEM(diag_tile.shape, f32),
            pltpu.VMEM(cols.shape, f32),
            pltpu.VMEM(left_rows.shape, f32),
            pltpu.VMEM((table.shape[0], size), f32),
            pltpu.SemaphoreType.DMA((3,)),
        ],
        flops=8 * size * size * width,
        moved=8 * total * size + 4 * size * (size + 2 * width),
    )(to_hbm(diag_tile), to_hbm(cols), to_hbm(left_rows), table, index)


def row_kernel(messages, halves, final, offs_ref, ranks_ref, *refs):
    gots = refs[: len(messages)]
    left_ref, diag_ref = refs[len(messages) : len(messages) + 2]
    outs = refs[len(messages) + 2 :]
    if final:
        outs, (picked, term_of, stage, sems) = outs[:-4], outs[-4:]
    else:
        outs, (picked, term_of) = outs[:-2], outs[-2:]
    terms = offs_ref.shape[1]
    rank, width = gots[0].shape[1:]
    slots = term_of.shape[0]
    reach = slots // 2
    for slot in range(slots):
        term_of[slot] = terms
    for k in range(terms):
        offset = offs_ref[0, k]
        term_of[jnp.where(offset < 0, offset + reach, offset + reach - 1)] = k
    line = lax.broadcasted_iota(jnp.int32, (rank, width), 0)

    def pick(got, w, term):
        last = ranks_ref[0, jnp.minimum(term, terms - 1)]
        kept = jnp.where(line < last, got[w], 0.0)
        picked[pl.ds(pl.multiple_of(term * rank, rank), rank)] = kept

    for got, message in zip(gots, messages):
        for w, slot in enumerate(message.slots):
            if message.odd_slots is not None:
                slot = jnp.where((lax.axis_index("tile") & 1) == 1, slot, message.odd_slots[w])
            pick(got, w, term_of[slot])
    both = side_by_side(picked[: terms * rank])
    part = diag_ref.shape[0] // halves
    sent = []
    got = fold(dot(left_ref[...], both))
    for half in range(halves):
        rows_of = pl.ds(half * part, part)
        base = 2 * half * part
        total = got[base : base + part] + got[base + part : base + 2 * part] + diag_ref[rows_of]
        if final:
            stage[rows_of] = total
            sent.append(
                pltpu.make_async_copy(stage.at[rows_of], outs[0].at[rows_of], sems.at[half])
            )
            sent[-1].start()
        else:
            outs[half][...] = total
    for copy in sent:
        copy.wait()


def rows(offsets, ranks, gots, messages, left_split, diag_part, slots, halves, final):
    size, width = diag_part.shape
    total = left_split.shape[1]
    rank = gots[0].shape[1]
    scratch = [pltpu.VMEM((total + rank, width), f32), pltpu.SMEM((slots,), jnp.int32)]
    if final:
        scratch += [pltpu.VMEM((size, width), f32), pltpu.SemaphoreType.DMA((halves,))]
    return call(
        functools.partial(row_kernel, messages, halves, final),
        pltpu.HBM((size, width), f32) if final else [struct(size // halves, width)] * halves,
        in_hbm if final else [in_vmem] * halves,
        [in_smem, in_smem] + [in_vmem] * (len(messages) + 2),
        scratch,
        flops=8 * total * size * width,
        moved=4 * total * (size + width),
    )(offsets, ranks, *gots, left_split, diag_part)


def send(value, message):
    return lax.ppermute(value, "tile", message.pairs)


def send_all(one, two, coeffs, more, waited, beside):
    gots = []
    for value, message in zip(coeffs, one):
        if message.odd_slots is not None and message.across:
            value = relay([value], [gots[waited], more[0], beside])[0]
        gots.append(send(value, message))
    return gots + [send(value, message) for value, message in zip(more, two)]


def local(
    diag_tiles,
    left_factors,
    right_factors,
    tile_offsets,
    tile_ranks,
    mixing,
    block_index,
    rhs_field,
):
    diag_tile = diag_tiles[0, 0]
    right_tile = right_factors[0, 0]
    offsets = tile_offsets[0]
    ranks = tile_ranks[0]
    slots, rank, size = right_tile.shape
    halves = 2 if size % 32 == 0 else 1
    left_rows = left_factors.reshape(-1, size)
    groups = lax.axis_size("kern")
    table = mixing.reshape(mixing.shape[0], groups * groups).T
    index = block_index[None]
    cols = rhs_field[0]

    one, two = message_sets_of(lax.axis_size("tile"), slots)
    messages = one + two
    coeffs, split_one, both = first_coefficients(cols, right_tile, one)
    more, split_two = rest_coefficients(both, right_tile, two)
    diag_part, left_split, weights = prepare(diag_tile, cols, left_rows, table, index, halves)
    gots = send_all(one, two, coeffs, more, -1, diag_part)
    first = rows(offsets, ranks, gots, messages, left_split, diag_part, slots, halves, False)
    mixed = mix(first, weights)
    coeffs, cols, both = mixed_coefficients(mixed, split_one, one, rank)
    more = next_coefficients(both, split_two, two, rank)
    diag_part = diagonal(diag_tile, cols)
    gots = send_all(one, two, coeffs, more, 0, diag_part)
    return rows(offsets, ranks, gots, messages, left_split, diag_part, slots, halves, True)[None]


def solution(mesh):
    in_specs = (
        P("kern", "tile", None, None),
        P("kern", "tile", None, None, None),
        P("kern", "tile", None, None, None),
        P("kern", "tile", None),
        P("kern", "tile", None),
        P(),
        P("tile"),
        P("kern", "tile", None),
    )
    out_specs = P("kern", "tile", None)
    return jax.shard_map(local, mesh=mesh, in_specs=in_specs, out_specs=out_specs, check_vma=False)
```
